32 devices in a mesh: seq: 16 (over z, y, x), dp: 2 (over core).
Axes of the slice: x: 2, y: 2, z: 4, core: 2. Of those that a mesh axis runs over, the one named last changes fastest.
Arguments:
- tokens: bfloat16 [2, 65536, 1024], P('dp', 'seq'), may hold values from -6 to 6
- lengths: int32 [2, 64], P('dp', 'seq'), may hold values from 512 to 1024, as said below
- routed_index: int32 [2, 64, 128], P('dp', 'seq'), may hold values from 0 to 1023, as said below
- out_grad: bfloat16 [2, 65536, 1024], P('dp', 'seq'), may hold values from -6 to 6
- gain_attn: bfloat16 [1024], replicated, may hold values from 0.099609375 to 1.8984375
- w_router: bfloat16 [1024], replicated, may hold values from -0.1875 to 0.1875
- w_query: bfloat16 [1024, 1024], replicated, may hold values from -0.25 to 0.25
- w_key: bfloat16 [1024, 1024], replicated, may hold values from -0.25 to 0.25
- w_value: bfloat16 [1024, 1024], replicated, may hold values from -0.1875 to 0.1875
- w_out: bfloat16 [1024, 1024], replicated, may hold values from -0.5 to 0.5
- gain_mlp: bfloat16 [1024], replicated, may hold values from 0.099609375 to 1.8984375
- w_up: bfloat16 [1024, 4096], replicated, may hold values from -0.1875 to 0.1875
- w_down: bfloat16 [4096, 1024], replicated, may hold values from -0.09375 to 0.09375
Outputs:
- mixed_out: bfloat16 [2, 65536, 1024], P('dp', 'seq')
- token_grad: float32 [2, 65536, 1024], P('dp', 'seq')
- grad_gain_attn: float32 [1024], P(('seq', 'dp'))
- grad_router: float32 [1024], P(('seq', 'dp'))
- grad_query: float32 [1024, 1024], P(None, ('seq', 'dp'))
- grad_key: float32 [1024, 1024], P(None, ('seq', 'dp'))
- grad_value: float32 [1024, 1024], P(None, ('seq', 'dp'))
- grad_out: float32 [1024, 1024], P(None, ('seq', 'dp'))
- grad_gain_mlp: float32 [1024], P(('seq', 'dp'))
- grad_up: float32 [1024, 4096], P(None, ('seq', 'dp'))
- grad_down: float32 [4096, 1024], P(None, ('seq', 'dp'))
The draws below stay inside these ranges and needn't reach their ends.
Inputs may be any that keep to these rules, and one draw needn't show every extreme that they name: Multiples of 8. In each row (a group of 64 sequences) the lengths sum to exactly 49152, and some length equals 1024. `routed_index`: for a sequence of length n the first n // 8 entries are distinct positions below n in increasing order; the remaining entries are positions below n that are not routed.
All inputs are finite; a program needn't handle non-finite values.
Results may differ from the reference program's by a relative error of at most 0.012.
The reference program's roundings to bfloat16 on the way count: a program that leaves them out, or rounds other values in their place, can miss the bound.
Values may be sent and summed in bfloat16 or wider, within the bound.
No kernel may reach another device: no remote copies, remote signals or barrier semaphores. Data moves between devices by JAX's collectives and lax.ppermute only.
A program may use at most 256 MiB of HBM per device.

```python
import jax
import jax.numpy as jnp
from jax import lax

D = 1024
H = 16
HD = 64
FF = 4096
LEN = 1024
SEQ_DEV = 4
CAP = 128
GROUP_SEQS = 64
GROUP_TOK = 65536
N_SEQ = 16
N_DP = 2


def shared_units(key):
    most_units = LEN // 8
    half_count = GROUP_SEQS // 2
    first_half = jax.random.randint(key, (N_DP, half_count), most_units // 2, most_units + 1)
    first_half = first_half.at[:, 0].set(most_units)
    second_half = 3 * most_units // 2 - first_half
    paired = jnp.concatenate([first_half, second_half], axis=1)
    order_keys = jax.random.split(jax.random.fold_in(key, 17), N_DP)
    orders = jax.vmap(lambda sub_key: jax.random.permutation(sub_key, GROUP_SEQS))(order_keys)
    return jnp.take_along_axis(paired, orders, axis=1).astype(jnp.int32)


def draw_lengths(key, part):
    units = shared_units(key)
    return (8 * units).astype(jnp.int32)


def draw_routed_index(key, part):
    units = shared_units(key)
    key = jax.random.fold_in(key, 2)
    seq_lens = 8 * units
    perm_keys = jax.random.split(key, N_DP * GROUP_SEQS)
    ranks = jax.vmap(lambda sub_key: jax.random.permutation(sub_key, LEN))(perm_keys).reshape(N_DP, GROUP_SEQS, LEN)
    places = jnp.arange(LEN, dtype=jnp.int32)
    ordered = jnp.where(places[None, None, :] < seq_lens[..., None], ranks, ranks + LEN)
    picked = jnp.argsort(ordered, axis=-1, stable=True)[..., :CAP].astype(jnp.int32)
    slot_ids = jnp.arange(CAP, dtype=jnp.int32)
    keyed = jnp.where(slot_ids[None, None, :] < units[..., None], picked, picked + LEN)
    sorted_keys = jnp.sort(keyed, axis=-1)
    return jnp.where(sorted_keys >= LEN, sorted_keys - LEN, sorted_keys).astype(jnp.int32)


def with_spikes(values, own_key, source, target, blocks, factor):
    owner, partner = [(jnp.arange(values.shape[axis_at]) // (values.shape[axis_at] // blocks)).reshape([-1 if axis == axis_at else 1 for axis in range(values.ndim)]) for axis_at in (source, target)]
    chosen = jax.random.permutation(own_key, blocks)[partner]
    strong = (owner == chosen) | (owner == (partner + blocks // 2) % blocks)
    return jnp.where(strong, factor * values, values)


def level_of(stream_key, extent, shards, least, largest):
    loudness, own = 1.0, jax.random.fold_in(stream_key, 6)
    for axis_at, shards_of in shards:
        steps = jnp.exp(jax.random.uniform(jax.random.fold_in(own, axis_at), (shards_of,), jnp.float32, least / len(shards), largest / len(shards)))
        loudness = loudness * jnp.repeat(steps, extent[axis_at] // shards_of).reshape([-1 if axis == axis_at else 1 for axis in range(len(extent))])
    return loudness


def bell_draw(rng, shape, width, most, cuts=(), held_as=jnp.bfloat16):
    level = level_of(rng, shape, cuts, -0.22, 0.18) if cuts else 1.0
    drawn = jax.random.normal(rng, shape, jnp.float32) * width * level
    return jnp.minimum(jnp.maximum(drawn, -most), most).astype(held_as)


def bell_draw_with(own_key, extent, width, reach, cuts, heavy, kind=jnp.bfloat16):
    drawn = width * jax.random.normal(own_key, extent, jnp.float32)
    if cuts:
        drawn = drawn * level_of(own_key, extent, cuts, -0.22, 0.18)
    return jnp.clip(with_spikes(drawn, jax.random.fold_in(own_key, 3), *heavy), -reach, reach).astype(kind)


def setup_inputs(seed: int = 0) -> dict:
    arg_keys = jax.random.split(jax.random.key(seed), 14)
    tokens = bell_draw(arg_keys[0], (N_DP, GROUP_TOK, D), 1.0, 6.0, ((0, 2), (1, 16)))
    lengths = draw_lengths(jax.random.fold_in(arg_keys[13], 71), 0)
    routed_index = draw_routed_index(jax.random.fold_in(arg_keys[13], 71), 0)
    out_grad = bell_draw_with(arg_keys[3], (N_DP, GROUP_TOK, D), 1.0, 6.0, ((0, 2), (1, 16)), (1, 2, 16, 2.0))
    gain_attn = jnp.clip(1.0 + 0.18 * jax.random.normal(arg_keys[4], (D,), jnp.float32), 0.099609375, 1.8984375).astype(jnp.bfloat16)
    w_router = bell_draw(arg_keys[5], (D,), D ** -0.5, 0.1875)
    w_query = bell_draw(arg_keys[6], (D, D), (D // 2) ** -0.5, 0.25)
    w_key = bell_draw(arg_keys[7], (D, D), (D // 2) ** -0.5, 0.25)
    w_value = bell_draw(arg_keys[8], (D, D), D ** -0.5, 0.1875)
    w_out = bell_draw(arg_keys[9], (D, D), (D // 8) ** -0.5, 0.5)
    gain_mlp = jnp.clip(1.0 + 0.18 * jax.random.normal(arg_keys[10], (D,), jnp.float32), 0.099609375, 1.8984375).astype(jnp.bfloat16)
    w_up = bell_draw(arg_keys[11], (D, FF), D ** -0.5, 0.1875)
    w_down = bell_draw(arg_keys[12], (FF, D), FF ** -0.5, 0.09375)
    return dict(tokens=tokens, lengths=lengths, routed_index=routed_index, out_grad=out_grad, gain_attn=gain_attn, w_router=w_router, w_query=w_query, w_key=w_key, w_value=w_value, w_out=w_out, gain_mlp=gain_mlp, w_up=w_up, w_down=w_down)


norm_eps = 1e-05

@jax.custom_vjp
def low(v):
    return lax.optimization_barrier(v.astype(jnp.bfloat16)).astype(jnp.float32)

@jax.custom_vjp
def low_back(v):
    return v

def low_keep(v):
    return (low(v), None)

def low_pass(kept, grad):
    return (grad,)

def back_keep(v):
    return (v, None)

def back_low(kept, grad):
    return (low(grad),)
low.defvjp(low_keep, low_pass)
low_back.defvjp(back_keep, back_low)

def highest_dot(left_side, right_side):
    return jnp.dot(left_side, right_side, precision=lax.Precision.HIGHEST)

def norm_ref(values):
    return values * lax.rsqrt(lax.optimization_barrier(jnp.mean(values * values, axis=-1, keepdims=True)) + norm_eps)

def layer_fwd(seq_tokens, seq_length, seq_index, gain_attn, w_router, w_query, w_key, w_value, w_out, gain_mlp, w_up, w_down):
    routed = seq_length // 8
    slot_ids = jnp.arange(CAP, dtype=jnp.int32)
    live_slot = slot_ids < routed
    chosen = jnp.take(seq_tokens, seq_index, axis=0)
    router_score = jax.nn.sigmoid(highest_dot(chosen, w_router))
    first_in = low(norm_ref(chosen) * gain_attn)
    queries = low(low_back(highest_dot(first_in, w_query) * 0.125)).reshape(CAP, H, HD)
    key_rows = low(low_back(highest_dot(first_in, w_key))).reshape(CAP, H, HD)
    value_rows = low(low_back(highest_dot(first_in, w_value))).reshape(CAP, H, HD)
    raw_scores = low_back(jnp.einsum('ihk,jhk->hij', queries, key_rows, precision=lax.Precision.HIGHEST))
    allowed = (slot_ids[None, :] <= slot_ids[:, None]) & live_slot[None, :]
    masked = jnp.where(allowed[None], raw_scores, -1e+30)
    row_peak = lax.optimization_barrier(jnp.max(masked, axis=-1, keepdims=True))
    exp_scores = jnp.exp(masked - row_peak)
    attn_probs = exp_scores / lax.optimization_barrier(jnp.sum(exp_scores, axis=-1, keepdims=True))
    attn_mix = low(low_back(jnp.einsum('hij,jhk->ihk', low(attn_probs), value_rows, precision=lax.Precision.HIGHEST))).reshape(CAP, D)
    attn_out = low_back(highest_dot(attn_mix, w_out))
    after_attn = chosen + attn_out
    second_in = low(low_back(norm_ref(after_attn) * gain_mlp))
    hidden_pre = low_back(highest_dot(second_in, w_up))
    hidden_act = low(jax.nn.gelu(hidden_pre, approximate=False))
    mlp_out = low(low_back(highest_dot(hidden_act, w_down)))
    weighted = jnp.where(live_slot, router_score, 0.0)[:, None] * (attn_out + mlp_out)
    return seq_tokens.at[seq_index].add(weighted)

def reference(tokens, lengths, routed_index, out_grad, gain_attn, w_router, w_query, w_key, w_value, w_out, gain_mlp, w_up, w_down):
    seq_total = N_DP * N_SEQ * SEQ_DEV
    flat_tokens = tokens.astype(jnp.float32).reshape(seq_total, LEN, D)
    flat_grads = out_grad.astype(jnp.float32).reshape(seq_total, LEN, D)
    flat_lengths = lengths.reshape(seq_total).astype(jnp.int32)
    flat_index = routed_index.reshape(seq_total, CAP).astype(jnp.int32)
    params = tuple((param.astype(jnp.float32) for param in (gain_attn, w_router, w_query, w_key, w_value, w_out, gain_mlp, w_up, w_down)))

    def one_seq(carry, item):
        seq_tokens, seq_grad, seq_length, seq_index = item

        def forward(tok_in, *weights_in):
            return layer_fwd(tok_in, seq_length, seq_index, *weights_in)
        seq_out, pull_back = jax.vjp(forward, seq_tokens, *params)
        grads = pull_back(seq_grad)
        summed = tuple((total + piece for total, piece in zip(carry, grads[1:])))
        return (summed, (seq_out, grads[0]))
    start = tuple((jnp.zeros(param.shape, jnp.float32) for param in params))
    sums, stacked = lax.scan(one_seq, start, (flat_tokens, flat_grads, flat_lengths, flat_index))
    mixed_out = stacked[0].reshape(tokens.shape).astype(jnp.bfloat16)
    token_grad = stacked[1].reshape(tokens.shape)
    return (mixed_out, token_grad, sums[0], sums[1], sums[2], sums[3], sums[4], sums[5], sums[6], sums[7], sums[8])
```

```python
import functools

import jax
import jax.experimental.pallas as pl
import jax.experimental.pallas.tpu as pltpu
import jax.numpy as jnp
from jax import lax
from jax.sharding import PartitionSpec as P

H = 16
norm_eps = 1e-05
f32 = jnp.float32
bf16 = jnp.bfloat16
VMEM_BYTES = 58 * 1024 * 1024


def params(count=1):
    return pltpu.CompilerParams(
        dimension_semantics=("arbitrary",) * count, vmem_limit_bytes=VMEM_BYTES
    )


def cost(micros):
    return pl.CostEstimate(
        flops=int(micros * 1e9), bytes_accessed=int(micros * 3.5e6), transcendentals=0
    )


def call(kernel, arrays, waits=(), scalars=(), **rest):
    first = len(scalars) + len(arrays)

    def body(*refs):
        kernel(*refs[:first], *refs[first + len(waits) :])

    grid = pltpu.PrefetchScalarGridSpec(
        num_scalar_prefetch=len(scalars),
        grid=rest.pop("grid"),
        in_specs=list(rest.pop("in_specs")) + [pl.BlockSpec(memory_space=pl.ANY)] * len(waits),
        out_specs=rest.pop("out_specs"),
        scratch_shapes=rest.pop("scratch_shapes", ()),
    )
    return pl.pallas_call(body, grid_spec=grid, **rest)(*scalars, *arrays, *waits)


def whole(array):
    rank = len(array.shape)
    return pl.BlockSpec(array.shape, lambda *_: (0,) * rank, pipeline_mode=pl.Buffered(1))


def dot_nn(left, right):
    return lax.dot_general(left, right, (((1,), (0,)), ((), ())), preferred_element_type=f32)


def dot_nt(left, right):
    return lax.dot_general(left, right, (((1,), (1,)), ((), ())), preferred_element_type=f32)


def dot_tn(left, right):
    return lax.dot_general(left, right, (((0,), (0,)), ((), ())), preferred_element_type=f32)


def inv_rms(values):
    return lax.rsqrt(jnp.mean(values * values, axis=-1, keepdims=True) + norm_eps)


GROUP = 4


def stacked(rows, head):
    lane_head = lax.broadcasted_iota(jnp.int32, rows.shape, 1) // head
    zero = jnp.zeros_like(rows)
    return jnp.concatenate([jnp.where(lane_head == h, rows, zero) for h in range(GROUP)], axis=0)


def unstacked(rows, head):
    slots = rows.shape[0] // GROUP
    lane_head = lax.broadcasted_iota(jnp.int32, (slots, rows.shape[1]), 1) // head
    out = rows[:slots]
    for h in range(1, GROUP):
        out = jnp.where(lane_head == h, rows[h * slots : (h + 1) * slots], out)
    return out


def front_kernel(
    routed_ref, index_ref, tokens_ref, cotangent_ref, gain_one_ref, router_ref, gain_two_ref,
    query_hbm, key_hbm, value_hbm, out_hbm,
    chosen_ref, first_ref, query_ref, key_ref, value_ref, probs_ref, mix_ref, attn_ref,
    second_ref, pulled_ref, mlp_grad_ref, score_ref,
    query_w, key_w, value_w, out_w, sems,
):
    seq = pl.program_id(0)
    weights = ((query_hbm, query_w), (key_hbm, key_w), (value_hbm, value_w), (out_hbm, out_w))
    copies = [pltpu.make_async_copy(src, dst, sems.at[i]) for i, (src, dst) in enumerate(weights)]

    @pl.when(seq == 0)
    def _():
        for copy in copies:
            copy.start()

    slots, places = index_ref.shape[1], tokens_ref.shape[0]
    width = tokens_ref.shape[1]
    head = width // H
    routed = routed_ref[seq]
    slot_id = lax.broadcasted_iota(jnp.int32, (slots, places), 0)
    place_id = lax.broadcasted_iota(jnp.int32, (slots, places), 1)
    pick = ((index_ref[0] == place_id) & (slot_id < routed)).astype(bf16)
    chosen = dot_nn(pick, tokens_ref[...])
    pulled = dot_nn(pick, cotangent_ref[...])
    chosen_ref[...] = chosen.astype(bf16)
    pulled_ref[...] = pulled.astype(bf16)
    logit = jnp.sum(chosen * router_ref[...].astype(f32), axis=-1, keepdims=True)
    score = 1.0 / (1.0 + jnp.exp(-logit))
    score_ref[...] = jnp.broadcast_to(score, score_ref.shape)
    mlp_grad_ref[...] = (score * pulled).astype(bf16)
    first = (chosen * inv_rms(chosen) * gain_one_ref[...].astype(f32)).astype(bf16)
    first_ref[...] = first

    @pl.when(seq == 0)
    def _():
        for copy in copies:
            copy.wait()

    query_ref[...] = (dot_nn(first, query_w[...]) * 0.125).astype(bf16)
    key_ref[...] = dot_nn(first, key_w[...]).astype(bf16)
    value_ref[...] = dot_nn(first, value_w[...]).astype(bf16)
    rows = GROUP * slots
    row_id = lax.broadcasted_iota(jnp.int32, (rows, slots), 0) % slots
    col_id = lax.broadcasted_iota(jnp.int32, (rows, slots), 1)
    allowed = (col_id <= row_id) & (col_id < routed)
    for g in range(H // GROUP):
        lanes = pl.ds(g * GROUP * head, GROUP * head)
        scores = dot_nt(stacked(query_ref[:, lanes], head), key_ref[:, lanes])
        scores = jnp.where(allowed, scores, -1e30)
        exped = jnp.exp(scores - jnp.max(scores, axis=-1, keepdims=True))
        probs = exped / jnp.sum(exped, axis=-1, keepdims=True)
        probs_ref[0, g] = probs
        mixed = dot_nn(probs.astype(bf16), value_ref[:, lanes])
        mix_ref[:, lanes] = unstacked(mixed, head).astype(bf16)
    attn = dot_nn(mix_ref[...], out_w[...])
    attn_ref[...] = attn
    after = chosen + attn
    second_ref[...] = (after * inv_rms(after) * gain_two_ref[...].astype(f32)).astype(bf16)


def front(routed, index, tokens, cotangent, gain_one, router, gain_two, wq, wk, wv, wo, waits=()):
    seqs, slots = index.shape
    places, width = tokens.shape[0] // seqs, tokens.shape[1]
    rows = seqs * slots
    by_seq = lambda shape: pl.BlockSpec(shape, lambda i, *_: (i, 0))
    vec = pl.BlockSpec((1, width), lambda i, *_: (0, 0))
    hbm = pl.BlockSpec(memory_space=pl.ANY)
    low = jax.ShapeDtypeStruct((rows, width), bf16)
    row_spec = by_seq((slots, width))
    return call(
        front_kernel,
        [index[:, :, None], tokens, cotangent, gain_one[None], router[None], gain_two[None], wq, wk, wv, wo],
        waits,
        [routed],
        grid=(seqs,),
        in_specs=[
            pl.BlockSpec((1, slots, 1), lambda i, *_: (i, 0, 0)),
            by_seq((places, width)),
            by_seq((places, width)),
            vec, vec, vec, hbm, hbm, hbm, hbm,
        ],
        out_specs=[row_spec] * 5
        + [
            pl.BlockSpec((1, H // GROUP, GROUP * slots, slots), lambda i, *_: (i, 0, 0, 0)),
            row_spec, row_spec, row_spec, row_spec, row_spec,
            by_seq((slots, 128)),
        ],
        scratch_shapes=[pltpu.VMEM((width, width), bf16)] * 4 + [pltpu.SemaphoreType.DMA((4,))],
        out_shape=[low] * 5
        + [
            jax.ShapeDtypeStruct((seqs, H // GROUP, GROUP * slots, slots), f32),
            low, jax.ShapeDtypeStruct((rows, width), f32), low, low, low,
            jax.ShapeDtypeStruct((rows, 128), f32),
        ],
        compiler_params=params(),
        name="front",
        cost_estimate=cost(20),
    )


def gelu_both(z):
    x = jnp.abs(z) * 0.7071067811865476
    t = 1.0 / (1.0 + 0.3275911 * x)
    bell = jnp.exp(-0.5 * z * z)
    poly = t * (
        0.254829592
        + t * (-0.284496736 + t * (1.421413741 + t * (-1.453152027 + t * 1.061405429)))
    )
    tail = 0.5 * poly * bell
    cdf = jnp.where(z < 0, tail, 1.0 - tail)
    return z * cdf, cdf + z * bell * 0.3989422804014327


def turn(rel, flat):
    bits = flat.bit_length() - 1
    half = bits // 2
    return rel // (1 << half) + rel % (1 << half) * (1 << (bits - half))


def place_blocks(me_ref, source, put_send, put_keep, size, nodes):
    core, node = me_ref[0], me_ref[1]
    flat = nodes // 4
    for rel in range(flat):
        for z in range(4):
            owner = lax.bitwise_xor(node, turn(z, 4) * flat + rel) * 2
            for put, side in ((put_keep, core), (put_send, 1 - core)):
                start = pl.multiple_of((owner + side) * size, size)
                put(rel, z, source[pl.ds(start, size), :].astype(bf16))


def up_kernel(
    me_ref, second_ref, mlp_grad_ref, up_ref, down_ref, act_ref, pre_ref, send_ref, keep_ref,
    turned_ref, terms_ref, *, nodes, blocks,
):
    @pl.when(pl.program_id(0) == 0)
    def _():
        turned_ref[...] = mlp_grad_ref[...].T

    hidden = dot_nn(second_ref[...], up_ref[...])
    act, slope = gelu_both(hidden)
    act = act.astype(bf16)
    act_ref[...] = act
    pre_ref[...] = (dot_nt(mlp_grad_ref[...], down_ref[...]) * slope).astype(bf16)
    terms_ref[...] = dot_nn(turned_ref[...], act)
    first_part = pl.program_id(0) < blocks // 2

    def put(ref):
        def store(rel, z, values):
            ref[0, jnp.where(first_part, turn(rel, nodes // 4), rel) * 4 + z] = values

        return store

    place_blocks(me_ref, terms_ref, put(send_ref), put(keep_ref), send_ref.shape[2], nodes)


def up_all(me, second, mlp_grad, w_up, w_down, nodes, block=512, waits=()):
    rows, width = second.shape
    hidden = w_up.shape[1]
    blocks = hidden // block
    half = blocks // 2
    size = width // (2 * nodes)
    held = whole(second)
    term_spec = pl.BlockSpec((1, nodes, size, block), lambda i, *_: (i // half, 0, 0, i % half))
    return call(
        functools.partial(up_kernel, nodes=nodes, blocks=blocks),
        [second, mlp_grad, w_up, w_down],
        waits,
        [me],
        grid=(blocks,),
        in_specs=[
            held,
            held,
            pl.BlockSpec((width, block), lambda i, *_: (0, i)),
            pl.BlockSpec((block, width), lambda i, *_: (i, 0)),
        ],
        out_specs=[pl.BlockSpec((rows, block), lambda i, *_: (0, i))] * 2 + [term_spec] * 2,
        scratch_shapes=[pltpu.VMEM((width, rows), bf16), pltpu.VMEM((width, block), f32)],
        out_shape=[jax.ShapeDtypeStruct((rows, hidden), bf16)] * 2
        + [jax.ShapeDtypeStruct((2, nodes, size, hidden // 2), bf16)] * 2,
        compiler_params=params(),
        name="up_all",
        cost_estimate=cost(22),
    )


def up_grad_kernel(me_ref, pre_ref, second_ref, send_ref, keep_ref):
    core = me_ref[0]
    size = keep_ref.shape[2]
    terms = dot_tn(pre_ref[...], second_ref[...])
    low, high = terms[:size].astype(bf16), terms[size:].astype(bf16)
    keep_ref[0, 0] = jnp.where(core == 0, low, high)
    send_ref[0, 0] = jnp.where(core == 0, high, low)


def up_grad(me, pre, second, nodes, waits=()):
    rows, hidden = pre.shape
    width = second.shape[1]
    size = hidden // (2 * nodes)
    flat = nodes // 4
    if 2 * size % 128:
        return plain_order(me, dot_tn(pre, second).astype(bf16).reshape(nodes, 2, size, width))

    def source(part, spot, me):
        xy = jnp.where(part == 0, turn(spot // 4, flat), spot // 4)
        return (0, lax.bitwise_xor(turn(spot % 4, 4) * flat + xy, me[1]))

    out = pl.BlockSpec((1, 1, size, width // 2), lambda part, spot, me: (part, spot, 0, 0))
    shape = jax.ShapeDtypeStruct((2, nodes, size, width // 2), bf16)
    return call(
        up_grad_kernel,
        [pre, second],
        waits,
        [me],
        grid=(2, nodes),
        in_specs=[
            pl.BlockSpec((rows, 2 * size), source),
            pl.BlockSpec((rows, width // 2), lambda part, spot, me: (0, part)),
        ],
        out_specs=[out, out],
        out_shape=[shape, shape],
        compiler_params=params(2),
        name="up_grad",
        cost_estimate=cost(12),
    )


def plain_order(me, terms):
    nodes = terms.shape[0]
    half = terms.shape[-1] // 2
    flat = nodes // 4
    spots = jnp.arange(nodes)
    rel_a, rel_b = turn(spots // 4, flat), spots // 4
    sides = []
    for side in (1 - me[0], me[0]):
        held = lax.dynamic_index_in_dim(terms, side, 1, keepdims=False)
        from_node = lambda rel: (turn(spots % 4, 4) * flat + rel) ^ me[1]
        sides.append(
            jnp.stack(
                [
                    jnp.take(held[..., :half], from_node(rel_a), axis=0),
                    jnp.take(held[..., half:], from_node(rel_b), axis=0),
                ]
            )
        )
    return sides


def back_kernel(
    chosen_ref, attn_ref, score_ref, pulled_ref, second_grad_ref, gain_ref, query_ref, key_ref,
    value_ref, probs_ref, out_ref,
    query_grad_ref, key_grad_ref, value_grad_ref, attn_grad_ref, after_grad_ref, gain_grad_ref,
):
    slots, width = chosen_ref.shape
    head = width // H
    after = chosen_ref[...].astype(f32) + attn_ref[...]
    inv = inv_rms(after)
    normed = after * inv
    arrived = second_grad_ref[...].astype(f32)
    gain_sum = jnp.sum((arrived * normed).reshape(slots // 8, 8, width), axis=0)

    @pl.when(pl.program_id(0) == 0)
    def _():
        gain_grad_ref[...] = gain_sum

    @pl.when(pl.program_id(0) > 0)
    def _():
        gain_grad_ref[...] += gain_sum

    weighted = arrived * gain_ref[...].astype(f32)
    after_grad = inv * (weighted - normed * jnp.mean(weighted * normed, axis=-1, keepdims=True))
    after_grad_ref[...] = after_grad
    delta = score_ref[:, :1] * pulled_ref[...].astype(f32)
    attn_grad = (delta + after_grad).astype(bf16)
    attn_grad_ref[...] = attn_grad
    mix_grad = dot_nt(attn_grad, out_ref[...]).astype(bf16)
    for g in range(H // GROUP):
        lanes = slice(g * GROUP * head, (g + 1) * GROUP * head)
        probs = probs_ref[0, g]
        keys, values = key_ref[:, lanes], value_ref[:, lanes]
        queries = stacked(query_ref[:, lanes], head)
        grads = stacked(mix_grad[:, lanes], head)
        prob_grad = dot_nt(grads, values)
        total = jnp.sum(prob_grad * probs, axis=-1, keepdims=True)
        score_grad = (probs * (prob_grad - total)).astype(bf16)
        value_grad_ref[:, lanes] = dot_tn(probs.astype(bf16), grads).astype(bf16)
        key_grad_ref[:, lanes] = dot_tn(score_grad, queries).astype(bf16)
        query_grad_ref[:, lanes] = unstacked(dot_nn(score_grad, keys), head).astype(bf16)


def back(chosen, attn, score, pulled, second_grad, gain, queries, keys, values, probs, w_out, waits=()):
    rows, width = chosen.shape
    seqs, groups, stack, slots = probs.shape
    row = pl.BlockSpec((slots, width), lambda i: (i, 0))
    low = jax.ShapeDtypeStruct((rows, width), bf16)
    return call(
        back_kernel,
        [chosen, attn, score, pulled, second_grad, gain[None], queries, keys, values, probs, w_out],
        waits,
        grid=(seqs,),
        in_specs=[
            row, row, pl.BlockSpec((slots, 128), lambda i: (i, 0)), row, row,
            pl.BlockSpec((1, width), lambda i: (0, 0)), row, row, row,
            pl.BlockSpec((1, groups, stack, slots), lambda i: (i, 0, 0, 0)), whole(w_out),
        ],
        out_specs=[row] * 5 + [pl.BlockSpec((8, width), lambda i: (0, 0))],
        out_shape=[low] * 4
        + [jax.ShapeDtypeStruct((rows, width), f32), jax.ShapeDtypeStruct((8, width), f32)],
        compiler_params=params(),
        name="back",
        cost_estimate=cost(14),
    )


def square_kernel(
    me_ref, query_ref, key_ref, value_ref, attn_ref, left_ref, right_ref, send_ref, keep_ref,
    terms_ref, *, nodes,
):
    half = send_ref.shape[4]
    for which, grads in enumerate((query_ref, key_ref, value_ref, attn_ref)):

        @pl.when(pl.program_id(0) == which)
        def _():
            rows = right_ref if which == 3 else left_ref
            terms = dot_tn(grads[...], rows[...])
            terms_ref[...] = terms * 0.125 if which == 0 else terms

    def put(ref):
        def store(rel, z, values):
            ref[0, turn(rel, nodes // 4) * 4 + z, 0] = values[:, :half]
            ref[1, rel * 4 + z, 0] = values[:, half:]

        return store

    place_blocks(me_ref, terms_ref, put(send_ref), put(keep_ref), send_ref.shape[3], nodes)


def square_grads(me, query_grad, key_grad, value_grad, attn_grad, first, mix, nodes, waits=()):
    rows, width = first.shape
    size = width // (2 * nodes)
    out = pl.BlockSpec((2, nodes, 1, size, width // 2), lambda i, *_: (0, 0, i, 0, 0))
    shape = jax.ShapeDtypeStruct((2, nodes, 4, size, width // 2), bf16)
    return call(
        functools.partial(square_kernel, nodes=nodes),
        [query_grad, key_grad, value_grad, attn_grad, first, mix],
        waits,
        [me],
        grid=(4,),
        in_specs=[whole(first)] * 6,
        out_specs=[out, out],
        scratch_shapes=[pltpu.VMEM((width, width), f32)],
        out_shape=[shape, shape],
        compiler_params=params(),
        name="square_grads",
        cost_estimate=cost(10),
    )


def hidden_sum_kernel(rows_ref, weight_ref, out_ref, total_ref, *, turned):
    step = pl.program_id(0)
    term = (dot_nt if turned else dot_nn)(rows_ref[...], weight_ref[...])

    @pl.when(step == 0)
    def _():
        total_ref[...] = term

    @pl.when(step > 0)
    def _():
        total_ref[...] += term

    @pl.when(step == pl.num_programs(0) - 1)
    def _():
        out_ref[...] = total_ref[...].astype(bf16)


def hidden_sum(rows, weight, turned, block=1024, waits=()):
    count, hidden = rows.shape
    width = weight.shape[0] if turned else weight.shape[1]
    spec = (
        pl.BlockSpec((width, block), lambda i: (0, i))
        if turned
        else pl.BlockSpec((block, width), lambda i: (i, 0))
    )
    return call(
        functools.partial(hidden_sum_kernel, turned=turned),
        [rows, weight],
        waits,
        grid=(hidden // block,),
        in_specs=[pl.BlockSpec((count, block), lambda i: (0, i)), spec],
        out_specs=pl.BlockSpec((count, width), lambda i: (0, 0)),
        out_shape=jax.ShapeDtypeStruct((count, width), bf16),
        scratch_shapes=[pltpu.VMEM((count, width), f32)],
        compiler_params=params(),
        name="hidden_sum",
        cost_estimate=cost(9),
    )


def last_kernel(
    chosen_ref, attn_ref, mlp_ref, score_ref, pulled_ref, after_grad_ref, query_grad_ref,
    key_grad_ref, value_grad_ref, gain_ref, router_ref, query_w, key_w, value_w,
    weighted_ref, chosen_grad_ref, gain_grad_ref, router_grad_ref,
):
    rows, width = chosen_ref.shape
    chosen = chosen_ref[...].astype(f32)
    score = score_ref[:, :1]
    branch = attn_ref[...] + mlp_ref[...].astype(f32)
    weighted_ref[...] = score * branch
    pull = jnp.sum(pulled_ref[...].astype(f32) * branch, axis=-1, keepdims=True)
    logit_grad = pull * score * (1.0 - score)
    first_grad = dot_nt(query_grad_ref[...], query_w[...]) * 0.125
    first_grad += dot_nt(key_grad_ref[...], key_w[...])
    first_grad += dot_nt(value_grad_ref[...], value_w[...])
    inv = inv_rms(chosen)
    normed = chosen * inv
    weighted = first_grad * gain_ref[...].astype(f32)
    chosen_grad_ref[...] = (
        inv * (weighted - normed * jnp.mean(weighted * normed, axis=-1, keepdims=True))
        + after_grad_ref[...]
        + logit_grad * router_ref[...].astype(f32)
    )
    fold = lambda values: jnp.sum(values.reshape(rows // 8, 8, width), axis=0)
    gain_sum, router_sum = fold(first_grad * normed), fold(logit_grad * chosen)

    @pl.when(pl.program_id(0) == 0)
    def _():
        gain_grad_ref[...] = gain_sum
        router_grad_ref[...] = router_sum

    @pl.when(pl.program_id(0) > 0)
    def _():
        gain_grad_ref[...] += gain_sum
        router_grad_ref[...] += router_sum


def last(
    chosen, attn, mlp, score, pulled, after_grad, dq, dk, dv, gain, router, wq, wk, wv, block=256, waits=()):
    rows, width = chosen.shape
    row = pl.BlockSpec((block, width), lambda i: (i, 0))
    vec = pl.BlockSpec((1, width), lambda i: (0, 0))
    sums = pl.BlockSpec((8, width), lambda i: (0, 0))
    wide = jax.ShapeDtypeStruct((rows, width), f32)
    return call(
        last_kernel,
        [chosen, attn, mlp, score, pulled, after_grad, dq, dk, dv, gain[None], router[None], wq, wk, wv],
        waits,
        grid=(rows // block,),
        in_specs=[row] * 3
        + [pl.BlockSpec((block, 128), lambda i: (i, 0))]
        + [row] * 5
        + [vec, vec]
        + [whole(wq)] * 3,
        out_specs=[row, row, sums, sums],
        out_shape=[wide, wide] + [jax.ShapeDtypeStruct((8, width), f32)] * 2,
        compiler_params=params(),
        name="last",
        cost_estimate=cost(11),
    )


def split_terms(values):
    high = values.astype(bf16)
    rest = values - high.astype(f32)
    middle = rest.astype(bf16)
    return jnp.concatenate([high, middle, (rest - middle.astype(f32)).astype(bf16)], axis=0)


def spread_kernel(routed_ref, index_ref, base_ref, delta_ref, out_ref, terms_ref):
    @pl.when(pl.program_id(1) == 0)
    def _():
        terms_ref[...] = split_terms(delta_ref[...])

    places, slots = base_ref.shape[0], delta_ref.shape[0]
    place = pl.program_id(1) * places + lax.broadcasted_iota(jnp.int32, (places, slots), 0)
    slot_id = lax.broadcasted_iota(jnp.int32, (places, slots), 1)
    live = slot_id < routed_ref[pl.program_id(0)]
    pick = ((index_ref[0] == place) & live).astype(bf16)
    pick = jnp.concatenate([pick] * 3, axis=1)
    added = dot_nn(pick, terms_ref[...])
    out_ref[...] = (base_ref[...].astype(f32) + added).astype(out_ref.dtype)


def spread(routed, index, base, delta, dtype, cuts=2, waits=()):
    seqs, slots = index.shape
    rows, width = base.shape
    block = rows // seqs // cuts
    big = pl.BlockSpec((block, width), lambda i, j, *_: (i * cuts + j, 0))
    return call(
        spread_kernel,
        [index[:, None, :], base, delta],
        waits,
        [routed],
        grid=(seqs, cuts),
        in_specs=[
            pl.BlockSpec((1, 1, slots), lambda i, j, *_: (i, 0, 0)),
            big,
            pl.BlockSpec((slots, width), lambda i, j, *_: (i, 0)),
        ],
        out_specs=big,
        scratch_shapes=[pltpu.VMEM((3 * slots, width), bf16)],
        out_shape=jax.ShapeDtypeStruct((rows, width), dtype),
        compiler_params=params(2),
        name="spread",
        cost_estimate=cost(13),
    )


def add_low(left, right):
    return (left.astype(f32) + right.astype(f32)).astype(bf16)


def swap_nodes(values, bit, nodes):
    return lax.ppermute(values, "seq", [(i, i ^ (1 << bit)) for i in range(nodes)])


def swap_cores(values):
    return lax.ppermute(values, "dp", [(0, 1), (1, 0)])


def halved(kept, got):
    count = kept.shape[0] // 2
    return add_low(kept[count:], got[count:]), add_low(kept[:count], got[:count])


class Chain:
    def __init__(self, send, keep, nodes):
        self.nodes, self.keep = nodes, keep
        self.bits = (nodes // 4).bit_length() - 1
        self.got = swap_cores(send)

    def swap(self):
        for part in range(2):
            top = self.bits - 1 - self.step
            bit = (top + self.bits // 2) % self.bits if part == 0 else top
            self.got[part] = swap_nodes(self.gone[part], bit, self.nodes)
        return list(self.gone)

    def first(self):
        pairs = [halved(self.keep[part], self.got[part]) for part in range(2)]
        self.gone, self.kept = [p[0] for p in pairs], [p[1] for p in pairs]
        self.got, self.step = [None, None], 0
        return self.swap()

    def second(self):
        sent = []
        while self.step < self.bits - 1:
            pairs = [halved(self.kept[part], self.got[part]) for part in range(2)]
            self.gone, self.kept = [p[0] for p in pairs], [p[1] for p in pairs]
            self.step += 1
            sent = self.swap()
        return sent

    def third(self):
        pairs = [halved(self.kept[part], self.got[part]) for part in range(2)]
        gone = jnp.stack([p[0] for p in pairs], axis=1)
        self.kept = [p[1] for p in pairs]
        self.got = swap_nodes(gone, self.bits, self.nodes)
        return [gone]

    def fourth(self):
        pairs = [halved(self.kept[part], self.got[:, part]) for part in range(2)]
        gone = jnp.stack([p[0] for p in pairs], axis=1)
        self.kept = [p[1] for p in pairs]
        self.got = swap_nodes(gone, self.bits + 1, self.nodes)
        return [gone]

    def sums(self):
        return [
            self.kept[part][0].astype(f32) + self.got[0, part].astype(f32) for part in range(2)
        ]


def on_device(
    tokens,
    lengths,
    routed_index,
    out_grad,
    gain_attn,
    w_router,
    w_query,
    w_key,
    w_value,
    w_out,
    gain_mlp,
    w_up,
    w_down,
):
    nodes = lax.axis_size("seq")
    width = tokens.shape[2]
    me = jnp.stack([lax.axis_index("dp"), lax.axis_index("seq")]).astype(jnp.int32)
    routed = lengths[0] // 8
    index = routed_index[0]
    inputs, cotangent = tokens[0], out_grad[0]
    (
        chosen, first_in, queries, keys, values, probs, mix, attn_out, second_in, pulled, mlp_grad, score,
    ) = front(
        routed, index, inputs, cotangent, gain_attn, w_router, gain_mlp, w_query, w_key, w_value, w_out
    )
    hidden_act, pre_grad, down_send, down_keep = up_all(
        me, second_in, mlp_grad, w_up, w_down, nodes
    )
    down = Chain(down_send, down_keep, nodes)
    second_grad = hidden_sum(pre_grad, w_up, True)
    query_grad, key_grad, value_grad, attn_grad, after_grad, gain_mlp_sum = back(
        chosen, attn_out, score, pulled, second_grad, gain_mlp, queries, keys, values, probs, w_out,
        waits=down.first(),
    )
    square_send, square_keep = square_grads(
        me, query_grad, key_grad, value_grad, attn_grad, first_in, mix, nodes
    )
    flatten = lambda terms: terms.reshape(2, nodes, -1, width // 2)
    square = Chain(flatten(square_send), flatten(square_keep), nodes)
    up_send, up_keep = up_grad(me, pre_grad, second_in, nodes, waits=down.second())
    up = Chain(up_send, up_keep, nodes)
    mlp_out = hidden_sum(hidden_act, w_down, False, waits=down.third() + square.first())
    weighted, chosen_grad, gain_attn_sum, router_sum = last(
        chosen, attn_out, mlp_out, score, pulled, after_grad, query_grad, key_grad, value_grad,
        gain_attn, w_router, w_query, w_key, w_value, waits=down.fourth() + up.first(),
    )
    vectors = jnp.sum(jnp.stack([gain_attn_sum, router_sum, gain_mlp_sum]), axis=1)
    vectors = vectors.reshape(3, 2 * nodes, -1).transpose(1, 0, 2)
    vectors = lax.all_to_all(vectors, ("seq", "dp"), 0, 0, tiled=True)
    mixed_out = spread(routed, index, inputs, weighted, bf16, waits=square.second())
    token_grad = spread(
        routed, index, cotangent, chosen_grad, f32, waits=square.third() + up.second()
    )
    square.fourth()
    up.third()
    up.fourth()
    vectors = jnp.sum(vectors, axis=0)
    down_sum, up_sum = down.sums(), up.sums()
    square_sum = [part.reshape(4, -1, width // 2) for part in square.sums()]
    turned = lambda parts: jnp.concatenate([part.T for part in parts], axis=0)
    return (
        mixed_out[None],
        token_grad[None],
        vectors[0],
        vectors[1],
        turned([part[0] for part in square_sum]),
        turned([part[1] for part in square_sum]),
        turned([part[2] for part in square_sum]),
        turned([part[3] for part in square_sum]),
        vectors[2],
        turned(up_sum),
        turned(down_sum),
    )


def solution(mesh):
    in_specs = (
        P("dp", "seq", None),
        P("dp", "seq"),
        P("dp", "seq", None),
        P("dp", "seq", None),
        P(),
        P(),
        P(),
        P(),
        P(),
        P(),
        P(),
        P(),
        P(),
    )
    out_specs = (
        P("dp", "seq", None),
        P("dp", "seq", None),
        P(("seq", "dp")),
        P(("seq", "dp")),
        P(None, ("seq", "dp")),
        P(None, ("seq", "dp")),
        P(None, ("seq", "dp")),
        P(None, ("seq", "dp")),
        P(("seq", "dp")),
        P(None, ("seq", "dp")),
        P(None, ("seq", "dp")),
    )
    return jax.shard_map(
        on_device, mesh=mesh, in_specs=in_specs, out_specs=out_specs, check_vma=False
    )
```

```python
import functools

import jax
import jax.experimental.pallas as pl
import jax.experimental.pallas.tpu as pltpu
import jax.numpy as jnp
from jax import lax
from jax.sharding import PartitionSpec as P

H = 16
norm_eps = 1e-05
f32 = jnp.float32
bf16 = jnp.bfloat16
VMEM_BYTES = 58 * 1024 * 1024


def params(count=1):
    return pltpu.CompilerParams(
        dimension_semantics=("arbitrary",) * count, vmem_limit_bytes=VMEM_BYTES
    )


def cost(micros):
    return pl.CostEstimate(
        flops=int(micros * 1e8), bytes_accessed=int(micros * 3.5e5), transcendentals=0
    )


def call(kernel, arrays, waits=(), scalars=(), **rest):
    first = len(scalars) + len(arrays)

    def body(*refs):
        kernel(*refs[:first], *refs[first + len(waits) :])

    grid = pltpu.PrefetchScalarGridSpec(
        num_scalar_prefetch=len(scalars),
        grid=rest.pop("grid"),
        in_specs=list(rest.pop("in_specs")) + [pl.BlockSpec(memory_space=pl.ANY)] * len(waits),
        out_specs=rest.pop("out_specs"),
        scratch_shapes=rest.pop("scratch_shapes", ()),
    )
    return pl.pallas_call(body, grid_spec=grid, **rest)(*scalars, *arrays, *waits)


def whole(array):
    rank = len(array.shape)
    return pl.BlockSpec(array.shape, lambda *_: (0,) * rank, pipeline_mode=pl.Buffered(1))


def dot_nn(left, right):
    return lax.dot_general(left, right, (((1,), (0,)), ((), ())), preferred_element_type=f32)


def dot_nt(left, right):
    return lax.dot_general(left, right, (((1,), (1,)), ((), ())), preferred_element_type=f32)


def dot_tn(left, right):
    return lax.dot_general(left, right, (((0,), (0,)), ((), ())), preferred_element_type=f32)


def inv_rms(values):
    return lax.rsqrt(jnp.mean(values * values, axis=-1, keepdims=True) + norm_eps)


GROUP = 4


def flat_row(ref):
    values = ref[...].astype(f32)
    return jnp.concatenate([values[i : i + 1] for i in range(values.shape[0])], axis=1)


def fold(values):
    rows, width = values.shape
    return jnp.sum(values.reshape(rows // 8, 8, width), axis=0)


class Copies:
    def __init__(self, sems):
        self.sems, self.count, self.sent = sems, 0, []

    def start(self, source, target):
        copy = pltpu.make_async_copy(source, target, self.sems.at[self.count])
        self.count += 1
        copy.start()
        return copy

    def send(self, source, target):
        self.sent.append(self.start(source, target))

    def finish(self):
        for copy in self.sent:
            copy.wait()


HBM = pl.BlockSpec(memory_space=pl.ANY)


def stacked(rows, head):
    lane_head = lax.broadcasted_iota(jnp.int32, rows.shape, 1) // head
    zero = jnp.zeros_like(rows)
    return jnp.concatenate([jnp.where(lane_head == h, rows, zero) for h in range(GROUP)], axis=0)


def unstacked(rows, head):
    slots = rows.shape[0] // GROUP
    lane_head = lax.broadcasted_iota(jnp.int32, (slots, rows.shape[1]), 1) // head
    out = rows[:slots]
    for h in range(1, GROUP):
        out = jnp.where(lane_head == h, rows[h * slots : (h + 1) * slots], out)
    return out


def front_kernel(
    lengths_ref, index_ref, gain_one_ref, router_ref, gain_two_ref,
    tokens_hbm, cotangent_hbm, query_hbm, key_hbm, value_hbm, out_hbm,
    chosen_out, lefts_out, queries_out, keys_out, values_out, probs_out, attn_out, feed_out, pulled_out,
    score_out,
    tokens, cotangent, query_w, key_w, value_w, out_w,
    chosen, lefts, queries, keys, values, probs, attn, feed, pulled, score, sems,
):
    copies = Copies(sems)
    seqs, _, slots = index_ref.shape
    places, width = tokens.shape[1], tokens.shape[2]
    head = width // H
    arriving = []
    for seq in range(seqs):
        part = pl.ds(seq * places, places)
        arriving.append(
            [
                copies.start(tokens_hbm.at[part], tokens.at[seq]),
                copies.start(cotangent_hbm.at[part], cotangent.at[seq]),
            ]
        )
    weights = [
        copies.start(*pair)
        for pair in (
            (query_hbm, query_w), (key_hbm, key_w), (value_hbm, value_w), (out_hbm, out_w),
        )
    ]
    gain_one, router, gain_two = [flat_row(r) for r in (gain_one_ref, router_ref, gain_two_ref)]
    slot_id = lax.broadcasted_iota(jnp.int32, (slots, places), 0)
    place_id = lax.broadcasted_iota(jnp.int32, (slots, places), 1)
    square = (slots, slots)
    diagonal = lax.broadcasted_iota(jnp.int32, square, 0) == lax.broadcasted_iota(jnp.int32, square, 1)
    for seq in range(seqs):
        rows = slice(seq * slots, (seq + 1) * slots)
        routed = lax.div(lengths_ref[0, seq], 8)
        index = jnp.sum(jnp.where(diagonal, index_ref[seq], 0), axis=1, keepdims=True)
        pick = ((index == place_id) & (slot_id < routed)).astype(bf16)
        arriving[seq][0].wait()
        wide = dot_nn(pick, tokens[seq])
        chosen[rows] = wide.astype(bf16)
        logit = jnp.sum(wide * router, axis=-1, keepdims=True)
        chance = 1.0 / (1.0 + jnp.exp(-logit))
        score[rows] = jnp.broadcast_to(chance, (slots, score.shape[1]))
        lefts[0, rows] = (wide * inv_rms(wide) * gain_one).astype(bf16)
        arriving[seq][1].wait()
        pull = dot_nn(pick, cotangent[seq])
        pulled[rows] = pull.astype(bf16)
        feed[1, rows] = (chance * pull).astype(bf16)
    copies.send(chosen, chosen_out)
    copies.send(pulled, pulled_out)
    copies.send(score, score_out)
    copies.send(feed.at[1], feed_out.at[1])
    copies.send(lefts.at[0], lefts_out.at[0])
    first = lefts[0]
    weights[0].wait()
    queries[...] = (dot_nn(first, query_w[...]) * 0.125).astype(bf16)
    copies.send(queries, queries_out)
    weights[1].wait()
    keys[...] = dot_nn(first, key_w[...]).astype(bf16)
    copies.send(keys, keys_out)
    weights[2].wait()
    values[...] = dot_nn(first, value_w[...]).astype(bf16)
    copies.send(values, values_out)
    stack = GROUP * slots
    row_id = lax.broadcasted_iota(jnp.int32, (stack, slots), 0) % slots
    col_id = lax.broadcasted_iota(jnp.int32, (stack, slots), 1)
    for seq in range(seqs):
        rows = slice(seq * slots, (seq + 1) * slots)
        allowed = (col_id <= row_id) & (col_id < lax.div(lengths_ref[0, seq], 8))
        for g in range(H // GROUP):
            lanes = slice(g * GROUP * head, (g + 1) * GROUP * head)
            scores = dot_nt(stacked(queries[rows, lanes], head), keys[rows, lanes])
            scores = jnp.where(allowed, scores, -1e30)
            exped = jnp.exp(scores - jnp.max(scores, axis=-1, keepdims=True))
            chances = (exped / jnp.sum(exped, axis=-1, keepdims=True)).astype(bf16)
            probs[seq, g] = chances
            mixed = dot_nn(chances, values[rows, lanes])
            lefts[1, rows, lanes] = unstacked(mixed, head).astype(bf16)
        copies.send(probs.at[seq], probs_out.at[seq])
    copies.send(lefts.at[1], lefts_out.at[1])
    weights[3].wait()
    attn[...] = dot_nn(lefts[1], out_w[...])
    copies.send(attn, attn_out)
    for seq in range(seqs):
        rows = slice(seq * slots, (seq + 1) * slots)
        after = chosen[rows].astype(f32) + attn[rows]
        feed[0, rows] = (after * inv_rms(after) * gain_two).astype(bf16)
    copies.send(feed.at[0], feed_out.at[0])
    copies.finish()


def front(lengths, index, tokens, cotangent, vectors, wq, wk, wv, wo):
    seqs, slots = index.shape
    places, width = tokens.shape[0] // seqs, tokens.shape[1]
    rows = seqs * slots
    low = ((rows, width), bf16)
    outs = [
        low, ((2, rows, width), bf16), low, low, low,
        ((seqs, H // GROUP, GROUP * slots, slots), bf16), ((rows, width), f32),
        ((2, rows, width), bf16), low, ((rows, 128), f32),
    ]
    small = [index[:, None, :], *vectors]
    return call(
        front_kernel,
        [*small, tokens, cotangent, wq, wk, wv, wo],
        (),
        [lengths],
        grid=(1,),
        in_specs=[whole(array) for array in small] + [HBM] * 6,
        out_specs=[HBM] * len(outs),
        scratch_shapes=[pltpu.VMEM((seqs, places, width), bf16)] * 2
        + [pltpu.VMEM((width, width), bf16)] * 4
        + [pltpu.VMEM(*out) for out in outs]
        + [pltpu.SemaphoreType.DMA((2 * seqs + 4 + 11 + seqs,))],
        out_shape=[jax.ShapeDtypeStruct(*out) for out in outs],
        compiler_params=params(),
        name="front",
        cost_estimate=cost(18),
    )


def gelu_both(z):
    cdf = 0.5 + 0.5 * lax.erf(z * 0.7071067811865476)
    return z * cdf, cdf + z * (jnp.exp(-0.5 * z * z) * 0.3989422804014327)


def link_bits(nodes):
    bits = nodes.bit_length() - 1
    half = (bits - 2) // 2
    return list(range(half)), list(range(half, bits - 2)), [bits - 2], [bits - 1]


def link_order(nodes, names):
    x, y, near, far = link_bits(nodes)
    return sum([{"x": x, "y": y, "n": near, "f": far}[name] for name in names], [])


def spot_of(rel, order):
    return sum(((rel >> bit) & 1) << (len(order) - 1 - i) for i, bit in enumerate(order))


def own_blocks(me_ref, source, size, nodes):
    core, node = me_ref[0], me_ref[1]
    for rel in range(nodes):
        owner = lax.bitwise_xor(node, rel) * 2
        starts = [pl.multiple_of((owner + side) * size, size) for side in (core, 1 - core)]
        yield rel, *[source[pl.ds(start, size), :].astype(bf16) for start in starts]


def held_type(size):
    return bf16 if size % 16 == 0 else f32


def feed_kernel(me_ref, own_ref, other_ref, *refs, nodes, pieces, orders):
    ups, downs, refs = refs[:pieces], refs[pieces : 2 * pieces], refs[2 * pieces :]
    (
        sums_ref, sent_ref, down_gone, down_kept, up_gone, up_kept,
        rows_ref, grads_ref, turned_ref, down_terms, up_terms, grad_sum, out_sum,
    ) = refs
    step, steps = pl.program_id(0), pl.num_programs(0)
    node = me_ref[1]
    flat = nodes // 4
    count = own_ref.shape[1]

    @pl.when(step == 0)
    def _():
        rows_ref[:count] = own_ref[0]
        rows_ref[count:] = other_ref[0]
        grads_ref[:count] = own_ref[1]
        grads_ref[count:] = other_ref[1]
        turned_ref[...] = grads_ref[...].T
        out_sum[...] = jnp.zeros_like(out_sum)
        grad_sum[...] = jnp.zeros_like(grad_sum)

    w_up = jnp.concatenate([ref[...] for ref in ups], axis=1)
    w_down = jnp.concatenate([ref[...] for ref in downs], axis=0)
    hidden = dot_nn(rows_ref[...], w_up)
    act, slope = gelu_both(hidden)
    act = act.astype(bf16)
    pre = (dot_nt(grads_ref[...], w_down) * slope).astype(bf16)

    down_terms[...] = dot_nn(turned_ref[...], act).astype(down_terms.dtype)
    size = down_terms.shape[0] // nodes
    for rel in range(nodes):
        spot = spot_of(rel, orders[0])
        start = pl.multiple_of(lax.bitwise_xor(node, rel) * size, size)
        values = down_terms[pl.ds(start, size), :].astype(bf16)
        (down_kept, down_gone)[spot // (nodes // 2)][spot % (nodes // 2)] = values

    up_terms[...] = dot_tn(pre, rows_ref[...]).astype(up_terms.dtype)
    size = up_kept.shape[2]
    for rel in range(flat):
        spot = spot_of(rel, orders[1][:-2])
        start = pl.multiple_of(lax.bitwise_xor(lax.rem(node, flat), rel) * size, size)
        values = up_terms[pl.ds(start, size), :].astype(bf16)
        (up_kept, up_gone)[spot // (flat // 2)][spot % (flat // 2), 0] = values

    out_sum[...] += dot_nn(act, w_down)
    grad_sum[...] += dot_nt(pre, w_up)

    @pl.when(step == steps - 1)
    def _():
        for i, total in enumerate((grad_sum, out_sum)):
            sums_ref[i] = total[:count].astype(bf16)
            sent_ref[i] = total[count:].astype(bf16)


def feed(me, own, other, w_up, w_down, nodes, orders, steps=4, waits=()):
    _, rows, width = own.shape
    hidden = w_up.shape[1]
    flat = nodes // 4
    size = hidden // (2 * nodes)
    block = hidden // 2 // steps
    if size % 128:
        w_up = lax.dynamic_index_in_dim(w_up.reshape(width, nodes, 2, size), me[0], 2, False)
        w_down = lax.dynamic_index_in_dim(w_down.reshape(nodes, 2, size, width), me[0], 1, False)
        w_up, w_down = w_up.reshape(width, -1), w_down.reshape(-1, width)
        pieces = 1
        place = lambda piece, i, me: i
    else:
        pieces = block // size
        place = lambda piece, i, me: (i * pieces + piece) * 2 + me[0]
    columns = block // pieces
    up_specs = [
        pl.BlockSpec((width, columns), lambda i, me, p=p: (0, place(p, i, me)))
        for p in range(pieces)
    ]
    down_specs = [
        pl.BlockSpec((columns, width), lambda i, me, p=p: (place(p, i, me), 0))
        for p in range(pieces)
    ]
    chunk = width // nodes
    down_spec = pl.BlockSpec((nodes // 2, chunk, block), lambda i, me: (0, 0, i))
    rel = lambda i, me: lax.bitwise_xor(i, lax.div(me[1], flat))
    up_spec = pl.BlockSpec(
        (flat // 2, 1, size, width),
        lambda i, me: (0, lax.rem(rel(i, me), 2) * 2 + lax.div(rel(i, me), 2), 0, 0),
    )
    pair = jax.ShapeDtypeStruct((2, rows, width), bf16)
    return call(
        functools.partial(feed_kernel, nodes=nodes, pieces=pieces, orders=orders),
        [own, other] + [w_up] * pieces + [w_down] * pieces,
        waits,
        [me],
        grid=(steps,),
        in_specs=[whole(own), whole(other)] + up_specs + down_specs,
        out_specs=[pl.BlockSpec((2, rows, width), lambda i, me: (0, 0, 0))] * 2
        + [down_spec, down_spec, up_spec, up_spec],
        scratch_shapes=[
            pltpu.VMEM((2 * rows, width), bf16),
            pltpu.VMEM((2 * rows, width), bf16),
            pltpu.VMEM((width, 2 * rows), bf16),
            pltpu.VMEM((width, block), held_type(chunk)),
            pltpu.VMEM((block, width), held_type(size)),
            pltpu.VMEM((2 * rows, width), f32),
            pltpu.VMEM((2 * rows, width), f32),
        ],
        out_shape=[pair] * 2
        + [jax.ShapeDtypeStruct((nodes // 2, chunk, hidden // 2), bf16)] * 2
        + [jax.ShapeDtypeStruct((flat // 2, 4, size, width), bf16)] * 2,
        compiler_params=params(),
        name="feed",
        cost_estimate=cost(34),
    )


def back_kernel(
    me_ref, gain_ref, chosen_hbm, attn_hbm, score_hbm, pulled_hbm, own_hbm, other_hbm, queries_hbm,
    keys_hbm, values_hbm, probs_hbm, lefts_hbm, out_hbm,
    grads_out, after_out, gain_out, send_gone_out, send_stay_out, keep_gone_out, keep_stay_out,
    send_b_out, keep_b_out,
    chosen, attn, score, pulled, own, other, queries, keys, values, probs, lefts, out_w,
    grads, after_grad, send_gone, send_stay, keep_gone, keep_stay, send_b, keep_b,
    attn_grad, mix_grad, terms, sems,
    *, nodes, orders,
):
    copies = Copies(sems)
    fetched = {}
    for name, source, target in (
        ("rows", chosen_hbm, chosen), ("rows", attn_hbm, attn), ("rows", own_hbm.at[0], own),
        ("rows", other_hbm.at[0], other), ("rows", score_hbm, score), ("rows", pulled_hbm, pulled),
        ("out", out_hbm, out_w), ("heads", queries_hbm, queries), ("heads", keys_hbm, keys),
        ("heads", values_hbm, values), ("heads", probs_hbm, probs), ("lefts", lefts_hbm, lefts),
    ):
        fetched.setdefault(name, []).append(copies.start(source, target))

    def arrive(name):
        for copy in fetched[name]:
            copy.wait()

    seqs, groups, stack, slots = probs.shape
    width = chosen.shape[1]
    head = width // H
    gain = flat_row(gain_ref)
    arrive("rows")
    for seq in range(seqs):
        rows = slice(seq * slots, (seq + 1) * slots)
        after = chosen[rows].astype(f32) + attn[rows]
        inv = inv_rms(after)
        normed = after * inv
        arrived = add_low(own[rows], other[rows]).astype(f32)
        total = fold(arrived * normed)
        gain_out[...] = total if seq == 0 else gain_out[...] + total
        weighted = arrived * gain
        back = inv * (weighted - normed * jnp.mean(weighted * normed, axis=-1, keepdims=True))
        after_grad[rows] = back
        delta = score[rows, :1] * pulled[rows].astype(f32)
        attn_grad[rows] = (delta + back).astype(bf16)
    copies.send(after_grad, after_out)
    arrive("out")
    mix_grad[...] = dot_nt(attn_grad[...], out_w[...]).astype(bf16)
    arrive("heads")
    for seq in range(seqs):
        rows = slice(seq * slots, (seq + 1) * slots)
        for g in range(groups):
            lanes = slice(g * GROUP * head, (g + 1) * GROUP * head)
            chances = probs[seq, g]
            wide = chances.astype(f32)
            stacked_queries = stacked(queries[rows, lanes], head)
            stacked_grads = stacked(mix_grad[rows, lanes], head)
            prob_grad = dot_nt(stacked_grads, values[rows, lanes])
            total = jnp.sum(prob_grad * wide, axis=-1, keepdims=True)
            score_grad = (wide * (prob_grad - total)).astype(bf16)
            grads[2, rows, lanes] = dot_tn(chances, stacked_grads).astype(bf16)
            grads[1, rows, lanes] = dot_tn(score_grad, stacked_queries).astype(bf16)
            grads[0, rows, lanes] = unstacked(dot_nn(score_grad, keys[rows, lanes]), head).astype(bf16)
    copies.send(grads, grads_out)
    arrive("lefts")
    half, cut = nodes // 2, send_gone.shape[3]
    outs = (
        (send_gone, send_gone_out), (keep_gone, keep_gone_out), (send_stay, send_stay_out),
        (keep_stay, keep_stay_out), (send_b, send_b_out), (keep_b, keep_b_out),
    )
    for which in range(4):
        if which < 3:
            product = dot_tn(grads[which], lefts[0])
        else:
            product = dot_tn(attn_grad[...], lefts[1])
        terms[...] = (product * 0.125 if which == 0 else product).astype(terms.dtype)
        for rel, kept, sent in own_blocks(me_ref, terms, send_b.shape[2], nodes):
            spot = spot_of(rel, orders[0])
            (keep_stay, keep_gone)[spot // half][spot % half, which] = kept[:, :cut]
            (send_stay, send_gone)[spot // half][spot % half, which] = sent[:, :cut]
            spot = spot_of(rel, orders[1])
            keep_b[spot, which] = kept[:, cut:]
            send_b[spot, which] = sent[:, cut:]
        for held, target in outs:
            copies.send(held.at[:, which], target.at[:, which])
    copies.finish()


def back(
    me, chosen, attn, score, pulled, own, other, gain, queries, keys, values, probs, lefts, w_out, nodes,
    orders, cut,
):
    rows, width = chosen.shape
    seqs, _, _, slots = probs.shape
    size = width // (2 * nodes)
    layout = [(nodes // 2, cut)] * 4 + [(nodes, width - cut)] * 2
    shapes = [((count, 4, size, columns), bf16) for count, columns in layout]
    outs = [((3, rows, width), bf16), ((rows, width), f32)]
    fetched = [chosen, attn, score, pulled, own, other, queries, keys, values, probs, lefts, w_out]
    held = [pltpu.VMEM(array.shape, array.dtype) for array in fetched]
    held[4] = held[5] = pltpu.VMEM((rows, width), bf16)
    return call(
        functools.partial(back_kernel, nodes=nodes, orders=orders),
        [gain, *fetched],
        (),
        [me],
        grid=(1,),
        in_specs=[whole(gain)] + [HBM] * len(fetched),
        out_specs=[HBM, HBM, pl.BlockSpec((8, width), lambda *_: (0, 0))] + [HBM] * 6,
        scratch_shapes=held
        + [pltpu.VMEM(*out) for out in outs + shapes]
        + [pltpu.VMEM((rows, width), bf16)] * 2
        + [pltpu.VMEM((width, width), held_type(size))]
        + [pltpu.SemaphoreType.DMA((len(fetched) + 2 + 24,))],
        out_shape=[jax.ShapeDtypeStruct(*out) for out in outs]
        + [jax.ShapeDtypeStruct((8, width), f32)]
        + [jax.ShapeDtypeStruct(*shape) for shape in shapes],
        compiler_params=params(),
        name="back",
        cost_estimate=cost(20),
    )


def last_kernel(
    gain_ref, router_ref, chosen_hbm, attn_hbm, own_hbm, other_hbm, score_hbm, pulled_hbm, after_hbm,
    grads_hbm, query_hbm, key_hbm, value_hbm,
    chosen_grad_out, gain_out, router_out,
    chosen, attn, own, other, score, pulled, after_grad, grads, query_w, key_w, value_w,
    first_grad, chosen_grad, sems,
):
    copies = Copies(sems)
    weights = ((query_hbm, query_w), (key_hbm, key_w), (value_hbm, value_w))
    pairs = [
        (copies.start(grads_hbm.at[i], grads.at[i]), copies.start(*weight))
        for i, weight in enumerate(weights)
    ]
    others = [
        copies.start(*pair)
        for pair in (
            (chosen_hbm, chosen), (attn_hbm, attn), (own_hbm.at[1], own), (other_hbm.at[1], other),
            (score_hbm, score), (pulled_hbm, pulled), (after_hbm, after_grad),
        )
    ]
    gain, router = flat_row(gain_ref), flat_row(router_ref)
    for i, pair in enumerate(pairs):
        for copy in pair:
            copy.wait()
        product = dot_nt(grads[i], weights[i][1][...])
        if i == 0:
            first_grad[...] = product * 0.125
        else:
            first_grad[...] += product
    for copy in others:
        copy.wait()
    rows = chosen.shape[0]
    block = rows // 4
    for i in range(4):
        part = slice(i * block, (i + 1) * block)
        wide = chosen[part].astype(f32)
        chance = score[part, :1]
        branch = attn[part] + add_low(own[part], other[part]).astype(f32)
        pull = jnp.sum(pulled[part].astype(f32) * branch, axis=-1, keepdims=True)
        logit_grad = pull * chance * (1.0 - chance)
        arrived = first_grad[part]
        inv = inv_rms(wide)
        normed = wide * inv
        weighted = arrived * gain
        chosen_grad[part] = (
            inv * (weighted - normed * jnp.mean(weighted * normed, axis=-1, keepdims=True))
            + after_grad[part]
            + logit_grad * router
        )
        copies.send(chosen_grad.at[pl.ds(i * block, block)], chosen_grad_out.at[pl.ds(i * block, block)])
        gain_sum, router_sum = fold(arrived * normed), fold(logit_grad * wide)
        gain_out[...] = gain_sum if i == 0 else gain_out[...] + gain_sum
        router_out[...] = router_sum if i == 0 else router_out[...] + router_sum
    copies.finish()


def last(
    chosen, attn, own, other, score, pulled, after_grad, grads, gain, router, wq, wk, wv, waits=()
):
    rows, width = chosen.shape
    fetched = [chosen, attn, own, other, score, pulled, after_grad, grads, wq, wk, wv]
    held = [pltpu.VMEM(array.shape, array.dtype) for array in fetched]
    held[2] = held[3] = pltpu.VMEM((rows, width), bf16)
    sums = pl.BlockSpec((8, width), lambda *_: (0, 0))
    return call(
        last_kernel,
        [gain, router, *fetched],
        waits,
        grid=(1,),
        in_specs=[whole(gain), whole(router)] + [HBM] * len(fetched),
        out_specs=[HBM, sums, sums],
        scratch_shapes=held
        + [pltpu.VMEM((rows, width), f32)] * 2
        + [pltpu.SemaphoreType.DMA((17,))],
        out_shape=[jax.ShapeDtypeStruct((rows, width), f32)]
        + [jax.ShapeDtypeStruct((8, width), f32)] * 2,
        compiler_params=params(),
        name="last",
        cost_estimate=cost(9),
    )


def spread_kernel(lengths_ref, index_ref, base_hbm, *refs, deltas, pieces):
    deltas_hbm, out_hbm, base, out = refs[:deltas], refs[deltas], refs[deltas + 1], refs[deltas + 2]
    held, sems = refs[deltas + 3 : -1], refs[-1]
    copies = Copies(sems)
    seqs, _, slots = index_ref.shape
    count = base.shape[1]
    arriving = []
    for seq in range(seqs):
        row = pl.ds(seq * slots, slots)
        steps = [
            copies.start(
                source.at[source.shape[0] - 1, row] if len(source.shape) == 3 else source.at[row],
                target.at[row],
            )
            for source, target in zip(deltas_hbm, held)
        ]
        for piece in range(seq * pieces, (seq + 1) * pieces):
            steps.append(copies.start(base_hbm.at[pl.ds(piece * count, count)], base.at[piece]))
        arriving.append(steps)
    for seq in range(seqs):
        rows = slice(seq * slots, (seq + 1) * slots)
        for copy in arriving[seq][:deltas]:
            copy.wait()
        if deltas == 1:
            delta = held[0][rows]
        else:
            score, attn, own, other = held
            delta = score[rows, :1] * (attn[rows] + add_low(own[rows], other[rows]).astype(f32))
        high = delta.astype(bf16)
        low = (delta - high.astype(f32)).astype(bf16)
        both = jnp.concatenate([high, low], axis=0)
        slot_id = lax.broadcasted_iota(jnp.int32, (count, slots), 1)
        live = slot_id < lax.div(lengths_ref[0, seq], 8)
        for piece in range(pieces):
            place = piece * count + lax.broadcasted_iota(jnp.int32, (count, slots), 0)
            pick = ((index_ref[seq] == place) & live).astype(bf16)
            at = seq * pieces + piece
            arriving[seq][deltas + piece].wait()
            added = dot_nn(jnp.concatenate([pick, pick], axis=1), both)
            out[at] = (base[at].astype(f32) + added).astype(out.dtype)
            copies.send(out.at[at], out_hbm.at[pl.ds(at * count, count)])
    copies.finish()


def spread(lengths, index, base, deltas, dtype, waits=(), pieces=2):
    seqs, slots = index.shape
    rows, width = base.shape
    steps = seqs * pieces
    index = index[:, None, :]
    held = [pltpu.VMEM(delta.shape[-2:], delta.dtype) for delta in deltas]
    return call(
        functools.partial(spread_kernel, deltas=len(deltas), pieces=pieces),
        [index, base, *deltas],
        waits,
        [lengths],
        grid=(1,),
        in_specs=[whole(index)] + [HBM] * (1 + len(deltas)),
        out_specs=HBM,
        scratch_shapes=[
            pltpu.VMEM((steps, rows // steps, width), bf16),
            pltpu.VMEM((steps, rows // steps, width), dtype),
            *held,
            pltpu.SemaphoreType.DMA((2 * steps + len(deltas) * seqs,)),
        ],
        out_shape=jax.ShapeDtypeStruct((rows, width), dtype),
        compiler_params=params(),
        name="spread",
        cost_estimate=cost(8),
    )


def add_low(left, right):
    return (left.astype(f32) + right.astype(f32)).astype(bf16)


def swap_nodes(values, bit, nodes):
    return lax.ppermute(values, "seq", [(i, i ^ (1 << bit)) for i in range(nodes)])


def swap_cores(values):
    return lax.ppermute(values, "dp", [(0, 1), (1, 0)])


class Part:
    def __init__(self, order, nodes):
        self.order, self.nodes = order, nodes

    @classmethod
    def halved(cls, gone, kept, order, nodes):
        part = cls(order, nodes)
        part.gone, part.kept = gone, kept
        part.swap()
        return part

    @classmethod
    def of_cores(cls, send, keep, order, nodes):
        part = cls(order, nodes)
        part.kept, part.got = keep, swap_cores(send)
        return part

    @classmethod
    def of_split_cores(cls, send_gone, send_stay, keep_gone, keep_stay, order, nodes):
        part = cls(order, nodes)
        part.halves = (keep_gone, swap_cores(send_gone)), (keep_stay, swap_cores(send_stay))
        return part

    halves = None

    def swap(self):
        self.got = swap_nodes(self.gone, self.order[0], self.nodes)
        self.order = self.order[1:]

    def halve(self, after=()):
        if self.halves:
            (keep_gone, got_gone), (keep_stay, got_stay), *_ = lax.optimization_barrier(
                (*self.halves, *after)
            )
            self.gone, self.kept = add_low(keep_gone, got_gone), add_low(keep_stay, got_stay)
            self.halves = None
            return
        if after:
            self.kept, self.got, *_ = lax.optimization_barrier((self.kept, self.got, *after))
        if self.kept.shape[0] == 1:
            self.kept, self.got = self.kept[0], self.got[0]
        count = self.kept.shape[0] // 2
        halves = [add_low(self.kept[c], self.got[c]) for c in (slice(count, None), slice(count))]
        self.gone, self.kept = [half[0] for half in halves] if count == 1 else halves

    def step(self, after=()):
        self.halve(after)
        self.swap()
        return self.gone


class Chain:
    def __init__(self, parts):
        self.parts = parts

    def step(self, count=1, after=()):
        sent = []
        for _ in range(count):
            sent = [part.step(after) for part in self.parts]
        return sent

    def final(self, after=()):
        for part in self.parts:
            part.halve(after)
        gone = jnp.concatenate([part.gone for part in self.parts], axis=-1)
        self.got = swap_nodes(gone, self.parts[0].order[0], self.parts[0].nodes)
        return [gone]

    def sum(self):
        kept = jnp.concatenate([part.kept for part in self.parts], axis=-1)
        return kept.astype(f32) + self.got.astype(f32)


def both_cores(core, rows, nodes):
    count = rows.shape[0] // 2
    mine, sent = [
        lax.dynamic_slice_in_dim(rows, side * count, count) for side in (core, 1 - core)
    ]
    got = swap_cores(sent)
    shape = (count, nodes, 1, rows.shape[1] // nodes)
    sides = [jnp.where(core == side, mine, got).reshape(shape) for side in (0, 1)]
    return jnp.concatenate(sides, axis=2).reshape(count, -1)


def on_device(
    tokens,
    lengths,
    routed_index,
    out_grad,
    gain_attn,
    w_router,
    w_query,
    w_key,
    w_value,
    w_out,
    gain_mlp,
    w_up,
    w_down,
):
    nodes = lax.axis_size("seq")
    width = tokens.shape[2]
    me = jnp.stack([lax.axis_index("dp"), lax.axis_index("seq")]).astype(jnp.int32)
    index = routed_index[0]
    inputs, cotangent = tokens[0], out_grad[0]
    vectors = [vector.reshape(-1, 128) for vector in (gain_attn, w_router, gain_mlp)]
    (
        chosen, lefts, queries, keys, values, probs, attn_out, feed_own, pulled, score,
    ) = front(
        lengths, index, inputs, cotangent, vectors, w_query, w_key, w_value, w_out
    )
    feed_other = swap_cores(feed_own)
    order = lambda names: link_order(nodes, names)
    span = len(order("x"))
    down_order, up_order = order("xynf"), order("yxnf")
    square_orders = [order("nxyf"), order("xynf")]
    own_sums, other_sums, *terms = feed(
        me, feed_own, feed_other, w_up, w_down, nodes, [down_order, up_order]
    )
    got_sums = swap_cores(other_sums)
    down = Chain([Part.halved(*terms[:2], down_order, nodes)])
    up = Chain([Part.halved(*terms[2:], up_order, nodes)])
    grads, after_grad, gain_mlp_sum, *square_terms = back(
        me, chosen, attn_out, score, pulled, own_sums, got_sums, vectors[2], queries, keys, values, probs,
        lefts, w_out, nodes, square_orders, width * 5 // 8,
    )
    square = Chain(
        [
            Part.of_split_cores(*square_terms[:4], square_orders[0], nodes),
            Part.of_cores(*square_terms[4:], square_orders[1], nodes),
        ]
    )
    mixed_out = spread(
        lengths, index, inputs, [score, attn_out, own_sums, got_sums], bf16, waits=square_terms[:1]
    )
    chosen_grad, gain_attn_sum, router_sum = last(
        chosen, attn_out, own_sums, got_sums, score, pulled, after_grad, grads,
        vectors[0], vectors[1], w_query, w_key, w_value, waits=[mixed_out],
    )
    sums = jnp.sum(jnp.stack([gain_attn_sum, router_sum, gain_mlp_sum]), axis=1)
    sums = sums.reshape(3, 2 * nodes, -1).transpose(1, 0, 2)
    gone = down.step(span, after=[chosen_grad])
    gone += up.step(span, after=gone)
    gone += square.step(after=gone)
    token_grad = spread(lengths, index, cotangent, [chosen_grad], f32, waits=gone)
    gone = down.step(span, after=[token_grad])
    gone = up.step(span, after=gone)
    gone = square.step(span, after=gone)
    gone = down.final(after=gone)
    gone = up.final(after=gone)
    gone = square.step(span, after=gone)
    down_sum, _ = lax.optimization_barrier((both_cores(me[0], down.sum(), nodes), gone[0]))
    gone = square.final(after=[up.sum()])
    sums, *_ = lax.optimization_barrier((sums, *gone))
    sums = jnp.sum(lax.all_to_all(sums, ("seq", "dp"), 0, 0, tiled=True), axis=0)
    square_sum = square.sum()
    return (
        mixed_out[None],
        token_grad[None],
        sums[0],
        sums[1],
        *[square_sum[which].T for which in range(4)],
        sums[2],
        up.sum().T,
        down_sum.T,
    )


def solution(mesh):
    in_specs = (
        P("dp", "seq", None),
        P("dp", "seq"),
        P("dp", "seq", None),
        P("dp", "seq", None),
        P(),
        P(),
        P(),
        P(),
        P(),
        P(),
        P(),
        P(),
        P(),
    )
    out_specs = (
        P("dp", "seq", None),
        P("dp", "seq", None),
        P(("seq", "dp")),
        P(("seq", "dp")),
        P(None, ("seq", "dp")),
        P(None, ("seq", "dp")),
        P(None, ("seq", "dp")),
        P(None, ("seq", "dp")),
        P(("seq", "dp")),
        P(None, ("seq", "dp")),
        P(None, ("seq", "dp")),
    )
    return jax.shard_map(
        on_device, mesh=mesh, in_specs=in_specs, out_specs=out_specs, check_vma=False
    )
```

```python
import functools

import jax
import jax.experimental.pallas as pl
import jax.experimental.pallas.tpu as pltpu
import jax.numpy as jnp
from jax import lax
from jax.sharding import PartitionSpec as P

H = 16
norm_eps = 1e-05
f32 = jnp.float32
bf16 = jnp.bfloat16


def params(mebibytes):
    return pltpu.CompilerParams(
        dimension_semantics=("arbitrary",), vmem_limit_bytes=mebibytes * 1024 * 1024
    )


def cost(micros):
    return pl.CostEstimate(
        flops=int(micros * 1e8), bytes_accessed=int(micros * 3.5e5), transcendentals=0
    )


def call(kernel, arrays, waits=(), scalars=(), **rest):
    first = len(scalars) + len(arrays)

    def body(*refs):
        kernel(*refs[:first], *refs[first + len(waits) :])

    grid = pltpu.PrefetchScalarGridSpec(
        num_scalar_prefetch=len(scalars),
        grid=rest.pop("grid"),
        in_specs=list(rest.pop("in_specs")) + [pl.BlockSpec(memory_space=pl.ANY)] * len(waits),
        out_specs=rest.pop("out_specs"),
        scratch_shapes=rest.pop("scratch_shapes", ()),
    )
    return pl.pallas_call(body, grid_spec=grid, **rest)(*scalars, *arrays, *waits)


def whole(array):
    rank = len(array.shape)
    return pl.BlockSpec(array.shape, lambda *_: (0,) * rank, pipeline_mode=pl.Buffered(1))


def dot_nn(left, right):
    return lax.dot_general(left, right, (((1,), (0,)), ((), ())), preferred_element_type=f32)


def dot_nt(left, right):
    return lax.dot_general(left, right, (((1,), (1,)), ((), ())), preferred_element_type=f32)


def dot_tn(left, right):
    return lax.dot_general(left, right, (((0,), (0,)), ((), ())), preferred_element_type=f32)


def inv_rms(values):
    return lax.rsqrt(jnp.mean(values * values, axis=-1, keepdims=True) + norm_eps)


GROUP = 4


def flat_row(ref):
    values = ref[...].astype(f32)
    return jnp.concatenate([values[i : i + 1] for i in range(values.shape[0])], axis=1)


def fold(values):
    rows, width = values.shape
    return jnp.sum(values.reshape(rows // 8, 8, width), axis=0)


class Copies:
    def __init__(self, sems):
        self.sems, self.count, self.sent = sems, 0, []

    def one(self, source, target):
        self.count += 1
        return pltpu.make_async_copy(source, target, self.sems.at[self.count - 1])

    def group(self, turns, pair):
        first = self.count
        self.count += turns

        def at(turn):
            source, target = pair(turn)
            return pltpu.make_async_copy(source, target, self.sems.at[first + turn])

        return at

    def start(self, source, target):
        copy = self.one(source, target)
        copy.start()
        return copy

    def send(self, source, target):
        self.sent.append(self.start(source, target))

    def send_group(self, turns, pair):
        at = self.group(turns, pair)
        self.sent += [at(turn) for turn in range(turns)]
        return at

    def finish(self):
        for copy in self.sent:
            copy.wait()


def repeat(turns, body):
    lax.fori_loop(0, turns, lambda turn, carry: body(turn), None)


def block_of(turn, size):
    return pl.ds(pl.multiple_of(turn * size, size), size)


HBM = pl.BlockSpec(memory_space=pl.ANY)


def stacked(rows, head):
    lane_head = lax.broadcasted_iota(jnp.int32, rows.shape, 1) // head
    zero = jnp.zeros_like(rows)
    return jnp.concatenate([jnp.where(lane_head == h, rows, zero) for h in range(GROUP)], axis=0)


def unstacked(rows, head):
    slots = rows.shape[0] // GROUP
    lane_head = lax.broadcasted_iota(jnp.int32, (slots, rows.shape[1]), 1) // head
    out = rows[:slots]
    for h in range(1, GROUP):
        out = jnp.where(lane_head == h, rows[h * slots : (h + 1) * slots], out)
    return out


def front_kernel(
    lengths_ref, index_ref, gain_one_ref, router_ref, gain_two_ref,
    tokens_hbm, cotangent_hbm, query_hbm, key_hbm, value_hbm, out_hbm,
    chosen_out, lefts_out, queries_out, keys_out, values_out, probs_out, attn_out, feed_out, pulled_out,
    score_out,
    tokens, cotangent, query_w, key_w, value_w, out_w,
    chosen, lefts, queries, keys, values, probs, attn, feed, pulled, score, sems,
):
    copies = Copies(sems)
    seqs, _, slots = index_ref.shape
    places, width = tokens.shape[1], tokens.shape[2]
    head = width // H
    token_copy = copies.group(
        seqs, lambda seq: (tokens_hbm.at[block_of(seq, places)], tokens.at[seq])
    )
    cotangent_copy = copies.group(
        seqs, lambda seq: (cotangent_hbm.at[block_of(seq, places)], cotangent.at[seq])
    )
    for seq in range(seqs):
        token_copy(seq).start()
        cotangent_copy(seq).start()
    weights = [
        copies.start(*pair)
        for pair in (
            (query_hbm, query_w), (key_hbm, key_w), (value_hbm, value_w), (out_hbm, out_w),
        )
    ]
    gain_one, router, gain_two = [flat_row(r) for r in (gain_one_ref, router_ref, gain_two_ref)]

    def gather(seq):
        rows = block_of(seq, slots)
        slot_id = lax.broadcasted_iota(jnp.int32, (slots, places), 0)
        place_id = lax.broadcasted_iota(jnp.int32, (slots, places), 1)
        square = (slots, slots)
        diagonal = lax.broadcasted_iota(jnp.int32, square, 0) == lax.broadcasted_iota(
            jnp.int32, square, 1
        )
        routed = lax.div(lengths_ref[0, seq], 8)
        index = jnp.sum(jnp.where(diagonal, index_ref[seq], 0), axis=1, keepdims=True)
        pick = ((index == place_id) & (slot_id < routed)).astype(bf16)
        token_copy(seq).wait()
        wide = dot_nn(pick, tokens[seq])
        chosen[rows] = wide.astype(bf16)
        logit = jnp.sum(wide * router, axis=-1, keepdims=True)
        chance = 1.0 / (1.0 + jnp.exp(-logit))
        score[rows] = jnp.broadcast_to(chance, (slots, score.shape[1]))
        lefts[0, rows] = (wide * inv_rms(wide) * gain_one).astype(bf16)
        cotangent_copy(seq).wait()
        pull = dot_nn(pick, cotangent[seq])
        pulled[rows] = pull.astype(bf16)
        feed[1, rows] = (chance * pull).astype(bf16)

    repeat(seqs, gather)
    copies.send(chosen, chosen_out)
    copies.send(pulled, pulled_out)
    copies.send(score, score_out)
    copies.send(feed.at[1], feed_out.at[1])
    copies.send(lefts.at[0], lefts_out.at[0])
    first = lefts[0]
    weights[0].wait()
    queries[...] = (dot_nn(first, query_w[...]) * 0.125).astype(bf16)
    copies.send(queries, queries_out)
    weights[1].wait()
    keys[...] = dot_nn(first, key_w[...]).astype(bf16)
    copies.send(keys, keys_out)
    weights[2].wait()
    values[...] = dot_nn(first, value_w[...]).astype(bf16)
    copies.send(values, values_out)
    probs_copy = copies.send_group(seqs, lambda seq: (probs.at[seq], probs_out.at[seq]))

    def attend(seq):
        rows = block_of(seq, slots)
        stack = GROUP * slots
        row_id = lax.broadcasted_iota(jnp.int32, (stack, slots), 0) % slots
        col_id = lax.broadcasted_iota(jnp.int32, (stack, slots), 1)
        allowed = (col_id <= row_id) & (col_id < lax.div(lengths_ref[0, seq], 8))
        for g in range(H // GROUP):
            lanes = slice(g * GROUP * head, (g + 1) * GROUP * head)
            scores = dot_nt(stacked(queries[rows, lanes], head), keys[rows, lanes])
            scores = jnp.where(allowed, scores, -1e30)
            exped = jnp.exp(scores - jnp.max(scores, axis=-1, keepdims=True))
            chances = (exped / jnp.sum(exped, axis=-1, keepdims=True)).astype(bf16)
            probs[seq, g] = chances
            mixed = dot_nn(chances, values[rows, lanes])
            lefts[1, rows, lanes] = unstacked(mixed, head).astype(bf16)
        probs_copy(seq).start()

    repeat(seqs, attend)
    copies.send(lefts.at[1], lefts_out.at[1])
    weights[3].wait()
    attn[...] = dot_nn(lefts[1], out_w[...])
    copies.send(attn, attn_out)

    def after_attention(seq):
        rows = block_of(seq, slots)
        after = chosen[rows].astype(f32) + attn[rows]
        feed[0, rows] = (after * inv_rms(after) * gain_two).astype(bf16)

    repeat(seqs, after_attention)
    copies.send(feed.at[0], feed_out.at[0])
    copies.finish()


def front(lengths, index, tokens, cotangent, vectors, wq, wk, wv, wo):
    seqs, slots = index.shape
    places, width = tokens.shape[0] // seqs, tokens.shape[1]
    rows = seqs * slots
    low = ((rows, width), bf16)
    outs = [
        low, ((2, rows, width), bf16), low, low, low,
        ((seqs, H // GROUP, GROUP * slots, slots), bf16), ((rows, width), f32),
        ((2, rows, width), bf16), low, ((rows, 128), f32),
    ]
    small = [index[:, None, :], *vectors]
    return call(
        front_kernel,
        [*small, tokens, cotangent, wq, wk, wv, wo],
        (),
        [lengths],
        grid=(1,),
        in_specs=[whole(array) for array in small] + [HBM] * 6,
        out_specs=[HBM] * len(outs),
        scratch_shapes=[pltpu.VMEM((seqs, places, width), bf16)] * 2
        + [pltpu.VMEM((width, width), bf16)] * 4
        + [pltpu.VMEM(*out) for out in outs]
        + [pltpu.SemaphoreType.DMA((2 * seqs + 4 + 11 + seqs,))],
        out_shape=[jax.ShapeDtypeStruct(*out) for out in outs],
        compiler_params=params(58),
        name="front",
        cost_estimate=cost(18),
    )


def gelu_both(z):
    cdf = 0.5 + 0.5 * lax.erf(z * 0.7071067811865476)
    return z * cdf, cdf + z * (jnp.exp(-0.5 * z * z) * 0.3989422804014327)


def link_bits(nodes):
    bits = nodes.bit_length() - 1
    half = (bits - 2) // 2
    return list(range(half)), list(range(half, bits - 2)), [bits - 2], [bits - 1]


def link_order(nodes, names):
    x, y, near, far = link_bits(nodes)
    return sum([{"x": x, "y": y, "n": near, "f": far}[name] for name in names], [])


def spot_of(rel, order):
    return sum(((rel >> bit) & 1) << (len(order) - 1 - i) for i, bit in enumerate(order))


def own_blocks(me_ref, source, size, nodes):
    core, node = me_ref[0], me_ref[1]
    for rel in range(nodes):
        owner = lax.bitwise_xor(node, rel) * 2
        starts = [pl.multiple_of((owner + side) * size, size) for side in (core, 1 - core)]
        yield rel, *[source[pl.ds(start, size), :].astype(bf16) for start in starts]


def held_type(size):
    return bf16 if size % 16 == 0 else f32


def feed_kernel(me_ref, own_ref, other_ref, *refs, nodes, pieces, orders):
    ups, downs, refs = refs[:pieces], refs[pieces : 2 * pieces], refs[2 * pieces :]
    (
        sums_ref, sent_ref, down_gone, down_kept, up_gone, up_kept,
        rows_ref, grads_ref, turned_ref, down_terms, up_terms, grad_sum, out_sum,
    ) = refs
    step, steps = pl.program_id(0), pl.num_programs(0)
    node = me_ref[1]
    flat = nodes // 4
    count = own_ref.shape[1]

    @pl.when(step == 0)
    def _():
        rows_ref[:count] = own_ref[0]
        rows_ref[count:] = other_ref[0]
        grads_ref[:count] = own_ref[1]
        grads_ref[count:] = other_ref[1]
        turned_ref[...] = grads_ref[...].T
        out_sum[...] = jnp.zeros_like(out_sum)
        grad_sum[...] = jnp.zeros_like(grad_sum)

    w_up = jnp.concatenate([ref[...] for ref in ups], axis=1)
    w_down = jnp.concatenate([ref[...] for ref in downs], axis=0)
    hidden = dot_nn(rows_ref[...], w_up)
    act, slope = gelu_both(hidden)
    act = act.astype(bf16)
    pre = (dot_nt(grads_ref[...], w_down) * slope).astype(bf16)

    down_terms[...] = dot_nn(turned_ref[...], act).astype(down_terms.dtype)
    size = down_terms.shape[0] // nodes
    for rel in range(nodes):
        spot = spot_of(rel, orders[0])
        start = pl.multiple_of(lax.bitwise_xor(node, rel) * size, size)
        values = down_terms[pl.ds(start, size), :].astype(bf16)
        (down_kept, down_gone)[spot // (nodes // 2)][spot % (nodes // 2)] = values

    up_terms[...] = dot_tn(pre, rows_ref[...]).astype(up_terms.dtype)
    size = up_kept.shape[2]
    for rel in range(flat):
        spot = spot_of(rel, orders[1][:-2])
        start = pl.multiple_of(lax.bitwise_xor(lax.rem(node, flat), rel) * size, size)
        values = up_terms[pl.ds(start, size), :].astype(bf16)
        (up_kept, up_gone)[spot // (flat // 2)][spot % (flat // 2), 0] = values

    out_sum[...] += dot_nn(act, w_down)
    grad_sum[...] += dot_nt(pre, w_up)

    @pl.when(step == steps - 1)
    def _():
        for i, total in enumerate((grad_sum, out_sum)):
            sums_ref[i] = total[:count].astype(bf16)
            sent_ref[i] = total[count:].astype(bf16)


def feed(me, own, other, w_up, w_down, nodes, orders, steps=4, waits=()):
    _, rows, width = own.shape
    hidden = w_up.shape[1]
    flat = nodes // 4
    size = hidden // (2 * nodes)
    block = hidden // 2 // steps
    if size % 128:
        w_up = lax.dynamic_index_in_dim(w_up.reshape(width, nodes, 2, size), me[0], 2, False)
        w_down = lax.dynamic_index_in_dim(w_down.reshape(nodes, 2, size, width), me[0], 1, False)
        w_up, w_down = w_up.reshape(width, -1), w_down.reshape(-1, width)
        pieces = 1
        place = lambda piece, i, me: i
    else:
        pieces = block // size
        place = lambda piece, i, me: (i * pieces + piece) * 2 + me[0]
    columns = block // pieces
    up_specs = [
        pl.BlockSpec((width, columns), lambda i, me, p=p: (0, place(p, i, me)))
        for p in range(pieces)
    ]
    down_specs = [
        pl.BlockSpec((columns, width), lambda i, me, p=p: (place(p, i, me), 0))
        for p in range(pieces)
    ]
    chunk = width // nodes
    down_spec = pl.BlockSpec((nodes // 2, chunk, block), lambda i, me: (0, 0, i))
    near_first = orders[1][-2] < orders[1][-1]

    def up_place(i, me):
        rel = lax.bitwise_xor(i, lax.div(me[1], flat))
        return (0, lax.rem(rel, 2) * 2 + lax.div(rel, 2) if near_first else rel, 0, 0)

    up_spec = pl.BlockSpec((flat // 2, 1, size, width), up_place)
    pair = jax.ShapeDtypeStruct((2, rows, width), bf16)
    return call(
        functools.partial(feed_kernel, nodes=nodes, pieces=pieces, orders=orders),
        [own, other] + [w_up] * pieces + [w_down] * pieces,
        waits,
        [me],
        grid=(steps,),
        in_specs=[whole(own), whole(other)] + up_specs + down_specs,
        out_specs=[pl.BlockSpec((2, rows, width), lambda i, me: (0, 0, 0))] * 2
        + [down_spec, down_spec, up_spec, up_spec],
        scratch_shapes=[
            pltpu.VMEM((2 * rows, width), bf16),
            pltpu.VMEM((2 * rows, width), bf16),
            pltpu.VMEM((width, 2 * rows), bf16),
            pltpu.VMEM((width, block), held_type(chunk)),
            pltpu.VMEM((block, width), held_type(size)),
            pltpu.VMEM((2 * rows, width), f32),
            pltpu.VMEM((2 * rows, width), f32),
        ],
        out_shape=[pair] * 2
        + [jax.ShapeDtypeStruct((nodes // 2, chunk, hidden // 2), bf16)] * 2
        + [jax.ShapeDtypeStruct((flat // 2, 4, size, width), bf16)] * 2,
        compiler_params=params(62),
        name="feed",
        cost_estimate=cost(34),
    )


def back_kernel(
    me_ref, gain_ref, chosen_hbm, attn_hbm, score_hbm, pulled_hbm, own_hbm, other_hbm, queries_hbm,
    keys_hbm, values_hbm, probs_hbm, lefts_hbm, out_hbm,
    grads_out, after_out, gain_out, send_gone_out, send_stay_out, keep_gone_out, keep_stay_out,
    send_b_out, keep_b_out,
    chosen, attn, score, pulled, own, other, queries, keys, values, probs, lefts, out_w,
    grads, after_grad, send_gone, send_stay, keep_gone, keep_stay, send_b, keep_b,
    mix_grad, terms, sems,
    *, nodes, orders,
):
    copies = Copies(sems)
    fetched = {}
    for name, source, target in (
        ("rows", chosen_hbm, chosen), ("rows", attn_hbm, attn), ("rows", own_hbm.at[0], own),
        ("rows", other_hbm.at[0], other), ("rows", score_hbm, score), ("rows", pulled_hbm, pulled),
        ("out", out_hbm, out_w), ("heads", queries_hbm, queries), ("heads", keys_hbm, keys),
        ("heads", values_hbm, values), ("heads", probs_hbm, probs), ("lefts", lefts_hbm, lefts),
    ):
        fetched.setdefault(name, []).append(copies.start(source, target))

    def arrive(name):
        for copy in fetched[name]:
            copy.wait()

    seqs, groups, stack, slots = probs.shape
    width = chosen.shape[1]
    head = width // H
    gain = flat_row(gain_ref)
    gain_out[...] = jnp.zeros_like(gain_out)
    arrive("rows")

    def norm_grad(seq):
        rows = block_of(seq, slots)
        after = chosen[rows].astype(f32) + attn[rows]
        inv = inv_rms(after)
        normed = after * inv
        arrived = add_low(own[rows], other[rows]).astype(f32)
        gain_out[...] += fold(arrived * normed)
        weighted = arrived * gain
        back = inv * (weighted - normed * jnp.mean(weighted * normed, axis=-1, keepdims=True))
        after_grad[rows] = back
        delta = score[rows, :1] * pulled[rows].astype(f32)
        grads[3, rows] = (delta + back).astype(bf16)

    repeat(seqs, norm_grad)
    copies.send(after_grad, after_out)
    arrive("out")
    mix_grad[...] = dot_nt(grads[3], out_w[...]).astype(bf16)
    arrive("heads")

    def attention_grad(seq):
        rows = block_of(seq, slots)
        for g in range(groups):
            lanes = slice(g * GROUP * head, (g + 1) * GROUP * head)
            chances = probs[seq, g]
            wide = chances.astype(f32)
            stacked_queries = stacked(queries[rows, lanes], head)
            stacked_grads = stacked(mix_grad[rows, lanes], head)
            prob_grad = dot_nt(stacked_grads, values[rows, lanes])
            total = jnp.sum(prob_grad * wide, axis=-1, keepdims=True)
            score_grad = (wide * (prob_grad - total)).astype(bf16)
            grads[2, rows, lanes] = dot_tn(chances, stacked_grads).astype(bf16)
            grads[1, rows, lanes] = dot_tn(score_grad, stacked_queries).astype(bf16)
            grads[0, rows, lanes] = unstacked(dot_nn(score_grad, keys[rows, lanes]), head).astype(bf16)

    repeat(seqs, attention_grad)
    copies.send(grads.at[pl.ds(0, 3)], grads_out)
    arrive("lefts")
    half, cut = nodes // 2, send_gone.shape[3]
    outs = [
        copies.send_group(4, lambda i, held=held, out=out: (held.at[:, i], out.at[:, i]))
        for held, out in (
            (send_gone, send_gone_out), (keep_gone, keep_gone_out), (send_stay, send_stay_out),
            (keep_stay, keep_stay_out), (send_b, send_b_out), (keep_b, keep_b_out),
        )
    ]

    def weight_grad(which):
        product = dot_tn(grads[which], lefts[lax.div(which, 3)])
        terms[...] = (product * jnp.where(which == 0, 0.125, 1.0)).astype(terms.dtype)
        for rel, kept, sent in own_blocks(me_ref, terms, send_b.shape[2], nodes):
            spot = spot_of(rel, orders[0])
            (keep_stay, keep_gone)[spot // half][spot % half, which] = kept[:, :cut]
            (send_stay, send_gone)[spot // half][spot % half, which] = sent[:, :cut]
            spot = spot_of(rel, orders[1])
            keep_b[spot, which] = kept[:, cut:]
            send_b[spot, which] = sent[:, cut:]
        for out in outs:
            out(which).start()

    repeat(4, weight_grad)
    copies.finish()


def back(
    me, chosen, attn, score, pulled, own, other, gain, queries, keys, values, probs, lefts, w_out, nodes,
    orders, cut,
):
    rows, width = chosen.shape
    seqs, _, _, slots = probs.shape
    size = width // (2 * nodes)
    layout = [(nodes // 2, cut)] * 4 + [(nodes, width - cut)] * 2
    shapes = [((count, 4, size, columns), bf16) for count, columns in layout]
    outs = [((3, rows, width), bf16), ((rows, width), f32)]
    fetched = [chosen, attn, score, pulled, own, other, queries, keys, values, probs, lefts, w_out]
    held = [pltpu.VMEM(array.shape, array.dtype) for array in fetched]
    held[4] = held[5] = pltpu.VMEM((rows, width), bf16)
    return call(
        functools.partial(back_kernel, nodes=nodes, orders=orders),
        [gain, *fetched],
        (),
        [me],
        grid=(1,),
        in_specs=[whole(gain)] + [HBM] * len(fetched),
        out_specs=[HBM, HBM, pl.BlockSpec((8, width), lambda *_: (0, 0))] + [HBM] * 6,
        scratch_shapes=held
        + [pltpu.VMEM(*out) for out in [((4, rows, width), bf16), outs[1]] + shapes]
        + [pltpu.VMEM((rows, width), bf16)]
        + [pltpu.VMEM((width, width), held_type(size))]
        + [pltpu.SemaphoreType.DMA((len(fetched) + 2 + 24,))],
        out_shape=[jax.ShapeDtypeStruct(*out) for out in outs]
        + [jax.ShapeDtypeStruct((8, width), f32)]
        + [jax.ShapeDtypeStruct(*shape) for shape in shapes],
        compiler_params=params(62),
        name="back",
        cost_estimate=cost(20),
    )


def last_kernel(
    gain_ref, router_ref, chosen_hbm, attn_hbm, own_hbm, other_hbm, score_hbm, pulled_hbm, after_hbm,
    grads_hbm, query_hbm, key_hbm, value_hbm,
    chosen_grad_out, gain_out, router_out,
    chosen, attn, own, other, score, pulled, after_grad, grads, weights, first_grad, chosen_grad, sems,
):
    copies = Copies(sems)
    pairs = [
        (copies.start(grads_hbm.at[i], grads.at[i]), copies.start(weight, weights.at[i]))
        for i, weight in enumerate((query_hbm, key_hbm, value_hbm))
    ]
    others = [
        copies.start(*pair)
        for pair in (
            (chosen_hbm, chosen), (attn_hbm, attn), (own_hbm.at[1], own), (other_hbm.at[1], other),
            (score_hbm, score), (pulled_hbm, pulled), (after_hbm, after_grad),
        )
    ]
    gain, router = flat_row(gain_ref), flat_row(router_ref)
    gain_out[...] = jnp.zeros_like(gain_out)
    router_out[...] = jnp.zeros_like(router_out)
    for i, pair in enumerate(pairs):
        for copy in pair:
            copy.wait()
        product = dot_nt(grads[i], weights[i])
        if i == 0:
            first_grad[...] = product * 0.125
        else:
            first_grad[...] += product
    for copy in others:
        copy.wait()
    turns = 4
    block = chosen.shape[0] // turns
    out = copies.send_group(
        turns,
        lambda i: (chosen_grad.at[block_of(i, block)], chosen_grad_out.at[block_of(i, block)]),
    )

    def rest(i):
        part = block_of(i, block)
        wide = chosen[part].astype(f32)
        chance = score[part, :1]
        branch = attn[part] + add_low(own[part], other[part]).astype(f32)
        pull = jnp.sum(pulled[part].astype(f32) * branch, axis=-1, keepdims=True)
        logit_grad = pull * chance * (1.0 - chance)
        arrived = first_grad[part]
        inv = inv_rms(wide)
        normed = wide * inv
        weighted = arrived * gain
        chosen_grad[part] = (
            inv * (weighted - normed * jnp.mean(weighted * normed, axis=-1, keepdims=True))
            + after_grad[part]
            + logit_grad * router
        )
        out(i).start()
        gain_out[...] += fold(arrived * normed)
        router_out[...] += fold(logit_grad * wide)

    repeat(turns, rest)
    copies.finish()


def last(
    chosen, attn, own, other, score, pulled, after_grad, grads, gain, router, wq, wk, wv, waits=()
):
    rows, width = chosen.shape
    fetched = [chosen, attn, own, other, score, pulled, after_grad, grads, wq, wk, wv]
    held = [pltpu.VMEM(array.shape, array.dtype) for array in fetched[:-3]]
    held[2] = held[3] = pltpu.VMEM((rows, width), bf16)
    held.append(pltpu.VMEM((3, width, width), bf16))
    sums = pl.BlockSpec((8, width), lambda *_: (0, 0))
    return call(
        last_kernel,
        [gain, router, *fetched],
        waits,
        grid=(1,),
        in_specs=[whole(gain), whole(router)] + [HBM] * len(fetched),
        out_specs=[HBM, sums, sums],
        scratch_shapes=held
        + [pltpu.VMEM((rows, width), f32)] * 2
        + [pltpu.SemaphoreType.DMA((17,))],
        out_shape=[jax.ShapeDtypeStruct((rows, width), f32)]
        + [jax.ShapeDtypeStruct((8, width), f32)] * 2,
        compiler_params=params(58),
        name="last",
        cost_estimate=cost(9),
    )


def spread_kernel(lengths_ref, index_ref, base_hbm, *refs, deltas, pieces):
    deltas_hbm, out_hbm, base, out = refs[:deltas], refs[deltas], refs[deltas + 1], refs[deltas + 2]
    held, sems = refs[deltas + 3 : -1], refs[-1]
    copies = Copies(sems)
    seqs, _, slots = index_ref.shape
    count = base.shape[1]

    def delta_copy(source, target):
        top = source.shape[0] - 1
        place = lambda row: source.at[top, row] if len(source.shape) == 3 else source.at[row]
        return copies.group(
            seqs, lambda seq: (place(block_of(seq, slots)), target.at[block_of(seq, slots)])
        )

    delta_copies = [delta_copy(*pair) for pair in zip(deltas_hbm, held)]
    base_copy = copies.group(
        seqs * pieces, lambda at: (base_hbm.at[block_of(at, count)], base.at[at])
    )
    for seq in range(seqs):
        for copy in delta_copies:
            copy(seq).start()
        for piece in range(pieces):
            base_copy(seq * pieces + piece).start()
    out_copy = copies.send_group(
        seqs * pieces, lambda at: (out.at[at], out_hbm.at[block_of(at, count)])
    )

    def one(seq):
        rows = block_of(seq, slots)
        for copy in delta_copies:
            copy(seq).wait()
        if deltas == 1:
            delta = held[0][rows]
        else:
            score, attn, own, other = held
            delta = score[rows, :1] * (attn[rows] + add_low(own[rows], other[rows]).astype(f32))
        high = delta.astype(bf16)
        low = (delta - high.astype(f32)).astype(bf16)
        both = jnp.concatenate([high, low], axis=0)
        slot_id = lax.broadcasted_iota(jnp.int32, (count, slots), 1)
        live = slot_id < lax.div(lengths_ref[0, seq], 8)
        for piece in range(pieces):
            place = piece * count + lax.broadcasted_iota(jnp.int32, (count, slots), 0)
            pick = ((index_ref[seq] == place) & live).astype(bf16)
            at = seq * pieces + piece
            base_copy(at).wait()
            added = dot_nn(jnp.concatenate([pick, pick], axis=1), both)
            out[at] = (base[at].astype(f32) + added).astype(out.dtype)
            out_copy(at).start()

    repeat(seqs, one)
    copies.finish()


def spread(lengths, index, base, deltas, dtype, waits=(), pieces=2):
    seqs, slots = index.shape
    rows, width = base.shape
    steps = seqs * pieces
    index = index[:, None, :]
    held = [pltpu.VMEM(delta.shape[-2:], delta.dtype) for delta in deltas]
    return call(
        functools.partial(spread_kernel, deltas=len(deltas), pieces=pieces),
        [index, base, *deltas],
        waits,
        [lengths],
        grid=(1,),
        in_specs=[whole(index)] + [HBM] * (1 + len(deltas)),
        out_specs=HBM,
        scratch_shapes=[
            pltpu.VMEM((steps, rows // steps, width), bf16),
            pltpu.VMEM((steps, rows // steps, width), dtype),
            *held,
            pltpu.SemaphoreType.DMA((2 * steps + len(deltas) * seqs,)),
        ],
        out_shape=jax.ShapeDtypeStruct((rows, width), dtype),
        compiler_params=params(58),
        name="spread",
        cost_estimate=cost(8),
    )


def add_low(left, right):
    return (left.astype(f32) + right.astype(f32)).astype(bf16)


def swap_nodes(values, bit, nodes):
    return lax.ppermute(values, "seq", [(i, i ^ (1 << bit)) for i in range(nodes)])


def swap_cores(values):
    return lax.ppermute(values, "dp", [(0, 1), (1, 0)])


class Part:
    def __init__(self, order, nodes):
        self.order, self.nodes = order, nodes

    @classmethod
    def halved(cls, gone, kept, order, nodes):
        part = cls(order, nodes)
        part.gone, part.kept = gone, kept
        part.swap()
        return part

    @classmethod
    def of_cores(cls, send, keep, order, nodes):
        part = cls(order, nodes)
        part.kept, part.got = keep, swap_cores(send)
        return part

    @classmethod
    def of_split_cores(cls, send_gone, send_stay, keep_gone, keep_stay, order, nodes):
        part = cls(order, nodes)
        part.halves = (keep_gone, swap_cores(send_gone)), (keep_stay, swap_cores(send_stay))
        return part

    halves = None

    def swap(self):
        self.got = swap_nodes(self.gone, self.order[0], self.nodes)
        self.order = self.order[1:]

    def halve(self, after=()):
        if self.halves:
            (keep_gone, got_gone), (keep_stay, got_stay), *_ = lax.optimization_barrier(
                (*self.halves, *after)
            )
            self.gone, self.kept = add_low(keep_gone, got_gone), add_low(keep_stay, got_stay)
            self.halves = None
            return
        if after:
            self.kept, self.got, *_ = lax.optimization_barrier((self.kept, self.got, *after))
        if self.kept.shape[0] == 1:
            self.kept, self.got = self.kept[0], self.got[0]
        count = self.kept.shape[0] // 2
        halves = [add_low(self.kept[c], self.got[c]) for c in (slice(count, None), slice(count))]
        self.gone, self.kept = [half[0] for half in halves] if count == 1 else halves

    def step(self, after=()):
        self.halve(after)
        self.swap()
        return self.gone


class Chain:
    def __init__(self, parts):
        self.parts = parts

    def step(self, count=1, after=()):
        sent = []
        for _ in range(count):
            sent = []
            for part in self.parts:
                sent.append(part.step([*after, *sent]))
        return sent

    def final(self, after=()):
        for part in self.parts:
            part.halve(after)
        gone = jnp.concatenate([part.gone for part in self.parts], axis=-1)
        self.got = swap_nodes(gone, self.parts[0].order[0], self.parts[0].nodes)
        return [gone]

    def sum(self):
        kept = jnp.concatenate([part.kept for part in self.parts], axis=-1)
        return kept.astype(f32) + self.got.astype(f32)


def both_cores(core, rows, nodes):
    count = rows.shape[0] // 2
    mine, sent = [
        lax.dynamic_slice_in_dim(rows, side * count, count) for side in (core, 1 - core)
    ]
    got = swap_cores(sent)
    shape = (count, nodes, 1, rows.shape[1] // nodes)
    sides = [jnp.where(core == side, mine, got).reshape(shape) for side in (0, 1)]
    return jnp.concatenate(sides, axis=2).reshape(count, -1)


def on_device(
    tokens,
    lengths,
    routed_index,
    out_grad,
    gain_attn,
    w_router,
    w_query,
    w_key,
    w_value,
    w_out,
    gain_mlp,
    w_up,
    w_down,
):
    nodes = lax.axis_size("seq")
    width = tokens.shape[2]
    me = jnp.stack([lax.axis_index("dp"), lax.axis_index("seq")]).astype(jnp.int32)
    index = routed_index[0]
    inputs, cotangent = tokens[0], out_grad[0]
    vectors = [vector.reshape(-1, 128) for vector in (gain_attn, w_router, gain_mlp)]
    (
        chosen, lefts, queries, keys, values, probs, attn_out, feed_own, pulled, score,
    ) = front(
        lengths, index, inputs, cotangent, vectors, w_query, w_key, w_value, w_out
    )
    feed_other = swap_cores(feed_own)
    order = lambda names: link_order(nodes, names)
    span = len(order("x"))
    down_order, up_order = order("nxfy"), order("xynf")
    square_orders = [order("nxyf"), order("yxnf")]
    own_sums, other_sums, *terms = feed(
        me, feed_own, feed_other, w_up, w_down, nodes, [down_order, up_order]
    )
    got_sums = swap_cores(other_sums)
    down = Chain([Part.halved(*terms[:2], down_order, nodes)])
    up = Chain([Part.halved(*terms[2:], up_order, nodes)])
    grads, after_grad, gain_mlp_sum, *square_terms = back(
        me, chosen, attn_out, score, pulled, own_sums, got_sums, vectors[2], queries, keys, values, probs,
        lefts, w_out, nodes, square_orders, width // 2,
    )
    square = Chain(
        [
            Part.of_split_cores(*square_terms[:4], square_orders[0], nodes),
            Part.of_cores(*square_terms[4:], square_orders[1], nodes),
        ]
    )
    mixed_out = spread(
        lengths, index, inputs, [score, attn_out, own_sums, got_sums], bf16, waits=square_terms[:1]
    )
    chosen_grad, gain_attn_sum, router_sum = last(
        chosen, attn_out, own_sums, got_sums, score, pulled, after_grad, grads,
        vectors[0], vectors[1], w_query, w_key, w_value, waits=[mixed_out],
    )
    sums = jnp.sum(jnp.stack([gain_attn_sum, router_sum, gain_mlp_sum]), axis=1)
    sums = sums.reshape(3, 2 * nodes, -1).transpose(1, 0, 2)
    gone = down.step(span, after=[chosen_grad])
    gone += up.step(span, after=gone)
    gone += square.step(after=gone)
    token_grad = spread(lengths, index, cotangent, [chosen_grad], f32, waits=gone)
    gone = down.step(span, after=[token_grad])
    gone = up.step(span, after=gone)
    gone = square.step(span, after=gone)
    gone = down.final(after=gone)
    gone = up.final(after=gone)
    gone = square.step(span, after=gone)
    down_sum, _ = lax.optimization_barrier((both_cores(me[0], down.sum(), nodes), gone[0]))
    gone = square.final(after=[up.sum()])
    sums, *_ = lax.optimization_barrier((sums, *gone))
    sums = jnp.sum(lax.all_to_all(sums, ("seq", "dp"), 0, 0, tiled=True), axis=0)
    square_sum = square.sum()
    return (
        mixed_out[None],
        token_grad[None],
        sums[0],
        sums[1],
        *[square_sum[which].T for which in range(4)],
        sums[2],
        up.sum().T,
        down_sum.T,
    )


def solution(mesh):
    in_specs = (
        P("dp", "seq", None),
        P("dp", "seq"),
        P("dp", "seq", None),
        P("dp", "seq", None),
        P(),
        P(),
        P(),
        P(),
        P(),
        P(),
        P(),
        P(),
        P(),
    )
    out_specs = (
        P("dp", "seq", None),
        P("dp", "seq", None),
        P(("seq", "dp")),
        P(("seq", "dp")),
        P(None, ("seq", "dp")),
        P(None, ("seq", "dp")),
        P(None, ("seq", "dp")),
        P(None, ("seq", "dp")),
        P(("seq", "dp")),
        P(None, ("seq", "dp")),
        P(None, ("seq", "dp")),
    )
    return jax.shard_map(
        on_device, mesh=mesh, in_specs=in_specs, out_specs=out_specs, check_vma=False
    )
```

```python
import functools

import jax
import jax.experimental.pallas as pl
import jax.experimental.pallas.tpu as pltpu
import jax.numpy as jnp
from jax import lax
from jax.sharding import PartitionSpec as P

H = 16
norm_eps = 1e-05
f32 = jnp.float32
bf16 = jnp.bfloat16


def params(mebibytes):
    return pltpu.CompilerParams(
        dimension_semantics=("arbitrary",), vmem_limit_bytes=mebibytes * 1024 * 1024
    )


def cost(micros):
    return pl.CostEstimate(
        flops=int(micros * 1e8), bytes_accessed=int(micros * 3.5e5), transcendentals=0
    )


def call(kernel, arrays, waits=(), scalars=(), **rest):
    first = len(scalars) + len(arrays)

    def body(*refs):
        kernel(*refs[:first], *refs[first + len(waits) :])

    grid = pltpu.PrefetchScalarGridSpec(
        num_scalar_prefetch=len(scalars),
        grid=rest.pop("grid"),
        in_specs=list(rest.pop("in_specs")) + [pl.BlockSpec(memory_space=pl.ANY)] * len(waits),
        out_specs=rest.pop("out_specs"),
        scratch_shapes=rest.pop("scratch_shapes", ()),
    )
    return pl.pallas_call(body, grid_spec=grid, **rest)(*scalars, *arrays, *waits)


def whole(array):
    rank = len(array.shape)
    return pl.BlockSpec(array.shape, lambda *_: (0,) * rank, pipeline_mode=pl.Buffered(1))


def dot_nn(left, right):
    return lax.dot_general(left, right, (((1,), (0,)), ((), ())), preferred_element_type=f32)


def dot_nt(left, right):
    return lax.dot_general(left, right, (((1,), (1,)), ((), ())), preferred_element_type=f32)


def dot_tn(left, right):
    return lax.dot_general(left, right, (((0,), (0,)), ((), ())), preferred_element_type=f32)


def inv_rms(values):
    return lax.rsqrt(jnp.mean(values * values, axis=-1, keepdims=True) + norm_eps)


GROUP = 4


def flat_row(ref):
    values = ref[...].astype(f32)
    return jnp.concatenate([values[i : i + 1] for i in range(values.shape[0])], axis=1)


def fold(values):
    rows, width = values.shape
    return jnp.sum(values.reshape(rows // 8, 8, width), axis=0)


class Copies:
    def __init__(self, sems):
        self.sems, self.count, self.sent = sems, 0, []

    def one(self, source, target):
        self.count += 1
        return pltpu.make_async_copy(source, target, self.sems.at[self.count - 1])

    def group(self, turns, pair):
        first = self.count
        self.count += turns

        def at(turn):
            source, target = pair(turn)
            return pltpu.make_async_copy(source, target, self.sems.at[first + turn])

        return at

    def start(self, source, target):
        copy = self.one(source, target)
        copy.start()
        return copy

    def send(self, source, target):
        self.sent.append(self.start(source, target))

    def send_group(self, turns, pair):
        at = self.group(turns, pair)
        self.sent += [at(turn) for turn in range(turns)]
        return at

    def finish(self):
        for copy in self.sent:
            copy.wait()


def repeat(turns, body, unroll=1):
    lax.fori_loop(0, turns, lambda turn, carry: body(turn), None, unroll=unroll)


def block_of(turn, size):
    return pl.ds(pl.multiple_of(turn * size, size), size)


HBM = pl.BlockSpec(memory_space=pl.ANY)


def stacked(rows, head):
    lane_head = lax.broadcasted_iota(jnp.int32, rows.shape, 1) // head
    zero = jnp.zeros_like(rows)
    return jnp.concatenate([jnp.where(lane_head == h, rows, zero) for h in range(GROUP)], axis=0)


def unstacked(rows, head):
    slots = rows.shape[0] // GROUP
    lane_head = lax.broadcasted_iota(jnp.int32, (slots, rows.shape[1]), 1) // head
    out = rows[:slots]
    for h in range(1, GROUP):
        out = jnp.where(lane_head == h, rows[h * slots : (h + 1) * slots], out)
    return out


def front_kernel(
    lengths_ref, index_ref, gain_one_ref, router_ref, gain_two_ref,
    tokens_hbm, cotangent_hbm, query_hbm, key_hbm, value_hbm, out_hbm,
    chosen_out, lefts_out, queries_out, keys_out, values_out, probs_out, attn_out, feed_out, pulled_out,
    score_out,
    tokens, cotangent, query_w, key_w, value_w, out_w,
    chosen, lefts, queries, keys, values, probs, attn, feed, pulled, score, sems,
):
    copies = Copies(sems)
    seqs, _, slots = index_ref.shape
    places, width = tokens.shape[1], tokens.shape[2]
    head = width // H
    token_copy = copies.group(
        seqs, lambda seq: (tokens_hbm.at[block_of(seq, places)], tokens.at[seq])
    )
    cotangent_copy = copies.group(
        seqs, lambda seq: (cotangent_hbm.at[block_of(seq, places)], cotangent.at[seq])
    )
    for seq in range(seqs):
        token_copy(seq).start()
        cotangent_copy(seq).start()
    weights = [
        copies.start(*pair)
        for pair in (
            (query_hbm, query_w), (key_hbm, key_w), (value_hbm, value_w), (out_hbm, out_w),
        )
    ]
    gain_one, router, gain_two = [flat_row(r) for r in (gain_one_ref, router_ref, gain_two_ref)]

    def gather(seq):
        rows = block_of(seq, slots)
        slot_id = lax.broadcasted_iota(jnp.int32, (slots, places), 0)
        place_id = lax.broadcasted_iota(jnp.int32, (slots, places), 1)
        square = (slots, slots)
        diagonal = lax.broadcasted_iota(jnp.int32, square, 0) == lax.broadcasted_iota(
            jnp.int32, square, 1
        )
        routed = lax.div(lengths_ref[0, seq], 8)
        index = jnp.sum(jnp.where(diagonal, index_ref[seq], 0), axis=1, keepdims=True)
        pick = ((index == place_id) & (slot_id < routed)).astype(bf16)
        token_copy(seq).wait()
        wide = dot_nn(pick, tokens[seq])
        chosen[rows] = wide.astype(bf16)
        logit = jnp.sum(wide * router, axis=-1, keepdims=True)
        chance = 1.0 / (1.0 + jnp.exp(-logit))
        score[rows] = jnp.broadcast_to(chance, (slots, score.shape[1]))
        lefts[0, rows] = (wide * inv_rms(wide) * gain_one).astype(bf16)
        cotangent_copy(seq).wait()
        pull = dot_nn(pick, cotangent[seq])
        pulled[rows] = pull.astype(bf16)
        feed[1, rows] = (chance * pull).astype(bf16)

    repeat(seqs, gather, 2)
    copies.send(chosen, chosen_out)
    copies.send(pulled, pulled_out)
    copies.send(score, score_out)
    copies.send(feed.at[1], feed_out.at[1])
    copies.send(lefts.at[0], lefts_out.at[0])
    first = lefts[0]
    weights[0].wait()
    queries[...] = (dot_nn(first, query_w[...]) * 0.125).astype(bf16)
    copies.send(queries, queries_out)
    weights[1].wait()
    keys[...] = dot_nn(first, key_w[...]).astype(bf16)
    copies.send(keys, keys_out)
    weights[2].wait()
    values[...] = dot_nn(first, value_w[...]).astype(bf16)
    copies.send(values, values_out)
    probs_copy = copies.send_group(seqs, lambda seq: (probs.at[seq], probs_out.at[seq]))

    def attend(seq):
        rows = block_of(seq, slots)
        stack = GROUP * slots
        row_id = lax.broadcasted_iota(jnp.int32, (stack, slots), 0) % slots
        col_id = lax.broadcasted_iota(jnp.int32, (stack, slots), 1)
        allowed = (col_id <= row_id) & (col_id < lax.div(lengths_ref[0, seq], 8))
        for g in range(H // GROUP):
            lanes = slice(g * GROUP * head, (g + 1) * GROUP * head)
            scores = dot_nt(stacked(queries[rows, lanes], head), keys[rows, lanes])
            scores = jnp.where(allowed, scores, -1e30)
            exped = jnp.exp(scores - jnp.max(scores, axis=-1, keepdims=True))
            chances = (exped / jnp.sum(exped, axis=-1, keepdims=True)).astype(bf16)
            probs[seq, g] = chances
            mixed = dot_nn(chances, values[rows, lanes])
            lefts[1, rows, lanes] = unstacked(mixed, head).astype(bf16)
        probs_copy(seq).start()

    repeat(seqs, attend, 2)
    copies.send(lefts.at[1], lefts_out.at[1])
    weights[3].wait()
    attn[...] = dot_nn(lefts[1], out_w[...])
    copies.send(attn, attn_out)

    def after_attention(seq):
        rows = block_of(seq, slots)
        after = chosen[rows].astype(f32) + attn[rows]
        feed[0, rows] = (after * inv_rms(after) * gain_two).astype(bf16)

    repeat(seqs, after_attention)
    copies.send(feed.at[0], feed_out.at[0])
    copies.finish()


def front(lengths, index, tokens, cotangent, vectors, wq, wk, wv, wo):
    seqs, slots = index.shape
    places, width = tokens.shape[0] // seqs, tokens.shape[1]
    rows = seqs * slots
    low = ((rows, width), bf16)
    outs = [
        low, ((2, rows, width), bf16), low, low, low,
        ((seqs, H // GROUP, GROUP * slots, slots), bf16), ((rows, width), f32),
        ((2, rows, width), bf16), low, ((rows, 128), f32),
    ]
    small = [index[:, None, :], *vectors]
    return call(
        front_kernel,
        [*small, tokens, cotangent, wq, wk, wv, wo],
        (),
        [lengths],
        grid=(1,),
        in_specs=[whole(array) for array in small] + [HBM] * 6,
        out_specs=[HBM] * len(outs),
        scratch_shapes=[pltpu.VMEM((seqs, places, width), bf16)] * 2
        + [pltpu.VMEM((width, width), bf16)] * 4
        + [pltpu.VMEM(*out) for out in outs]
        + [pltpu.SemaphoreType.DMA((2 * seqs + 4 + 11 + seqs,))],
        out_shape=[jax.ShapeDtypeStruct(*out) for out in outs],
        compiler_params=params(58),
        name="front",
        cost_estimate=cost(18),
    )


def gelu_both(z):
    cdf = 0.5 + 0.5 * lax.erf(z * 0.7071067811865476)
    return z * cdf, cdf + z * (jnp.exp(-0.5 * z * z) * 0.3989422804014327)


def link_bits(nodes):
    bits = nodes.bit_length() - 1
    half = (bits - 2) // 2
    return list(range(half)), list(range(half, bits - 2)), [bits - 2], [bits - 1]


def link_order(nodes, names):
    x, y, near, far = link_bits(nodes)
    return sum([{"x": x, "y": y, "n": near, "f": far}[name] for name in names], [])


def spot_of(rel, order):
    return sum(((rel >> bit) & 1) << (len(order) - 1 - i) for i, bit in enumerate(order))


def own_blocks(me_ref, source, size, nodes):
    core, node = me_ref[0], me_ref[1]
    for rel in range(nodes):
        owner = lax.bitwise_xor(node, rel) * 2
        starts = [pl.multiple_of((owner + side) * size, size) for side in (core, 1 - core)]
        yield rel, *[source[pl.ds(start, size), :].astype(bf16) for start in starts]


def held_type(size):
    return bf16 if size % 16 == 0 else f32


def feed_kernel(me_ref, own_ref, other_ref, *refs, nodes, pieces, orders):
    ups, downs, refs = refs[:pieces], refs[pieces : 2 * pieces], refs[2 * pieces :]
    (
        sums_ref, sent_ref, down_gone, down_kept, up_gone, up_kept,
        rows_ref, grads_ref, turned_ref, down_terms, up_terms, grad_sum, out_sum,
    ) = refs
    step, steps = pl.program_id(0), pl.num_programs(0)
    node = me_ref[1]
    flat = nodes // 4
    count = own_ref.shape[1]

    @pl.when(step == 0)
    def _():
        rows_ref[:count] = own_ref[0]
        rows_ref[count:] = other_ref[0]
        grads_ref[:count] = own_ref[1]
        grads_ref[count:] = other_ref[1]
        turned_ref[...] = grads_ref[...].T
        out_sum[...] = jnp.zeros_like(out_sum)
        grad_sum[...] = jnp.zeros_like(grad_sum)

    w_up = jnp.concatenate([ref[...] for ref in ups], axis=1)
    w_down = jnp.concatenate([ref[...] for ref in downs], axis=0)
    hidden = dot_nn(rows_ref[...], w_up)
    act, slope = gelu_both(hidden)
    act = act.astype(bf16)
    pre = (dot_nt(grads_ref[...], w_down) * slope).astype(bf16)

    down_terms[...] = dot_nn(turned_ref[...], act).astype(down_terms.dtype)
    size = down_terms.shape[0] // nodes
    for rel in range(nodes):
        spot = spot_of(rel, orders[0])
        start = pl.multiple_of(lax.bitwise_xor(node, rel) * size, size)
        values = down_terms[pl.ds(start, size), :].astype(bf16)
        (down_kept, down_gone)[spot // (nodes // 2)][spot % (nodes // 2)] = values

    up_terms[...] = dot_tn(pre, rows_ref[...]).astype(up_terms.dtype)
    size = up_kept.shape[2]
    for rel in range(flat):
        spot = spot_of(rel, orders[1][:-2])
        start = pl.multiple_of(lax.bitwise_xor(lax.rem(node, flat), rel) * size, size)
        values = up_terms[pl.ds(start, size), :].astype(bf16)
        (up_kept, up_gone)[spot // (flat // 2)][spot % (flat // 2), 0] = values

    out_sum[...] += dot_nn(act, w_down)
    grad_sum[...] += dot_nt(pre, w_up)

    @pl.when(step == steps - 1)
    def _():
        for i, total in enumerate((grad_sum, out_sum)):
            sums_ref[i] = total[:count].astype(bf16)
            sent_ref[i] = total[count:].astype(bf16)


def feed(me, own, other, w_up, w_down, nodes, orders, steps=4, waits=()):
    _, rows, width = own.shape
    hidden = w_up.shape[1]
    flat = nodes // 4
    size = hidden // (2 * nodes)
    block = hidden // 2 // steps
    if size % 128:
        w_up = lax.dynamic_index_in_dim(w_up.reshape(width, nodes, 2, size), me[0], 2, False)
        w_down = lax.dynamic_index_in_dim(w_down.reshape(nodes, 2, size, width), me[0], 1, False)
        w_up, w_down = w_up.reshape(width, -1), w_down.reshape(-1, width)
        pieces = 1
        place = lambda piece, i, me: i
    else:
        pieces = block // size
        place = lambda piece, i, me: (i * pieces + piece) * 2 + me[0]
    columns = block // pieces
    up_specs = [
        pl.BlockSpec((width, columns), lambda i, me, p=p: (0, place(p, i, me)))
        for p in range(pieces)
    ]
    down_specs = [
        pl.BlockSpec((columns, width), lambda i, me, p=p: (place(p, i, me), 0))
        for p in range(pieces)
    ]
    chunk = width // nodes
    down_spec = pl.BlockSpec((nodes // 2, chunk, block), lambda i, me: (0, 0, i))
    near_first = orders[1][-2] < orders[1][-1]

    def up_place(i, me):
        rel = lax.bitwise_xor(i, lax.div(me[1], flat))
        return (0, lax.rem(rel, 2) * 2 + lax.div(rel, 2) if near_first else rel, 0, 0)

    up_spec = pl.BlockSpec((flat // 2, 1, size, width), up_place)
    pair = jax.ShapeDtypeStruct((2, rows, width), bf16)
    return call(
        functools.partial(feed_kernel, nodes=nodes, pieces=pieces, orders=orders),
        [own, other] + [w_up] * pieces + [w_down] * pieces,
        waits,
        [me],
        grid=(steps,),
        in_specs=[whole(own), whole(other)] + up_specs + down_specs,
        out_specs=[pl.BlockSpec((2, rows, width), lambda i, me: (0, 0, 0))] * 2
        + [down_spec, down_spec, up_spec, up_spec],
        scratch_shapes=[
            pltpu.VMEM((2 * rows, width), bf16),
            pltpu.VMEM((2 * rows, width), bf16),
            pltpu.VMEM((width, 2 * rows), bf16),
            pltpu.VMEM((width, block), held_type(chunk)),
            pltpu.VMEM((block, width), held_type(size)),
            pltpu.VMEM((2 * rows, width), f32),
            pltpu.VMEM((2 * rows, width), f32),
        ],
        out_shape=[pair] * 2
        + [jax.ShapeDtypeStruct((nodes // 2, chunk, hidden // 2), bf16)] * 2
        + [jax.ShapeDtypeStruct((flat // 2, 4, size, width), bf16)] * 2,
        compiler_params=params(62),
        name="feed",
        cost_estimate=cost(34),
    )


def back_kernel(
    me_ref, gain_ref, chosen_hbm, attn_hbm, score_hbm, pulled_hbm, own_hbm, other_hbm, queries_hbm,
    keys_hbm, values_hbm, probs_hbm, lefts_hbm, out_hbm,
    grads_out, after_out, gain_out, send_gone_out, send_stay_out, keep_gone_out, keep_stay_out,
    send_b_out, keep_b_out,
    chosen, attn, score, pulled, own, other, queries, keys, values, probs, lefts, out_w,
    grads, after_grad, send_gone, send_stay, keep_gone, keep_stay, send_b, keep_b,
    mix_grad, terms, sems,
    *, nodes, orders,
):
    copies = Copies(sems)
    fetched = {}
    for name, source, target in (
        ("rows", chosen_hbm, chosen), ("rows", attn_hbm, attn), ("rows", own_hbm.at[0], own),
        ("rows", other_hbm.at[0], other), ("rows", score_hbm, score), ("rows", pulled_hbm, pulled),
        ("out", out_hbm, out_w), ("heads", queries_hbm, queries), ("heads", keys_hbm, keys),
        ("heads", values_hbm, values), ("heads", probs_hbm, probs), ("lefts", lefts_hbm, lefts),
    ):
        fetched.setdefault(name, []).append(copies.start(source, target))

    def arrive(name):
        for copy in fetched[name]:
            copy.wait()

    seqs, groups, stack, slots = probs.shape
    width = chosen.shape[1]
    head = width // H
    gain = flat_row(gain_ref)
    gain_out[...] = jnp.zeros_like(gain_out)
    arrive("rows")

    def norm_grad(seq):
        rows = block_of(seq, slots)
        after = chosen[rows].astype(f32) + attn[rows]
        inv = inv_rms(after)
        normed = after * inv
        arrived = add_low(own[rows], other[rows]).astype(f32)
        gain_out[...] += fold(arrived * normed)
        weighted = arrived * gain
        back = inv * (weighted - normed * jnp.mean(weighted * normed, axis=-1, keepdims=True))
        after_grad[rows] = back
        delta = score[rows, :1] * pulled[rows].astype(f32)
        grads[3, rows] = (delta + back).astype(bf16)

    repeat(seqs, norm_grad)
    copies.send(after_grad, after_out)
    arrive("out")
    mix_grad[...] = dot_nt(grads[3], out_w[...]).astype(bf16)
    arrive("heads")

    def attention_grad(seq):
        rows = block_of(seq, slots)
        for g in range(groups):
            lanes = slice(g * GROUP * head, (g + 1) * GROUP * head)
            chances = probs[seq, g]
            wide = chances.astype(f32)
            stacked_queries = stacked(queries[rows, lanes], head)
            stacked_grads = stacked(mix_grad[rows, lanes], head)
            prob_grad = dot_nt(stacked_grads, values[rows, lanes])
            total = jnp.sum(prob_grad * wide, axis=-1, keepdims=True)
            score_grad = (wide * (prob_grad - total)).astype(bf16)
            grads[2, rows, lanes] = dot_tn(chances, stacked_grads).astype(bf16)
            grads[1, rows, lanes] = dot_tn(score_grad, stacked_queries).astype(bf16)
            grads[0, rows, lanes] = unstacked(dot_nn(score_grad, keys[rows, lanes]), head).astype(bf16)

    repeat(seqs, attention_grad, 2)
    copies.send(grads.at[pl.ds(0, 3)], grads_out)
    arrive("lefts")
    half, cut = nodes // 2, send_gone.shape[3]
    outs = [
        copies.send_group(4, lambda i, held=held, out=out: (held.at[:, i], out.at[:, i]))
        for held, out in (
            (send_gone, send_gone_out), (keep_gone, keep_gone_out), (send_stay, send_stay_out),
            (keep_stay, keep_stay_out), (send_b, send_b_out), (keep_b, keep_b_out),
        )
    ]

    def weight_grad(which):
        product = dot_tn(grads[which], lefts[lax.div(which, 3)])
        terms[...] = (product * jnp.where(which == 0, 0.125, 1.0)).astype(terms.dtype)
        for rel, kept, sent in own_blocks(me_ref, terms, send_b.shape[2], nodes):
            spot = spot_of(rel, orders[0])
            (keep_stay, keep_gone)[spot // half][spot % half, which] = kept[:, :cut]
            (send_stay, send_gone)[spot // half][spot % half, which] = sent[:, :cut]
            spot = spot_of(rel, orders[1])
            keep_b[spot, which] = kept[:, cut:]
            send_b[spot, which] = sent[:, cut:]
        for out in outs:
            out(which).start()

    repeat(4, weight_grad)
    copies.finish()


def back(
    me, chosen, attn, score, pulled, own, other, gain, queries, keys, values, probs, lefts, w_out, nodes,
    orders, cut,
):
    rows, width = chosen.shape
    seqs, _, _, slots = probs.shape
    size = width // (2 * nodes)
    layout = [(nodes // 2, cut)] * 4 + [(nodes, width - cut)] * 2
    shapes = [((count, 4, size, columns), bf16) for count, columns in layout]
    outs = [((3, rows, width), bf16), ((rows, width), f32)]
    fetched = [chosen, attn, score, pulled, own, other, queries, keys, values, probs, lefts, w_out]
    held = [pltpu.VMEM(array.shape, array.dtype) for array in fetched]
    held[4] = held[5] = pltpu.VMEM((rows, width), bf16)
    return call(
        functools.partial(back_kernel, nodes=nodes, orders=orders),
        [gain, *fetched],
        (),
        [me],
        grid=(1,),
        in_specs=[whole(gain)] + [HBM] * len(fetched),
        out_specs=[HBM, HBM, pl.BlockSpec((8, width), lambda *_: (0, 0))] + [HBM] * 6,
        scratch_shapes=held
        + [pltpu.VMEM(*out) for out in [((4, rows, width), bf16), outs[1]] + shapes]
        + [pltpu.VMEM((rows, width), bf16)]
        + [pltpu.VMEM((width, width), held_type(size))]
        + [pltpu.SemaphoreType.DMA((len(fetched) + 2 + 24,))],
        out_shape=[jax.ShapeDtypeStruct(*out) for out in outs]
        + [jax.ShapeDtypeStruct((8, width), f32)]
        + [jax.ShapeDtypeStruct(*shape) for shape in shapes],
        compiler_params=params(62),
        name="back",
        cost_estimate=cost(20),
    )


def last_kernel(
    gain_ref, router_ref, chosen_hbm, attn_hbm, own_hbm, other_hbm, score_hbm, pulled_hbm, after_hbm,
    grads_hbm, query_hbm, key_hbm, value_hbm,
    chosen_grad_out, gain_out, router_out,
    chosen, attn, own, other, score, pulled, after_grad, grads, weights, first_grad, chosen_grad, sems,
):
    copies = Copies(sems)
    pairs = [
        (copies.start(grads_hbm.at[i], grads.at[i]), copies.start(weight, weights.at[i]))
        for i, weight in enumerate((query_hbm, key_hbm, value_hbm))
    ]
    others = [
        copies.start(*pair)
        for pair in (
            (chosen_hbm, chosen), (attn_hbm, attn), (own_hbm.at[1], own), (other_hbm.at[1], other),
            (score_hbm, score), (pulled_hbm, pulled), (after_hbm, after_grad),
        )
    ]
    gain, router = flat_row(gain_ref), flat_row(router_ref)
    gain_out[...] = jnp.zeros_like(gain_out)
    router_out[...] = jnp.zeros_like(router_out)
    for i, pair in enumerate(pairs):
        for copy in pair:
            copy.wait()
        product = dot_nt(grads[i], weights[i])
        if i == 0:
            first_grad[...] = product * 0.125
        else:
            first_grad[...] += product
    for copy in others:
        copy.wait()
    turns = 4
    block = chosen.shape[0] // turns
    out = copies.send_group(
        turns,
        lambda i: (chosen_grad.at[block_of(i, block)], chosen_grad_out.at[block_of(i, block)]),
    )

    def rest(i):
        part = block_of(i, block)
        wide = chosen[part].astype(f32)
        chance = score[part, :1]
        branch = attn[part] + add_low(own[part], other[part]).astype(f32)
        pull = jnp.sum(pulled[part].astype(f32) * branch, axis=-1, keepdims=True)
        logit_grad = pull * chance * (1.0 - chance)
        arrived = first_grad[part]
        inv = inv_rms(wide)
        normed = wide * inv
        weighted = arrived * gain
        chosen_grad[part] = (
            inv * (weighted - normed * jnp.mean(weighted * normed, axis=-1, keepdims=True))
            + after_grad[part]
            + logit_grad * router
        )
        out(i).start()
        gain_out[...] += fold(arrived * normed)
        router_out[...] += fold(logit_grad * wide)

    repeat(turns, rest)
    copies.finish()


def last(
    chosen, attn, own, other, score, pulled, after_grad, grads, gain, router, wq, wk, wv, waits=()
):
    rows, width = chosen.shape
    fetched = [chosen, attn, own, other, score, pulled, after_grad, grads, wq, wk, wv]
    held = [pltpu.VMEM(array.shape, array.dtype) for array in fetched[:-3]]
    held[2] = held[3] = pltpu.VMEM((rows, width), bf16)
    held.append(pltpu.VMEM((3, width, width), bf16))
    sums = pl.BlockSpec((8, width), lambda *_: (0, 0))
    return call(
        last_kernel,
        [gain, router, *fetched],
        waits,
        grid=(1,),
        in_specs=[whole(gain), whole(router)] + [HBM] * len(fetched),
        out_specs=[HBM, sums, sums],
        scratch_shapes=held
        + [pltpu.VMEM((rows, width), f32)] * 2
        + [pltpu.SemaphoreType.DMA((17,))],
        out_shape=[jax.ShapeDtypeStruct((rows, width), f32)]
        + [jax.ShapeDtypeStruct((8, width), f32)] * 2,
        compiler_params=params(58),
        name="last",
        cost_estimate=cost(9),
    )


def spread_kernel(lengths_ref, index_ref, base_hbm, *refs, deltas, pieces):
    deltas_hbm, out_hbm, base, out = refs[:deltas], refs[deltas], refs[deltas + 1], refs[deltas + 2]
    held, sems = refs[deltas + 3 : -1], refs[-1]
    copies = Copies(sems)
    seqs, _, slots = index_ref.shape
    count = base.shape[1]

    def delta_copy(source, target):
        top = source.shape[0] - 1
        place = lambda row: source.at[top, row] if len(source.shape) == 3 else source.at[row]
        return copies.group(
            seqs, lambda seq: (place(block_of(seq, slots)), target.at[block_of(seq, slots)])
        )

    delta_copies = [delta_copy(*pair) for pair in zip(deltas_hbm, held)]
    base_copy = copies.group(
        seqs * pieces, lambda at: (base_hbm.at[block_of(at, count)], base.at[at])
    )
    for seq in range(seqs):
        for copy in delta_copies:
            copy(seq).start()
        for piece in range(pieces):
            base_copy(seq * pieces + piece).start()
    out_copy = copies.send_group(
        seqs * pieces, lambda at: (out.at[at], out_hbm.at[block_of(at, count)])
    )

    def one(seq):
        rows = block_of(seq, slots)
        for copy in delta_copies:
            copy(seq).wait()
        if deltas == 1:
            delta = held[0][rows]
        else:
            score, attn, own, other = held
            delta = score[rows, :1] * (attn[rows] + add_low(own[rows], other[rows]).astype(f32))
        high = delta.astype(bf16)
        low = (delta - high.astype(f32)).astype(bf16)
        both = jnp.concatenate([high, low], axis=0)
        slot_id = lax.broadcasted_iota(jnp.int32, (count, slots), 1)
        live = slot_id < lax.div(lengths_ref[0, seq], 8)
        for piece in range(pieces):
            place = piece * count + lax.broadcasted_iota(jnp.int32, (count, slots), 0)
            pick = ((index_ref[seq] == place) & live).astype(bf16)
            at = seq * pieces + piece
            base_copy(at).wait()
            added = dot_nn(jnp.concatenate([pick, pick], axis=1), both)
            out[at] = (base[at].astype(f32) + added).astype(out.dtype)
            out_copy(at).start()

    repeat(seqs, one)
    copies.finish()


def spread(lengths, index, base, deltas, dtype, waits=(), pieces=2):
    seqs, slots = index.shape
    rows, width = base.shape
    steps = seqs * pieces
    index = index[:, None, :]
    held = [pltpu.VMEM(delta.shape[-2:], delta.dtype) for delta in deltas]
    return call(
        functools.partial(spread_kernel, deltas=len(deltas), pieces=pieces),
        [index, base, *deltas],
        waits,
        [lengths],
        grid=(1,),
        in_specs=[whole(index)] + [HBM] * (1 + len(deltas)),
        out_specs=HBM,
        scratch_shapes=[
            pltpu.VMEM((steps, rows // steps, width), bf16),
            pltpu.VMEM((steps, rows // steps, width), dtype),
            *held,
            pltpu.SemaphoreType.DMA((2 * steps + len(deltas) * seqs,)),
        ],
        out_shape=jax.ShapeDtypeStruct((rows, width), dtype),
        compiler_params=params(58),
        name="spread",
        cost_estimate=cost(8),
    )


def add_low(left, right):
    return (left.astype(f32) + right.astype(f32)).astype(bf16)


def swap_nodes(values, bit, nodes):
    return lax.ppermute(values, "seq", [(i, i ^ (1 << bit)) for i in range(nodes)])


def swap_cores(values):
    return lax.ppermute(values, "dp", [(0, 1), (1, 0)])


class Part:
    def __init__(self, order, nodes):
        self.order, self.nodes = order, nodes

    @classmethod
    def halved(cls, gone, kept, order, nodes):
        part = cls(order, nodes)
        part.gone, part.kept = gone, kept
        part.swap()
        return part

    @classmethod
    def of_cores(cls, send, keep, order, nodes):
        part = cls(order, nodes)
        part.kept, part.got = keep, swap_cores(send)
        return part

    @classmethod
    def of_split_cores(cls, send_gone, send_stay, keep_gone, keep_stay, order, nodes):
        part = cls(order, nodes)
        part.halves = (keep_gone, swap_cores(send_gone)), (keep_stay, swap_cores(send_stay))
        return part

    halves = None

    def swap(self):
        self.got = swap_nodes(self.gone, self.order[0], self.nodes)
        self.order = self.order[1:]

    def halve(self, after=()):
        if self.halves:
            (keep_gone, got_gone), (keep_stay, got_stay), *_ = lax.optimization_barrier(
                (*self.halves, *after)
            )
            self.gone, self.kept = add_low(keep_gone, got_gone), add_low(keep_stay, got_stay)
            self.halves = None
            return
        if after:
            self.kept, self.got, *_ = lax.optimization_barrier((self.kept, self.got, *after))
        if self.kept.shape[0] == 1:
            self.kept, self.got = self.kept[0], self.got[0]
        count = self.kept.shape[0] // 2
        halves = [add_low(self.kept[c], self.got[c]) for c in (slice(count, None), slice(count))]
        self.gone, self.kept = [half[0] for half in halves] if count == 1 else halves

    def step(self, after=()):
        self.halve(after)
        self.swap()
        return self.gone


class Chain:
    def __init__(self, parts):
        self.parts = parts

    def step(self, count=1, after=()):
        sent = []
        for _ in range(count):
            sent = []
            for part in self.parts:
                sent.append(part.step([*after, *sent]))
        return sent

    def final(self, after=()):
        for part in self.parts:
            part.halve(after)
        gone = jnp.concatenate([part.gone for part in self.parts], axis=-1)
        self.got = swap_nodes(gone, self.parts[0].order[0], self.parts[0].nodes)
        return [gone]

    def sum(self):
        kept = jnp.concatenate([part.kept for part in self.parts], axis=-1)
        return kept.astype(f32) + self.got.astype(f32)


def both_cores(core, rows, nodes):
    count = rows.shape[0] // 2
    mine, sent = [
        lax.dynamic_slice_in_dim(rows, side * count, count) for side in (core, 1 - core)
    ]
    got = swap_cores(sent)
    shape = (count, nodes, 1, rows.shape[1] // nodes)
    sides = [jnp.where(core == side, mine, got).reshape(shape) for side in (0, 1)]
    return jnp.concatenate(sides, axis=2).reshape(count, -1)


def on_device(
    tokens,
    lengths,
    routed_index,
    out_grad,
    gain_attn,
    w_router,
    w_query,
    w_key,
    w_value,
    w_out,
    gain_mlp,
    w_up,
    w_down,
):
    nodes = lax.axis_size("seq")
    width = tokens.shape[2]
    me = jnp.stack([lax.axis_index("dp"), lax.axis_index("seq")]).astype(jnp.int32)
    index = routed_index[0]
    inputs, cotangent = tokens[0], out_grad[0]
    vectors = [vector.reshape(-1, 128) for vector in (gain_attn, w_router, gain_mlp)]
    (
        chosen, lefts, queries, keys, values, probs, attn_out, feed_own, pulled, score,
    ) = front(
        lengths, index, inputs, cotangent, vectors, w_query, w_key, w_value, w_out
    )
    feed_other = swap_cores(feed_own)
    order = lambda names: link_order(nodes, names)
    span = len(order("x"))
    down_order, up_order = order("nxfy"), order("xynf")
    square_orders = [order("nxyf"), order("yxnf")]
    own_sums, other_sums, *terms = feed(
        me, feed_own, feed_other, w_up, w_down, nodes, [down_order, up_order]
    )
    got_sums = swap_cores(other_sums)
    down = Chain([Part.halved(*terms[:2], down_order, nodes)])
    up = Chain([Part.halved(*terms[2:], up_order, nodes)])
    grads, after_grad, gain_mlp_sum, *square_terms = back(
        me, chosen, attn_out, score, pulled, own_sums, got_sums, vectors[2], queries, keys, values, probs,
        lefts, w_out, nodes, square_orders, width // 2,
    )
    square = Chain(
        [
            Part.of_split_cores(*square_terms[:4], square_orders[0], nodes),
            Part.of_cores(*square_terms[4:], square_orders[1], nodes),
        ]
    )
    mixed_out = spread(
        lengths, index, inputs, [score, attn_out, own_sums, got_sums], bf16, waits=square_terms[:1]
    )
    chosen_grad, gain_attn_sum, router_sum = last(
        chosen, attn_out, own_sums, got_sums, score, pulled, after_grad, grads,
        vectors[0], vectors[1], w_query, w_key, w_value, waits=[mixed_out],
    )
    sums = jnp.sum(jnp.stack([gain_attn_sum, router_sum, gain_mlp_sum]), axis=1)
    sums = sums.reshape(3, 2 * nodes, -1).transpose(1, 0, 2)
    gone = down.step(span, after=[chosen_grad])
    gone += up.step(span, after=gone)
    gone += square.step(after=gone)
    token_grad = spread(lengths, index, cotangent, [chosen_grad], f32, waits=gone)
    gone = down.step(span, after=[token_grad])
    gone = up.step(span, after=gone)
    gone = square.step(span, after=gone)
    gone = down.final(after=gone)
    gone = up.final(after=gone)
    gone = square.step(span, after=gone)
    down_sum, _ = lax.optimization_barrier((both_cores(me[0], down.sum(), nodes), gone[0]))
    gone = square.final(after=[up.sum()])
    sums, *_ = lax.optimization_barrier((sums, *gone))
    sums = jnp.sum(lax.all_to_all(sums, ("seq", "dp"), 0, 0, tiled=True), axis=0)
    square_sum = square.sum()
    return (
        mixed_out[None],
        token_grad[None],
        sums[0],
        sums[1],
        *[square_sum[which].T for which in range(4)],
        sums[2],
        up.sum().T,
        down_sum.T,
    )


def solution(mesh):
    in_specs = (
        P("dp", "seq", None),
        P("dp", "seq"),
        P("dp", "seq", None),
        P("dp", "seq", None),
        P(),
        P(),
        P(),
        P(),
        P(),
        P(),
        P(),
        P(),
        P(),
    )
    out_specs = (
        P("dp", "seq", None),
        P("dp", "seq", None),
        P(("seq", "dp")),
        P(("seq", "dp")),
        P(None, ("seq", "dp")),
        P(None, ("seq", "dp")),
        P(None, ("seq", "dp")),
        P(None, ("seq", "dp")),
        P(("seq", "dp")),
        P(None, ("seq", "dp")),
        P(None, ("seq", "dp")),
    )
    return jax.shard_map(
        on_device, mesh=mesh, in_specs=in_specs, out_specs=out_specs, check_vma=False
    )
```

```python
import functools

import jax
import jax.experimental.pallas as pl
import jax.experimental.pallas.tpu as pltpu
import jax.numpy as jnp
from jax import lax
from jax.sharding import PartitionSpec as P

H = 16
norm_eps = 1e-05
f32 = jnp.float32
bf16 = jnp.bfloat16


def params(mebibytes):
    return pltpu.CompilerParams(
        dimension_semantics=("arbitrary",), vmem_limit_bytes=mebibytes * 1024 * 1024
    )


def cost(micros):
    return pl.CostEstimate(
        flops=int(micros * 1e8), bytes_accessed=int(micros * 3.5e5), transcendentals=0
    )


def call(kernel, arrays, waits=(), scalars=(), **rest):
    first = len(scalars) + len(arrays)

    def body(*refs):
        kernel(*refs[:first], *refs[first + len(waits) :])

    grid = pltpu.PrefetchScalarGridSpec(
        num_scalar_prefetch=len(scalars),
        grid=rest.pop("grid"),
        in_specs=list(rest.pop("in_specs")) + [pl.BlockSpec(memory_space=pl.ANY)] * len(waits),
        out_specs=rest.pop("out_specs"),
        scratch_shapes=rest.pop("scratch_shapes", ()),
    )
    return pl.pallas_call(body, grid_spec=grid, **rest)(*scalars, *arrays, *waits)


def whole(array):
    rank = len(array.shape)
    return pl.BlockSpec(array.shape, lambda *_: (0,) * rank, pipeline_mode=pl.Buffered(1))


def dot_nn(left, right):
    return lax.dot_general(left, right, (((1,), (0,)), ((), ())), preferred_element_type=f32)


def dot_nt(left, right):
    return lax.dot_general(left, right, (((1,), (1,)), ((), ())), preferred_element_type=f32)


def dot_tn(left, right):
    return lax.dot_general(left, right, (((0,), (0,)), ((), ())), preferred_element_type=f32)


def inv_rms(values):
    return lax.rsqrt(jnp.mean(values * values, axis=-1, keepdims=True) + norm_eps)


GROUP = 4


def flat_row(ref):
    values = ref[...].astype(f32)
    return jnp.concatenate([values[i : i + 1] for i in range(values.shape[0])], axis=1)


def fold(values):
    rows, width = values.shape
    return jnp.sum(values.reshape(rows // 8, 8, width), axis=0)


class Copies:
    def __init__(self, sems):
        self.sems, self.count, self.sent = sems, 0, []

    def one(self, source, target):
        self.count += 1
        return pltpu.make_async_copy(source, target, self.sems.at[self.count - 1])

    def group(self, turns, pair):
        first = self.count
        self.count += turns

        def at(turn):
            source, target = pair(turn)
            return pltpu.make_async_copy(source, target, self.sems.at[first + turn])

        return at

    def start(self, source, target):
        copy = self.one(source, target)
        copy.start()
        return copy

    def send(self, source, target):
        self.sent.append(self.start(source, target))

    def send_group(self, turns, pair):
        at = self.group(turns, pair)
        self.sent += [at(turn) for turn in range(turns)]
        return at

    def finish(self):
        for copy in self.sent:
            copy.wait()


def repeat(turns, body, unroll=1):
    lax.fori_loop(0, turns, lambda turn, carry: body(turn), None, unroll=unroll)


def block_of(turn, size):
    return pl.ds(pl.multiple_of(turn * size, size), size)


HBM = pl.BlockSpec(memory_space=pl.ANY)


def stacked(rows, head):
    lane_head = lax.broadcasted_iota(jnp.int32, rows.shape, 1) // head
    zero = jnp.zeros_like(rows)
    return jnp.concatenate([jnp.where(lane_head == h, rows, zero) for h in range(GROUP)], axis=0)


def unstacked(rows, head):
    slots = rows.shape[0] // GROUP
    lane_head = lax.broadcasted_iota(jnp.int32, (slots, rows.shape[1]), 1) // head
    out = rows[:slots]
    for h in range(1, GROUP):
        out = jnp.where(lane_head == h, rows[h * slots : (h + 1) * slots], out)
    return out


def front_kernel(
    lengths_ref, index_ref, gain_one_ref, router_ref, gain_two_ref,
    tokens_hbm, cotangent_hbm, query_hbm, key_hbm, value_hbm, out_hbm,
    chosen_out, lefts_out, queries_out, keys_out, values_out, probs_out, attn_out, feed_out, pulled_out,
    score_out,
    tokens, cotangent, query_w, key_w, value_w, out_w,
    chosen, lefts, queries, keys, values, probs, attn, feed, pulled, score, sems,
):
    copies = Copies(sems)
    seqs, _, slots = index_ref.shape
    places, width = tokens.shape[1], tokens.shape[2]
    head = width // H
    token_copy = copies.group(
        seqs, lambda seq: (tokens_hbm.at[block_of(seq, places)], tokens.at[seq])
    )
    cotangent_copy = copies.group(
        seqs, lambda seq: (cotangent_hbm.at[block_of(seq, places)], cotangent.at[seq])
    )
    for seq in range(seqs):
        token_copy(seq).start()
        cotangent_copy(seq).start()
    weights = [
        copies.start(*pair)
        for pair in (
            (query_hbm, query_w), (key_hbm, key_w), (value_hbm, value_w), (out_hbm, out_w),
        )
    ]
    gain_one, router, gain_two = [flat_row(r) for r in (gain_one_ref, router_ref, gain_two_ref)]

    def gather(seq):
        rows = block_of(seq, slots)
        slot_id = lax.broadcasted_iota(jnp.int32, (slots, places), 0)
        place_id = lax.broadcasted_iota(jnp.int32, (slots, places), 1)
        square = (slots, slots)
        diagonal = lax.broadcasted_iota(jnp.int32, square, 0) == lax.broadcasted_iota(
            jnp.int32, square, 1
        )
        routed = lax.div(lengths_ref[0, seq], 8)
        index = jnp.sum(jnp.where(diagonal, index_ref[seq], 0), axis=1, keepdims=True)
        pick = ((index == place_id) & (slot_id < routed)).astype(bf16)
        token_copy(seq).wait()
        wide = dot_nn(pick, tokens[seq])
        chosen[rows] = wide.astype(bf16)
        logit = jnp.sum(wide * router, axis=-1, keepdims=True)
        chance = 1.0 / (1.0 + jnp.exp(-logit))
        score[rows] = jnp.broadcast_to(chance, (slots, score.shape[1]))
        lefts[0, rows] = (wide * inv_rms(wide) * gain_one).astype(bf16)
        cotangent_copy(seq).wait()
        pull = dot_nn(pick, cotangent[seq])
        pulled[rows] = pull.astype(bf16)
        feed[1, rows] = (chance * pull).astype(bf16)

    repeat(seqs, gather, 4)
    copies.send(chosen, chosen_out)
    copies.send(pulled, pulled_out)
    copies.send(score, score_out)
    copies.send(feed.at[1], feed_out.at[1])
    copies.send(lefts.at[0], lefts_out.at[0])
    first = lefts[0]
    weights[0].wait()
    queries[...] = (dot_nn(first, query_w[...]) * 0.125).astype(bf16)
    copies.send(queries, queries_out)
    weights[1].wait()
    keys[...] = dot_nn(first, key_w[...]).astype(bf16)
    copies.send(keys, keys_out)
    weights[2].wait()
    values[...] = dot_nn(first, value_w[...]).astype(bf16)
    copies.send(values, values_out)
    probs_copy = copies.send_group(seqs, lambda seq: (probs.at[seq], probs_out.at[seq]))

    def attend(seq):
        rows = block_of(seq, slots)
        stack = GROUP * slots
        row_id = lax.broadcasted_iota(jnp.int32, (stack, slots), 0) % slots
        col_id = lax.broadcasted_iota(jnp.int32, (stack, slots), 1)
        allowed = (col_id <= row_id) & (col_id < lax.div(lengths_ref[0, seq], 8))
        for g in range(H // GROUP):
            lanes = slice(g * GROUP * head, (g + 1) * GROUP * head)
            scores = dot_nt(stacked(queries[rows, lanes], head), keys[rows, lanes])
            scores = jnp.where(allowed, scores, -1e30)
            exped = jnp.exp(scores - jnp.max(scores, axis=-1, keepdims=True))
            chances = (exped / jnp.sum(exped, axis=-1, keepdims=True)).astype(bf16)
            probs[seq, g] = chances
            mixed = dot_nn(chances, values[rows, lanes])
            lefts[1, rows, lanes] = unstacked(mixed, head).astype(bf16)
        probs_copy(seq).start()

    repeat(seqs, attend, 4)
    copies.send(lefts.at[1], lefts_out.at[1])
    weights[3].wait()
    attn[...] = dot_nn(lefts[1], out_w[...])
    copies.send(attn, attn_out)

    def after_attention(seq):
        rows = block_of(seq, slots)
        after = chosen[rows].astype(f32) + attn[rows]
        feed[0, rows] = (after * inv_rms(after) * gain_two).astype(bf16)

    repeat(seqs, after_attention)
    copies.send(feed.at[0], feed_out.at[0])
    copies.finish()


def front(lengths, index, tokens, cotangent, vectors, wq, wk, wv, wo):
    seqs, slots = index.shape
    places, width = tokens.shape[0] // seqs, tokens.shape[1]
    rows = seqs * slots
    low = ((rows, width), bf16)
    outs = [
        low, ((2, rows, width), bf16), low, low, low,
        ((seqs, H // GROUP, GROUP * slots, slots), bf16), ((rows, width), f32),
        ((2, rows, width), bf16), low, ((rows, 128), f32),
    ]
    small = [index[:, None, :], *vectors]
    return call(
        front_kernel,
        [*small, tokens, cotangent, wq, wk, wv, wo],
        (),
        [lengths],
        grid=(1,),
        in_specs=[whole(array) for array in small] + [HBM] * 6,
        out_specs=[HBM] * len(outs),
        scratch_shapes=[pltpu.VMEM((seqs, places, width), bf16)] * 2
        + [pltpu.VMEM((width, width), bf16)] * 4
        + [pltpu.VMEM(*out) for out in outs]
        + [pltpu.SemaphoreType.DMA((2 * seqs + 4 + 11 + seqs,))],
        out_shape=[jax.ShapeDtypeStruct(*out) for out in outs],
        compiler_params=params(58),
        name="front",
        cost_estimate=cost(18),
    )


def gelu_both(z):
    cdf = 0.5 + 0.5 * lax.erf(z * 0.7071067811865476)
    return z * cdf, cdf + z * (jnp.exp(-0.5 * z * z) * 0.3989422804014327)


def link_bits(nodes):
    bits = nodes.bit_length() - 1
    half = (bits - 2) // 2
    return list(range(half)), list(range(half, bits - 2)), [bits - 2], [bits - 1]


def link_order(nodes, names):
    x, y, near, far = link_bits(nodes)
    return sum([{"x": x, "y": y, "n": near, "f": far}[name] for name in names], [])


def spot_of(rel, order):
    return sum(((rel >> bit) & 1) << (len(order) - 1 - i) for i, bit in enumerate(order))


def own_blocks(me_ref, source, size, nodes):
    core, node = me_ref[0], me_ref[1]
    for rel in range(nodes):
        owner = lax.bitwise_xor(node, rel) * 2
        starts = [pl.multiple_of((owner + side) * size, size) for side in (core, 1 - core)]
        yield rel, *[source[pl.ds(start, size), :].astype(bf16) for start in starts]


def held_type(size):
    return bf16 if size % 16 == 0 else f32


def feed_kernel(me_ref, own_ref, other_ref, *refs, nodes, pieces, orders):
    ups, downs, refs = refs[:pieces], refs[pieces : 2 * pieces], refs[2 * pieces :]
    (
        sums_ref, sent_ref, down_gone, down_kept, up_gone, up_kept,
        rows_ref, grads_ref, turned_ref, down_terms, up_terms, grad_sum, out_sum,
    ) = refs
    step, steps = pl.program_id(0), pl.num_programs(0)
    node = me_ref[1]
    flat = nodes // 4
    count = own_ref.shape[1]

    @pl.when(step == 0)
    def _():
        rows_ref[:count] = own_ref[0]
        rows_ref[count:] = other_ref[0]
        grads_ref[:count] = own_ref[1]
        grads_ref[count:] = other_ref[1]
        turned_ref[...] = grads_ref[...].T
        out_sum[...] = jnp.zeros_like(out_sum)
        grad_sum[...] = jnp.zeros_like(grad_sum)

    w_up = jnp.concatenate([ref[...] for ref in ups], axis=1)
    w_down = jnp.concatenate([ref[...] for ref in downs], axis=0)
    hidden = dot_nn(rows_ref[...], w_up)
    act, slope = gelu_both(hidden)
    act = act.astype(bf16)
    pre = (dot_nt(grads_ref[...], w_down) * slope).astype(bf16)

    down_terms[...] = dot_nn(turned_ref[...], act).astype(down_terms.dtype)
    size = down_terms.shape[0] // nodes
    for rel in range(nodes):
        spot = spot_of(rel, orders[0])
        start = pl.multiple_of(lax.bitwise_xor(node, rel) * size, size)
        values = down_terms[pl.ds(start, size), :].astype(bf16)
        (down_kept, down_gone)[spot // (nodes // 2)][spot % (nodes // 2)] = values

    up_terms[...] = dot_tn(pre, rows_ref[...]).astype(up_terms.dtype)
    size = up_kept.shape[2]
    for rel in range(flat):
        spot = spot_of(rel, orders[1][:-2])
        start = pl.multiple_of(lax.bitwise_xor(lax.rem(node, flat), rel) * size, size)
        values = up_terms[pl.ds(start, size), :].astype(bf16)
        (up_kept, up_gone)[spot // (flat // 2)][spot % (flat // 2), 0] = values

    out_sum[...] += dot_nn(act, w_down)
    grad_sum[...] += dot_nt(pre, w_up)

    @pl.when(step == steps - 1)
    def _():
        for i, total in enumerate((grad_sum, out_sum)):
            sums_ref[i] = total[:count].astype(bf16)
            sent_ref[i] = total[count:].astype(bf16)


def feed(me, own, other, w_up, w_down, nodes, orders, steps=4, waits=()):
    _, rows, width = own.shape
    hidden = w_up.shape[1]
    flat = nodes // 4
    size = hidden // (2 * nodes)
    block = hidden // 2 // steps
    if size % 128:
        w_up = lax.dynamic_index_in_dim(w_up.reshape(width, nodes, 2, size), me[0], 2, False)
        w_down = lax.dynamic_index_in_dim(w_down.reshape(nodes, 2, size, width), me[0], 1, False)
        w_up, w_down = w_up.reshape(width, -1), w_down.reshape(-1, width)
        pieces = 1
        place = lambda piece, i, me: i
    else:
        pieces = block // size
        place = lambda piece, i, me: (i * pieces + piece) * 2 + me[0]
    columns = block // pieces
    up_specs = [
        pl.BlockSpec((width, columns), lambda i, me, p=p: (0, place(p, i, me)))
        for p in range(pieces)
    ]
    down_specs = [
        pl.BlockSpec((columns, width), lambda i, me, p=p: (place(p, i, me), 0))
        for p in range(pieces)
    ]
    chunk = width // nodes
    down_spec = pl.BlockSpec((nodes // 2, chunk, block), lambda i, me: (0, 0, i))
    near_first = orders[1][-2] < orders[1][-1]

    def up_place(i, me):
        rel = lax.bitwise_xor(i, lax.div(me[1], flat))
        return (0, lax.rem(rel, 2) * 2 + lax.div(rel, 2) if near_first else rel, 0, 0)

    up_spec = pl.BlockSpec((flat // 2, 1, size, width), up_place)
    pair = jax.ShapeDtypeStruct((2, rows, width), bf16)
    return call(
        functools.partial(feed_kernel, nodes=nodes, pieces=pieces, orders=orders),
        [own, other] + [w_up] * pieces + [w_down] * pieces,
        waits,
        [me],
        grid=(steps,),
        in_specs=[whole(own), whole(other)] + up_specs + down_specs,
        out_specs=[pl.BlockSpec((2, rows, width), lambda i, me: (0, 0, 0))] * 2
        + [down_spec, down_spec, up_spec, up_spec],
        scratch_shapes=[
            pltpu.VMEM((2 * rows, width), bf16),
            pltpu.VMEM((2 * rows, width), bf16),
            pltpu.VMEM((width, 2 * rows), bf16),
            pltpu.VMEM((width, block), held_type(chunk)),
            pltpu.VMEM((block, width), held_type(size)),
            pltpu.VMEM((2 * rows, width), f32),
            pltpu.VMEM((2 * rows, width), f32),
        ],
        out_shape=[pair] * 2
        + [jax.ShapeDtypeStruct((nodes // 2, chunk, hidden // 2), bf16)] * 2
        + [jax.ShapeDtypeStruct((flat // 2, 4, size, width), bf16)] * 2,
        compiler_params=params(62),
        name="feed",
        cost_estimate=cost(34),
    )


def back_kernel(
    me_ref, gain_ref, chosen_hbm, attn_hbm, score_hbm, pulled_hbm, own_hbm, other_hbm, queries_hbm,
    keys_hbm, values_hbm, probs_hbm, lefts_hbm, out_hbm,
    grads_out, after_out, gain_out, send_gone_out, send_stay_out, keep_gone_out, keep_stay_out,
    send_b_out, keep_b_out,
    chosen, attn, score, pulled, own, other, queries, keys, values, probs, lefts, out_w,
    grads, after_grad, send_gone, send_stay, keep_gone, keep_stay, send_b, keep_b,
    mix_grad, terms, sems,
    *, nodes, orders,
):
    copies = Copies(sems)
    fetched = {}
    for name, source, target in (
        ("rows", chosen_hbm, chosen), ("rows", attn_hbm, attn), ("rows", own_hbm.at[0], own),
        ("rows", other_hbm.at[0], other), ("rows", score_hbm, score), ("rows", pulled_hbm, pulled),
        ("out", out_hbm, out_w), ("heads", queries_hbm, queries), ("heads", keys_hbm, keys),
        ("heads", values_hbm, values), ("heads", probs_hbm, probs), ("lefts", lefts_hbm, lefts),
    ):
        fetched.setdefault(name, []).append(copies.start(source, target))

    def arrive(name):
        for copy in fetched[name]:
            copy.wait()

    seqs, groups, stack, slots = probs.shape
    width = chosen.shape[1]
    head = width // H
    gain = flat_row(gain_ref)
    gain_out[...] = jnp.zeros_like(gain_out)
    arrive("rows")

    def norm_grad(seq):
        rows = block_of(seq, slots)
        after = chosen[rows].astype(f32) + attn[rows]
        inv = inv_rms(after)
        normed = after * inv
        arrived = add_low(own[rows], other[rows]).astype(f32)
        gain_out[...] += fold(arrived * normed)
        weighted = arrived * gain
        back = inv * (weighted - normed * jnp.mean(weighted * normed, axis=-1, keepdims=True))
        after_grad[rows] = back
        delta = score[rows, :1] * pulled[rows].astype(f32)
        grads[3, rows] = (delta + back).astype(bf16)

    repeat(seqs, norm_grad)
    copies.send(after_grad, after_out)
    arrive("out")
    mix_grad[...] = dot_nt(grads[3], out_w[...]).astype(bf16)
    arrive("heads")

    def attention_grad(seq):
        rows = block_of(seq, slots)
        for g in range(groups):
            lanes = slice(g * GROUP * head, (g + 1) * GROUP * head)
            chances = probs[seq, g]
            wide = chances.astype(f32)
            stacked_queries = stacked(queries[rows, lanes], head)
            stacked_grads = stacked(mix_grad[rows, lanes], head)
            prob_grad = dot_nt(stacked_grads, values[rows, lanes])
            total = jnp.sum(prob_grad * wide, axis=-1, keepdims=True)
            score_grad = (wide * (prob_grad - total)).astype(bf16)
            grads[2, rows, lanes] = dot_tn(chances, stacked_grads).astype(bf16)
            grads[1, rows, lanes] = dot_tn(score_grad, stacked_queries).astype(bf16)
            grads[0, rows, lanes] = unstacked(dot_nn(score_grad, keys[rows, lanes]), head).astype(bf16)

    repeat(seqs, attention_grad)
    copies.send(grads.at[pl.ds(0, 3)], grads_out)
    arrive("lefts")
    half, cut = nodes // 2, send_gone.shape[3]
    outs = [
        copies.send_group(4, lambda i, held=held, out=out: (held.at[:, i], out.at[:, i]))
        for held, out in (
            (send_gone, send_gone_out), (keep_gone, keep_gone_out), (send_stay, send_stay_out),
            (keep_stay, keep_stay_out), (send_b, send_b_out), (keep_b, keep_b_out),
        )
    ]

    def weight_grad(which):
        product = dot_tn(grads[which], lefts[lax.div(which, 3)])
        terms[...] = (product * jnp.where(which == 0, 0.125, 1.0)).astype(terms.dtype)
        for rel, kept, sent in own_blocks(me_ref, terms, send_b.shape[2], nodes):
            spot = spot_of(rel, orders[0])
            (keep_stay, keep_gone)[spot // half][spot % half, which] = kept[:, :cut]
            (send_stay, send_gone)[spot // half][spot % half, which] = sent[:, :cut]
            spot = spot_of(rel, orders[1])
            keep_b[spot, which] = kept[:, cut:]
            send_b[spot, which] = sent[:, cut:]
        for out in outs:
            out(which).start()

    repeat(4, weight_grad)
    copies.finish()


def back(
    me, chosen, attn, score, pulled, own, other, gain, queries, keys, values, probs, lefts, w_out, nodes,
    orders, cut,
):
    rows, width = chosen.shape
    seqs, _, _, slots = probs.shape
    size = width // (2 * nodes)
    layout = [(nodes // 2, cut)] * 4 + [(nodes, width - cut)] * 2
    shapes = [((count, 4, size, columns), bf16) for count, columns in layout]
    outs = [((3, rows, width), bf16), ((rows, width), f32)]
    fetched = [chosen, attn, score, pulled, own, other, queries, keys, values, probs, lefts, w_out]
    held = [pltpu.VMEM(array.shape, array.dtype) for array in fetched]
    held[4] = held[5] = pltpu.VMEM((rows, width), bf16)
    return call(
        functools.partial(back_kernel, nodes=nodes, orders=orders),
        [gain, *fetched],
        (),
        [me],
        grid=(1,),
        in_specs=[whole(gain)] + [HBM] * len(fetched),
        out_specs=[HBM, HBM, pl.BlockSpec((8, width), lambda *_: (0, 0))] + [HBM] * 6,
        scratch_shapes=held
        + [pltpu.VMEM(*out) for out in [((4, rows, width), bf16), outs[1]] + shapes]
        + [pltpu.VMEM((rows, width), bf16)]
        + [pltpu.VMEM((width, width), held_type(size))]
        + [pltpu.SemaphoreType.DMA((len(fetched) + 2 + 24,))],
        out_shape=[jax.ShapeDtypeStruct(*out) for out in outs]
        + [jax.ShapeDtypeStruct((8, width), f32)]
        + [jax.ShapeDtypeStruct(*shape) for shape in shapes],
        compiler_params=params(62),
        name="back",
        cost_estimate=cost(20),
    )


def last_kernel(
    gain_ref, router_ref, chosen_hbm, attn_hbm, own_hbm, other_hbm, score_hbm, pulled_hbm, after_hbm,
    grads_hbm, query_hbm, key_hbm, value_hbm,
    chosen_grad_out, gain_out, router_out,
    chosen, attn, own, other, score, pulled, after_grad, grads, weights, first_grad, chosen_grad, sems,
):
    copies = Copies(sems)
    pairs = [
        (copies.start(grads_hbm.at[i], grads.at[i]), copies.start(weight, weights.at[i]))
        for i, weight in enumerate((query_hbm, key_hbm, value_hbm))
    ]
    others = [
        copies.start(*pair)
        for pair in (
            (chosen_hbm, chosen), (attn_hbm, attn), (own_hbm.at[1], own), (other_hbm.at[1], other),
            (score_hbm, score), (pulled_hbm, pulled), (after_hbm, after_grad),
        )
    ]
    gain, router = flat_row(gain_ref), flat_row(router_ref)
    gain_out[...] = jnp.zeros_like(gain_out)
    router_out[...] = jnp.zeros_like(router_out)
    for i, pair in enumerate(pairs):
        for copy in pair:
            copy.wait()
        product = dot_nt(grads[i], weights[i])
        if i == 0:
            first_grad[...] = product * 0.125
        else:
            first_grad[...] += product
    for copy in others:
        copy.wait()
    turns = 4
    block = chosen.shape[0] // turns
    out = copies.send_group(
        turns,
        lambda i: (chosen_grad.at[block_of(i, block)], chosen_grad_out.at[block_of(i, block)]),
    )

    def rest(i):
        part = block_of(i, block)
        wide = chosen[part].astype(f32)
        chance = score[part, :1]
        branch = attn[part] + add_low(own[part], other[part]).astype(f32)
        pull = jnp.sum(pulled[part].astype(f32) * branch, axis=-1, keepdims=True)
        logit_grad = pull * chance * (1.0 - chance)
        arrived = first_grad[part]
        inv = inv_rms(wide)
        normed = wide * inv
        weighted = arrived * gain
        chosen_grad[part] = (
            inv * (weighted - normed * jnp.mean(weighted * normed, axis=-1, keepdims=True))
            + after_grad[part]
            + logit_grad * router
        )
        out(i).start()
        gain_out[...] += fold(arrived * normed)
        router_out[...] += fold(logit_grad * wide)

    repeat(turns, rest)
    copies.finish()


def last(
    chosen, attn, own, other, score, pulled, after_grad, grads, gain, router, wq, wk, wv, waits=()
):
    rows, width = chosen.shape
    fetched = [chosen, attn, own, other, score, pulled, after_grad, grads, wq, wk, wv]
    held = [pltpu.VMEM(array.shape, array.dtype) for array in fetched[:-3]]
    held[2] = held[3] = pltpu.VMEM((rows, width), bf16)
    held.append(pltpu.VMEM((3, width, width), bf16))
    sums = pl.BlockSpec((8, width), lambda *_: (0, 0))
    return call(
        last_kernel,
        [gain, router, *fetched],
        waits,
        grid=(1,),
        in_specs=[whole(gain), whole(router)] + [HBM] * len(fetched),
        out_specs=[HBM, sums, sums],
        scratch_shapes=held
        + [pltpu.VMEM((rows, width), f32)] * 2
        + [pltpu.SemaphoreType.DMA((17,))],
        out_shape=[jax.ShapeDtypeStruct((rows, width), f32)]
        + [jax.ShapeDtypeStruct((8, width), f32)] * 2,
        compiler_params=params(58),
        name="last",
        cost_estimate=cost(9),
    )


def spread_kernel(lengths_ref, index_ref, base_hbm, *refs, deltas, pieces):
    deltas_hbm, out_hbm, base, out = refs[:deltas], refs[deltas], refs[deltas + 1], refs[deltas + 2]
    held, sems = refs[deltas + 3 : -1], refs[-1]
    copies = Copies(sems)
    seqs, _, slots = index_ref.shape
    count = base.shape[1]

    def delta_copy(source, target):
        top = source.shape[0] - 1
        place = lambda row: source.at[top, row] if len(source.shape) == 3 else source.at[row]
        return copies.group(
            seqs, lambda seq: (place(block_of(seq, slots)), target.at[block_of(seq, slots)])
        )

    delta_copies = [delta_copy(*pair) for pair in zip(deltas_hbm, held)]
    base_copy = copies.group(
        seqs * pieces, lambda at: (base_hbm.at[block_of(at, count)], base.at[at])
    )
    for seq in range(seqs):
        for copy in delta_copies:
            copy(seq).start()
        for piece in range(pieces):
            base_copy(seq * pieces + piece).start()
    out_copy = copies.send_group(
        seqs * pieces, lambda at: (out.at[at], out_hbm.at[block_of(at, count)])
    )

    def one(seq):
        rows = block_of(seq, slots)
        for copy in delta_copies:
            copy(seq).wait()
        if deltas == 1:
            delta = held[0][rows]
        else:
            score, attn, own, other = held
            delta = score[rows, :1] * (attn[rows] + add_low(own[rows], other[rows]).astype(f32))
        high = delta.astype(bf16)
        low = (delta - high.astype(f32)).astype(bf16)
        both = jnp.concatenate([high, low], axis=0)
        slot_id = lax.broadcasted_iota(jnp.int32, (count, slots), 1)
        live = slot_id < lax.div(lengths_ref[0, seq], 8)
        for piece in range(pieces):
            place = piece * count + lax.broadcasted_iota(jnp.int32, (count, slots), 0)
            pick = ((index_ref[seq] == place) & live).astype(bf16)
            at = seq * pieces + piece
            base_copy(at).wait()
            added = dot_nn(jnp.concatenate([pick, pick], axis=1), both)
            out[at] = (base[at].astype(f32) + added).astype(out.dtype)
            out_copy(at).start()

    repeat(seqs, one)
    copies.finish()


def spread(lengths, index, base, deltas, dtype, waits=(), pieces=2):
    seqs, slots = index.shape
    rows, width = base.shape
    steps = seqs * pieces
    index = index[:, None, :]
    held = [pltpu.VMEM(delta.shape[-2:], delta.dtype) for delta in deltas]
    return call(
        functools.partial(spread_kernel, deltas=len(deltas), pieces=pieces),
        [index, base, *deltas],
        waits,
        [lengths],
        grid=(1,),
        in_specs=[whole(index)] + [HBM] * (1 + len(deltas)),
        out_specs=HBM,
        scratch_shapes=[
            pltpu.VMEM((steps, rows // steps, width), bf16),
            pltpu.VMEM((steps, rows // steps, width), dtype),
            *held,
            pltpu.SemaphoreType.DMA((2 * steps + len(deltas) * seqs,)),
        ],
        out_shape=jax.ShapeDtypeStruct((rows, width), dtype),
        compiler_params=params(58),
        name="spread",
        cost_estimate=cost(8),
    )


def add_low(left, right):
    return (left.astype(f32) + right.astype(f32)).astype(bf16)


def swap_nodes(values, bit, nodes):
    return lax.ppermute(values, "seq", [(i, i ^ (1 << bit)) for i in range(nodes)])


def swap_cores(values):
    return lax.ppermute(values, "dp", [(0, 1), (1, 0)])


class Part:
    def __init__(self, order, nodes):
        self.order, self.nodes = order, nodes

    @classmethod
    def halved(cls, gone, kept, order, nodes):
        part = cls(order, nodes)
        part.gone, part.kept = gone, kept
        part.swap()
        return part

    @classmethod
    def of_cores(cls, send, keep, order, nodes):
        part = cls(order, nodes)
        part.kept, part.got = keep, swap_cores(send)
        return part

    @classmethod
    def of_split_cores(cls, send_gone, send_stay, keep_gone, keep_stay, order, nodes):
        part = cls(order, nodes)
        part.halves = (keep_gone, swap_cores(send_gone)), (keep_stay, swap_cores(send_stay))
        return part

    halves = None

    def swap(self):
        self.got = swap_nodes(self.gone, self.order[0], self.nodes)
        self.order = self.order[1:]

    def halve(self, after=()):
        if self.halves:
            (keep_gone, got_gone), (keep_stay, got_stay), *_ = lax.optimization_barrier(
                (*self.halves, *after)
            )
            self.gone, self.kept = add_low(keep_gone, got_gone), add_low(keep_stay, got_stay)
            self.halves = None
            return
        if after:
            self.kept, self.got, *_ = lax.optimization_barrier((self.kept, self.got, *after))
        if self.kept.shape[0] == 1:
            self.kept, self.got = self.kept[0], self.got[0]
        count = self.kept.shape[0] // 2
        halves = [add_low(self.kept[c], self.got[c]) for c in (slice(count, None), slice(count))]
        self.gone, self.kept = [half[0] for half in halves] if count == 1 else halves

    def step(self, after=()):
        self.halve(after)
        self.swap()
        return self.gone


class Chain:
    def __init__(self, parts):
        self.parts = parts

    def step(self, count=1, after=()):
        sent = []
        for _ in range(count):
            sent = []
            for part in self.parts:
                sent.append(part.step([*after, *sent]))
        return sent

    def final(self, after=()):
        for part in self.parts:
            part.halve(after)
        gone = jnp.concatenate([part.gone for part in self.parts], axis=-1)
        self.got = swap_nodes(gone, self.parts[0].order[0], self.parts[0].nodes)
        return [gone]

    def sum(self):
        kept = jnp.concatenate([part.kept for part in self.parts], axis=-1)
        return kept.astype(f32) + self.got.astype(f32)


def both_cores(core, rows, nodes):
    count = rows.shape[0] // 2
    mine, sent = [
        lax.dynamic_slice_in_dim(rows, side * count, count) for side in (core, 1 - core)
    ]
    got = swap_cores(sent)
    shape = (count, nodes, 1, rows.shape[1] // nodes)
    sides = [jnp.where(core == side, mine, got).reshape(shape) for side in (0, 1)]
    return jnp.concatenate(sides, axis=2).reshape(count, -1)


def on_device(
    tokens,
    lengths,
    routed_index,
    out_grad,
    gain_attn,
    w_router,
    w_query,
    w_key,
    w_value,
    w_out,
    gain_mlp,
    w_up,
    w_down,
):
    nodes = lax.axis_size("seq")
    width = tokens.shape[2]
    me = jnp.stack([lax.axis_index("dp"), lax.axis_index("seq")]).astype(jnp.int32)
    index = routed_index[0]
    inputs, cotangent = tokens[0], out_grad[0]
    vectors = [vector.reshape(-1, 128) for vector in (gain_attn, w_router, gain_mlp)]
    (
        chosen, lefts, queries, keys, values, probs, attn_out, feed_own, pulled, score,
    ) = front(
        lengths, index, inputs, cotangent, vectors, w_query, w_key, w_value, w_out
    )
    feed_other = swap_cores(feed_own)
    order = lambda names: link_order(nodes, names)
    span = len(order("x"))
    down_order, up_order = order("nxfy"), order("xynf")
    square_orders = [order("nxyf"), order("yxnf")]
    own_sums, other_sums, *terms = feed(
        me, feed_own, feed_other, w_up, w_down, nodes, [down_order, up_order]
    )
    got_sums = swap_cores(other_sums)
    down = Chain([Part.halved(*terms[:2], down_order, nodes)])
    up = Chain([Part.halved(*terms[2:], up_order, nodes)])
    grads, after_grad, gain_mlp_sum, *square_terms = back(
        me, chosen, attn_out, score, pulled, own_sums, got_sums, vectors[2], queries, keys, values, probs,
        lefts, w_out, nodes, square_orders, width // 2,
    )
    square = Chain(
        [
            Part.of_split_cores(*square_terms[:4], square_orders[0], nodes),
            Part.of_cores(*square_terms[4:], square_orders[1], nodes),
        ]
    )
    mixed_out = spread(
        lengths, index, inputs, [score, attn_out, own_sums, got_sums], bf16, waits=square_terms[:1]
    )
    chosen_grad, gain_attn_sum, router_sum = last(
        chosen, attn_out, own_sums, got_sums, score, pulled, after_grad, grads,
        vectors[0], vectors[1], w_query, w_key, w_value, waits=[mixed_out],
    )
    sums = jnp.sum(jnp.stack([gain_attn_sum, router_sum, gain_mlp_sum]), axis=1)
    sums = sums.reshape(3, 2 * nodes, -1).transpose(1, 0, 2)
    gone = down.step(span, after=[chosen_grad])
    gone += up.step(span, after=gone)
    gone += square.step(after=gone)
    token_grad = spread(lengths, index, cotangent, [chosen_grad], f32, waits=gone)
    gone = down.step(span, after=[token_grad])
    gone = up.step(span, after=gone)
    gone = square.step(span, after=gone)
    gone = down.final(after=gone)
    gone = up.final(after=gone)
    gone = square.step(span, after=gone)
    down_sum, _ = lax.optimization_barrier((both_cores(me[0], down.sum(), nodes), gone[0]))
    gone = square.final(after=[up.sum()])
    sums, *_ = lax.optimization_barrier((sums, *gone))
    sums = jnp.sum(lax.all_to_all(sums, ("seq", "dp"), 0, 0, tiled=True), axis=0)
    square_sum = square.sum()
    return (
        mixed_out[None],
        token_grad[None],
        sums[0],
        sums[1],
        *[square_sum[which].T for which in range(4)],
        sums[2],
        up.sum().T,
        down_sum.T,
    )


def solution(mesh):
    in_specs = (
        P("dp", "seq", None),
        P("dp", "seq"),
        P("dp", "seq", None),
        P("dp", "seq", None),
        P(),
        P(),
        P(),
        P(),
        P(),
        P(),
        P(),
        P(),
        P(),
    )
    out_specs = (
        P("dp", "seq", None),
        P("dp", "seq", None),
        P(("seq", "dp")),
        P(("seq", "dp")),
        P(None, ("seq", "dp")),
        P(None, ("seq", "dp")),
        P(None, ("seq", "dp")),
        P(None, ("seq", "dp")),
        P(("seq", "dp")),
        P(None, ("seq", "dp")),
        P(None, ("seq", "dp")),
    )
    return jax.shard_map(
        on_device, mesh=mesh, in_specs=in_specs, out_specs=out_specs, check_vma=False
    )
```

```python
import functools

import jax
import jax.experimental.pallas as pl
import jax.experimental.pallas.tpu as pltpu
import jax.numpy as jnp
from jax import lax
from jax.sharding import PartitionSpec as P

H = 16
norm_eps = 1e-05
f32 = jnp.float32
bf16 = jnp.bfloat16


def params(mebibytes):
    return pltpu.CompilerParams(
        dimension_semantics=("arbitrary",), vmem_limit_bytes=mebibytes * 1024 * 1024
    )


def cost(micros):
    return pl.CostEstimate(
        flops=int(micros * 1e8), bytes_accessed=int(micros * 3.5e5), transcendentals=0
    )


def call(kernel, arrays, waits=(), scalars=(), **rest):
    first = len(scalars) + len(arrays)

    def body(*refs):
        kernel(*refs[:first], *refs[first + len(waits) :])

    grid = pltpu.PrefetchScalarGridSpec(
        num_scalar_prefetch=len(scalars),
        grid=rest.pop("grid"),
        in_specs=list(rest.pop("in_specs")) + [pl.BlockSpec(memory_space=pl.ANY)] * len(waits),
        out_specs=rest.pop("out_specs"),
        scratch_shapes=rest.pop("scratch_shapes", ()),
    )
    return pl.pallas_call(body, grid_spec=grid, **rest)(*scalars, *arrays, *waits)


def whole(array):
    rank = len(array.shape)
    return pl.BlockSpec(array.shape, lambda *_: (0,) * rank, pipeline_mode=pl.Buffered(1))


def dot_nn(left, right):
    return lax.dot_general(left, right, (((1,), (0,)), ((), ())), preferred_element_type=f32)


def dot_nt(left, right):
    return lax.dot_general(left, right, (((1,), (1,)), ((), ())), preferred_element_type=f32)


def dot_tn(left, right):
    return lax.dot_general(left, right, (((0,), (0,)), ((), ())), preferred_element_type=f32)


def inv_rms(values):
    return lax.rsqrt(jnp.mean(values * values, axis=-1, keepdims=True) + norm_eps)


GROUP = 4


def flat_row(ref):
    values = ref[...].astype(f32)
    return jnp.concatenate([values[i : i + 1] for i in range(values.shape[0])], axis=1)


def fold(values):
    rows, width = values.shape
    return jnp.sum(values.reshape(rows // 8, 8, width), axis=0)


class Copies:
    def __init__(self, sems):
        self.sems, self.count, self.sent = sems, 0, []

    def one(self, source, target):
        self.count += 1
        return pltpu.make_async_copy(source, target, self.sems.at[self.count - 1])

    def group(self, turns, pair):
        first = self.count
        self.count += turns

        def at(turn):
            source, target = pair(turn)
            return pltpu.make_async_copy(source, target, self.sems.at[first + turn])

        return at

    def start(self, source, target):
        copy = self.one(source, target)
        copy.start()
        return copy

    def send(self, source, target):
        self.sent.append(self.start(source, target))

    def send_group(self, turns, pair):
        at = self.group(turns, pair)
        self.sent += [at(turn) for turn in range(turns)]
        return at

    def finish(self):
        for copy in self.sent:
            copy.wait()


def repeat(turns, body, unroll=1):
    lax.fori_loop(0, turns, lambda turn, carry: body(turn), None, unroll=unroll)


def block_of(turn, size):
    return pl.ds(pl.multiple_of(turn * size, size), size)


HBM = pl.BlockSpec(memory_space=pl.ANY)


def stacked(rows, head):
    lane_head = lax.broadcasted_iota(jnp.int32, rows.shape, 1) // head
    zero = jnp.zeros_like(rows)
    return jnp.concatenate([jnp.where(lane_head == h, rows, zero) for h in range(GROUP)], axis=0)


def unstacked(rows, head):
    slots = rows.shape[0] // GROUP
    lane_head = lax.broadcasted_iota(jnp.int32, (slots, rows.shape[1]), 1) // head
    out = rows[:slots]
    for h in range(1, GROUP):
        out = jnp.where(lane_head == h, rows[h * slots : (h + 1) * slots], out)
    return out


def front_kernel(
    lengths_ref, index_ref, gain_one_ref, router_ref, gain_two_ref,
    tokens_hbm, cotangent_hbm, query_hbm, key_hbm, value_hbm, out_hbm,
    chosen_out, lefts_out, queries_out, keys_out, values_out, probs_out, attn_out, feed_out, pulled_out,
    score_out,
    tokens, cotangent, query_w, key_w, value_w, out_w,
    chosen, lefts, queries, keys, values, probs, attn, feed, pulled, score, sems,
):
    copies = Copies(sems)
    seqs, _, slots = index_ref.shape
    places, width = tokens.shape[1], tokens.shape[2]
    head = width // H
    token_copy = copies.group(
        seqs, lambda seq: (tokens_hbm.at[block_of(seq, places)], tokens.at[seq])
    )
    cotangent_copy = copies.group(
        seqs, lambda seq: (cotangent_hbm.at[block_of(seq, places)], cotangent.at[seq])
    )
    for seq in range(seqs):
        token_copy(seq).start()
        cotangent_copy(seq).start()
    weights = [
        copies.start(*pair)
        for pair in (
            (query_hbm, query_w), (key_hbm, key_w), (value_hbm, value_w), (out_hbm, out_w),
        )
    ]
    gain_one, router, gain_two = [flat_row(r) for r in (gain_one_ref, router_ref, gain_two_ref)]

    def gather(seq):
        rows = block_of(seq, slots)
        slot_id = lax.broadcasted_iota(jnp.int32, (slots, places), 0)
        place_id = lax.broadcasted_iota(jnp.int32, (slots, places), 1)
        square = (slots, slots)
        diagonal = lax.broadcasted_iota(jnp.int32, square, 0) == lax.broadcasted_iota(
            jnp.int32, square, 1
        )
        routed = lax.div(lengths_ref[0, seq], 8)
        index = jnp.sum(jnp.where(diagonal, index_ref[seq], 0), axis=1, keepdims=True)
        pick = ((index == place_id) & (slot_id < routed)).astype(bf16)
        token_copy(seq).wait()
        wide = dot_nn(pick, tokens[seq])
        chosen[rows] = wide.astype(bf16)
        logit = jnp.sum(wide * router, axis=-1, keepdims=True)
        chance = 1.0 / (1.0 + jnp.exp(-logit))
        score[rows] = jnp.broadcast_to(chance, (slots, score.shape[1]))
        lefts[0, rows] = (wide * inv_rms(wide) * gain_one).astype(bf16)
        cotangent_copy(seq).wait()
        pull = dot_nn(pick, cotangent[seq])
        pulled[rows] = pull.astype(bf16)
        feed[1, rows] = (chance * pull).astype(bf16)

    repeat(seqs, gather, 2)
    copies.send(chosen, chosen_out)
    copies.send(pulled, pulled_out)
    copies.send(score, score_out)
    copies.send(feed.at[1], feed_out.at[1])
    copies.send(lefts.at[0], lefts_out.at[0])
    first = lefts[0]
    weights[0].wait()
    queries[...] = (dot_nn(first, query_w[...]) * 0.125).astype(bf16)
    copies.send(queries, queries_out)
    weights[1].wait()
    keys[...] = dot_nn(first, key_w[...]).astype(bf16)
    copies.send(keys, keys_out)
    weights[2].wait()
    values[...] = dot_nn(first, value_w[...]).astype(bf16)
    copies.send(values, values_out)
    probs_copy = copies.send_group(seqs, lambda seq: (probs.at[seq], probs_out.at[seq]))

    def attend(seq):
        rows = block_of(seq, slots)
        stack = GROUP * slots
        row_id = lax.broadcasted_iota(jnp.int32, (stack, slots), 0) % slots
        col_id = lax.broadcasted_iota(jnp.int32, (stack, slots), 1)
        allowed = (col_id <= row_id) & (col_id < lax.div(lengths_ref[0, seq], 8))
        for g in range(H // GROUP):
            lanes = slice(g * GROUP * head, (g + 1) * GROUP * head)
            scores = dot_nt(stacked(queries[rows, lanes], head), keys[rows, lanes])
            scores = jnp.where(allowed, scores, -1e30)
            exped = jnp.exp(scores - jnp.max(scores, axis=-1, keepdims=True))
            chances = (exped / jnp.sum(exped, axis=-1, keepdims=True)).astype(bf16)
            probs[seq, g] = chances
            mixed = dot_nn(chances, values[rows, lanes])
            lefts[1, rows, lanes] = unstacked(mixed, head).astype(bf16)
        probs_copy(seq).start()

    repeat(seqs, attend, 2)
    copies.send(lefts.at[1], lefts_out.at[1])
    weights[3].wait()
    attn[...] = dot_nn(lefts[1], out_w[...])
    copies.send(attn, attn_out)

    feed_copy = copies.send_group(
        seqs, lambda seq: (feed.at[0, block_of(seq, slots)], feed_out.at[0, block_of(seq, slots)])
    )

    def after_attention(seq):
        rows = block_of(seq, slots)
        after = chosen[rows].astype(f32) + attn[rows]
        feed[0, rows] = (after * inv_rms(after) * gain_two).astype(bf16)
        feed_copy(seq).start()

    repeat(seqs, after_attention)
    copies.finish()


def front(lengths, index, tokens, cotangent, vectors, wq, wk, wv, wo):
    seqs, slots = index.shape
    places, width = tokens.shape[0] // seqs, tokens.shape[1]
    rows = seqs * slots
    low = ((rows, width), bf16)
    outs = [
        low, ((2, rows, width), bf16), low, low, low,
        ((seqs, H // GROUP, GROUP * slots, slots), bf16), ((rows, width), f32),
        ((2, rows, width), bf16), low, ((rows, 128), f32),
    ]
    small = [index[:, None, :], *vectors]
    return call(
        front_kernel,
        [*small, tokens, cotangent, wq, wk, wv, wo],
        (),
        [lengths],
        grid=(1,),
        in_specs=[whole(array) for array in small] + [HBM] * 6,
        out_specs=[HBM] * len(outs),
        scratch_shapes=[pltpu.VMEM((seqs, places, width), bf16)] * 2
        + [pltpu.VMEM((width, width), bf16)] * 4
        + [pltpu.VMEM(*out) for out in outs]
        + [pltpu.SemaphoreType.DMA((2 * seqs + 4 + 10 + 2 * seqs,))],
        out_shape=[jax.ShapeDtypeStruct(*out) for out in outs],
        compiler_params=params(58),
        name="front",
        cost_estimate=cost(18),
    )


def gelu_both(z):
    cdf = 0.5 + 0.5 * lax.erf(z * 0.7071067811865476)
    return z * cdf, cdf + z * (jnp.exp(-0.5 * z * z) * 0.3989422804014327)


def link_bits(nodes):
    bits = nodes.bit_length() - 1
    half = (bits - 2) // 2
    return list(range(half)), list(range(half, bits - 2)), [bits - 2], [bits - 1]


def link_order(nodes, names):
    x, y, near, far = link_bits(nodes)
    return sum([{"x": x, "y": y, "n": near, "f": far}[name] for name in names], [])


def spot_of(rel, order):
    return sum(((rel >> bit) & 1) << (len(order) - 1 - i) for i, bit in enumerate(order))


def own_blocks(me_ref, source, size, nodes):
    core, node = me_ref[0], me_ref[1]
    for rel in range(nodes):
        owner = lax.bitwise_xor(node, rel) * 2
        starts = [pl.multiple_of((owner + side) * size, size) for side in (core, 1 - core)]
        yield rel, *[source[pl.ds(start, size), :].astype(bf16) for start in starts]


def held_type(size):
    return bf16 if size % 16 == 0 else f32


def feed_kernel(me_ref, own_ref, other_ref, *refs, nodes, pieces, orders):
    ups, downs, refs = refs[:pieces], refs[pieces : 2 * pieces], refs[2 * pieces :]
    (
        sums_ref, sent_ref, down_gone, down_kept, up_gone, up_kept,
        rows_ref, grads_ref, turned_ref, down_terms, up_terms, grad_sum, out_sum,
    ) = refs
    step, steps = pl.program_id(0), pl.num_programs(0)
    node = me_ref[1]
    flat = nodes // 4
    count = own_ref.shape[1]

    @pl.when(step == 0)
    def _():
        rows_ref[:count] = own_ref[0]
        rows_ref[count:] = other_ref[0]
        grads_ref[:count] = own_ref[1]
        grads_ref[count:] = other_ref[1]
        turned_ref[...] = grads_ref[...].T
        out_sum[...] = jnp.zeros_like(out_sum)
        grad_sum[...] = jnp.zeros_like(grad_sum)

    w_up = jnp.concatenate([ref[...] for ref in ups], axis=1)
    w_down = jnp.concatenate([ref[...] for ref in downs], axis=0)
    hidden = dot_nn(rows_ref[...], w_up)
    act, slope = gelu_both(hidden)
    act = act.astype(bf16)
    pre = (dot_nt(grads_ref[...], w_down) * slope).astype(bf16)

    down_terms[...] = dot_nn(turned_ref[...], act).astype(down_terms.dtype)
    size = down_terms.shape[0] // nodes
    for rel in range(nodes):
        spot = spot_of(rel, orders[0])
        start = pl.multiple_of(lax.bitwise_xor(node, rel) * size, size)
        values = down_terms[pl.ds(start, size), :].astype(bf16)
        (down_kept, down_gone)[spot // (nodes // 2)][spot % (nodes // 2)] = values

    up_terms[...] = dot_tn(pre, rows_ref[...]).astype(up_terms.dtype)
    size = up_kept.shape[2]
    for rel in range(flat):
        spot = spot_of(rel, orders[1][:-2])
        start = pl.multiple_of(lax.bitwise_xor(lax.rem(node, flat), rel) * size, size)
        values = up_terms[pl.ds(start, size), :].astype(bf16)
        (up_kept, up_gone)[spot // (flat // 2)][spot % (flat // 2), 0] = values

    out_sum[...] += dot_nn(act, w_down)
    grad_sum[...] += dot_nt(pre, w_up)

    @pl.when(step == steps - 1)
    def _():
        for i, total in enumerate((grad_sum, out_sum)):
            sums_ref[i] = total[:count].astype(bf16)
            sent_ref[i] = total[count:].astype(bf16)


def feed(me, own, other, w_up, w_down, nodes, orders, steps=4, waits=()):
    _, rows, width = own.shape
    hidden = w_up.shape[1]
    flat = nodes // 4
    size = hidden // (2 * nodes)
    block = hidden // 2 // steps
    if size % 128:
        w_up = lax.dynamic_index_in_dim(w_up.reshape(width, nodes, 2, size), me[0], 2, False)
        w_down = lax.dynamic_index_in_dim(w_down.reshape(nodes, 2, size, width), me[0], 1, False)
        w_up, w_down = w_up.reshape(width, -1), w_down.reshape(-1, width)
        pieces = 1
        place = lambda piece, i, me: i
    else:
        pieces = block // size
        place = lambda piece, i, me: (i * pieces + piece) * 2 + me[0]
    columns = block // pieces
    up_specs = [
        pl.BlockSpec((width, columns), lambda i, me, p=p: (0, place(p, i, me)))
        for p in range(pieces)
    ]
    down_specs = [
        pl.BlockSpec((columns, width), lambda i, me, p=p: (place(p, i, me), 0))
        for p in range(pieces)
    ]
    chunk = width // nodes
    down_spec = pl.BlockSpec((nodes // 2, chunk, block), lambda i, me: (0, 0, i))
    near_first = orders[1][-2] < orders[1][-1]

    def up_place(i, me):
        rel = lax.bitwise_xor(i, lax.div(me[1], flat))
        return (0, lax.rem(rel, 2) * 2 + lax.div(rel, 2) if near_first else rel, 0, 0)

    up_spec = pl.BlockSpec((flat // 2, 1, size, width), up_place)
    pair = jax.ShapeDtypeStruct((2, rows, width), bf16)
    return call(
        functools.partial(feed_kernel, nodes=nodes, pieces=pieces, orders=orders),
        [own, other] + [w_up] * pieces + [w_down] * pieces,
        waits,
        [me],
        grid=(steps,),
        in_specs=[whole(own), whole(other)] + up_specs + down_specs,
        out_specs=[pl.BlockSpec((2, rows, width), lambda i, me: (0, 0, 0))] * 2
        + [down_spec, down_spec, up_spec, up_spec],
        scratch_shapes=[
            pltpu.VMEM((2 * rows, width), bf16),
            pltpu.VMEM((2 * rows, width), bf16),
            pltpu.VMEM((width, 2 * rows), bf16),
            pltpu.VMEM((width, block), held_type(chunk)),
            pltpu.VMEM((block, width), held_type(size)),
            pltpu.VMEM((2 * rows, width), f32),
            pltpu.VMEM((2 * rows, width), f32),
        ],
        out_shape=[pair] * 2
        + [jax.ShapeDtypeStruct((nodes // 2, chunk, hidden // 2), bf16)] * 2
        + [jax.ShapeDtypeStruct((flat // 2, 4, size, width), bf16)] * 2,
        compiler_params=params(62),
        name="feed",
        cost_estimate=cost(34),
    )


def back_kernel(
    me_ref, gain_ref, chosen_hbm, attn_hbm, score_hbm, pulled_hbm, own_hbm, other_hbm, queries_hbm,
    keys_hbm, values_hbm, probs_hbm, lefts_hbm, out_hbm,
    grads_out, after_out, gain_out, send_gone_out, send_stay_out, keep_gone_out, keep_stay_out,
    send_b_out, keep_b_out,
    chosen, attn, score, pulled, own, other, queries, keys, values, probs, lefts, out_w,
    grads, after_grad, send_gone, send_stay, keep_gone, keep_stay, send_b, keep_b,
    mix_grad, terms, sems,
    *, nodes, orders,
):
    copies = Copies(sems)
    fetched = {}
    for name, source, target in (
        ("rows", chosen_hbm, chosen), ("rows", attn_hbm, attn), ("rows", own_hbm.at[0], own),
        ("rows", other_hbm.at[0], other), ("rows", score_hbm, score), ("rows", pulled_hbm, pulled),
        ("out", out_hbm, out_w), ("heads", queries_hbm, queries), ("heads", keys_hbm, keys),
        ("heads", values_hbm, values), ("heads", probs_hbm, probs), ("lefts", lefts_hbm, lefts),
    ):
        fetched.setdefault(name, []).append(copies.start(source, target))

    def arrive(name):
        for copy in fetched[name]:
            copy.wait()

    seqs, groups, stack, slots = probs.shape
    width = chosen.shape[1]
    head = width // H
    gain = flat_row(gain_ref)
    gain_out[...] = jnp.zeros_like(gain_out)
    arrive("rows")

    def norm_grad(seq):
        rows = block_of(seq, slots)
        after = chosen[rows].astype(f32) + attn[rows]
        inv = inv_rms(after)
        normed = after * inv
        arrived = add_low(own[rows], other[rows]).astype(f32)
        gain_out[...] += fold(arrived * normed)
        weighted = arrived * gain
        back = inv * (weighted - normed * jnp.mean(weighted * normed, axis=-1, keepdims=True))
        after_grad[rows] = back
        delta = score[rows, :1] * pulled[rows].astype(f32)
        grads[3, rows] = (delta + back).astype(bf16)

    repeat(seqs, norm_grad)
    copies.send(after_grad, after_out)
    arrive("out")
    mix_grad[...] = dot_nt(grads[3], out_w[...]).astype(bf16)
    arrive("heads")

    def attention_grad(seq):
        rows = block_of(seq, slots)
        for g in range(groups):
            lanes = slice(g * GROUP * head, (g + 1) * GROUP * head)
            chances = probs[seq, g]
            wide = chances.astype(f32)
            stacked_queries = stacked(queries[rows, lanes], head)
            stacked_grads = stacked(mix_grad[rows, lanes], head)
            prob_grad = dot_nt(stacked_grads, values[rows, lanes])
            total = jnp.sum(prob_grad * wide, axis=-1, keepdims=True)
            score_grad = (wide * (prob_grad - total)).astype(bf16)
            grads[2, rows, lanes] = dot_tn(chances, stacked_grads).astype(bf16)
            grads[1, rows, lanes] = dot_tn(score_grad, stacked_queries).astype(bf16)
            grads[0, rows, lanes] = unstacked(dot_nn(score_grad, keys[rows, lanes]), head).astype(bf16)

    repeat(seqs, attention_grad, 2)
    copies.send(grads.at[pl.ds(0, 3)], grads_out)
    arrive("lefts")
    half, cut = nodes // 2, send_gone.shape[3]
    outs = [
        copies.send_group(4, lambda i, held=held, out=out: (held.at[:, i], out.at[:, i]))
        for held, out in (
            (send_gone, send_gone_out), (keep_gone, keep_gone_out), (send_stay, send_stay_out),
            (keep_stay, keep_stay_out), (send_b, send_b_out), (keep_b, keep_b_out),
        )
    ]

    def weight_grad(which):
        product = dot_tn(grads[which], lefts[lax.div(which, 3)])
        terms[...] = (product * jnp.where(which == 0, 0.125, 1.0)).astype(terms.dtype)
        for rel, kept, sent in own_blocks(me_ref, terms, send_b.shape[2], nodes):
            spot = spot_of(rel, orders[0])
            (keep_stay, keep_gone)[spot // half][spot % half, which] = kept[:, :cut]
            (send_stay, send_gone)[spot // half][spot % half, which] = sent[:, :cut]
            spot = spot_of(rel, orders[1])
            keep_b[spot, which] = kept[:, cut:]
            send_b[spot, which] = sent[:, cut:]
        for out in outs:
            out(which).start()

    repeat(4, weight_grad)
    copies.finish()


def back(
    me, chosen, attn, score, pulled, own, other, gain, queries, keys, values, probs, lefts, w_out, nodes,
    orders, cut,
):
    rows, width = chosen.shape
    seqs, _, _, slots = probs.shape
    size = width // (2 * nodes)
    layout = [(nodes // 2, cut)] * 4 + [(nodes, width - cut)] * 2
    shapes = [((count, 4, size, columns), bf16) for count, columns in layout]
    outs = [((3, rows, width), bf16), ((rows, width), f32)]
    fetched = [chosen, attn, score, pulled, own, other, queries, keys, values, probs, lefts, w_out]
    held = [pltpu.VMEM(array.shape, array.dtype) for array in fetched]
    held[4] = held[5] = pltpu.VMEM((rows, width), bf16)
    return call(
        functools.partial(back_kernel, nodes=nodes, orders=orders),
        [gain, *fetched],
        (),
        [me],
        grid=(1,),
        in_specs=[whole(gain)] + [HBM] * len(fetched),
        out_specs=[HBM, HBM, pl.BlockSpec((8, width), lambda *_: (0, 0))] + [HBM] * 6,
        scratch_shapes=held
        + [pltpu.VMEM(*out) for out in [((4, rows, width), bf16), outs[1]] + shapes]
        + [pltpu.VMEM((rows, width), bf16)]
        + [pltpu.VMEM((width, width), held_type(size))]
        + [pltpu.SemaphoreType.DMA((len(fetched) + 2 + 24,))],
        out_shape=[jax.ShapeDtypeStruct(*out) for out in outs]
        + [jax.ShapeDtypeStruct((8, width), f32)]
        + [jax.ShapeDtypeStruct(*shape) for shape in shapes],
        compiler_params=params(62),
        name="back",
        cost_estimate=cost(20),
    )


def last_kernel(
    gain_ref, router_ref, chosen_hbm, attn_hbm, own_hbm, other_hbm, score_hbm, pulled_hbm, after_hbm,
    grads_hbm, query_hbm, key_hbm, value_hbm,
    chosen_grad_out, gain_out, router_out,
    chosen, attn, own, other, score, pulled, after_grad, grads, weights, first_grad, chosen_grad, sems,
):
    copies = Copies(sems)
    pairs = [
        (copies.start(grads_hbm.at[i], grads.at[i]), copies.start(weight, weights.at[i]))
        for i, weight in enumerate((query_hbm, key_hbm, value_hbm))
    ]
    others = [
        copies.start(*pair)
        for pair in (
            (chosen_hbm, chosen), (attn_hbm, attn), (own_hbm.at[1], own), (other_hbm.at[1], other),
            (score_hbm, score), (pulled_hbm, pulled), (after_hbm, after_grad),
        )
    ]
    gain, router = flat_row(gain_ref), flat_row(router_ref)
    gain_out[...] = jnp.zeros_like(gain_out)
    router_out[...] = jnp.zeros_like(router_out)
    for i, pair in enumerate(pairs):
        for copy in pair:
            copy.wait()
        product = dot_nt(grads[i], weights[i])
        if i == 0:
            first_grad[...] = product * 0.125
        else:
            first_grad[...] += product
    for copy in others:
        copy.wait()
    turns = 4
    block = chosen.shape[0] // turns
    out = copies.send_group(
        turns,
        lambda i: (chosen_grad.at[block_of(i, block)], chosen_grad_out.at[block_of(i, block)]),
    )

    def rest(i):
        part = block_of(i, block)
        wide = chosen[part].astype(f32)
        chance = score[part, :1]
        branch = attn[part] + add_low(own[part], other[part]).astype(f32)
        pull = jnp.sum(pulled[part].astype(f32) * branch, axis=-1, keepdims=True)
        logit_grad = pull * chance * (1.0 - chance)
        arrived = first_grad[part]
        inv = inv_rms(wide)
        normed = wide * inv
        weighted = arrived * gain
        chosen_grad[part] = (
            inv * (weighted - normed * jnp.mean(weighted * normed, axis=-1, keepdims=True))
            + after_grad[part]
            + logit_grad * router
        )
        out(i).start()
        gain_out[...] += fold(arrived * normed)
        router_out[...] += fold(logit_grad * wide)

    repeat(turns, rest)
    copies.finish()


def last(
    chosen, attn, own, other, score, pulled, after_grad, grads, gain, router, wq, wk, wv, waits=()
):
    rows, width = chosen.shape
    fetched = [chosen, attn, own, other, score, pulled, after_grad, grads, wq, wk, wv]
    held = [pltpu.VMEM(array.shape, array.dtype) for array in fetched[:-3]]
    held[2] = held[3] = pltpu.VMEM((rows, width), bf16)
    held.append(pltpu.VMEM((3, width, width), bf16))
    sums = pl.BlockSpec((8, width), lambda *_: (0, 0))
    return call(
        last_kernel,
        [gain, router, *fetched],
        waits,
        grid=(1,),
        in_specs=[whole(gain), whole(router)] + [HBM] * len(fetched),
        out_specs=[HBM, sums, sums],
        scratch_shapes=held
        + [pltpu.VMEM((rows, width), f32)] * 2
        + [pltpu.SemaphoreType.DMA((17,))],
        out_shape=[jax.ShapeDtypeStruct((rows, width), f32)]
        + [jax.ShapeDtypeStruct((8, width), f32)] * 2,
        compiler_params=params(58),
        name="last",
        cost_estimate=cost(9),
    )


def spread_kernel(lengths_ref, index_ref, base_hbm, *refs, deltas, pieces):
    deltas_hbm, out_hbm, base, out = refs[:deltas], refs[deltas], refs[deltas + 1], refs[deltas + 2]
    held, sems = refs[deltas + 3 : -1], refs[-1]
    copies = Copies(sems)
    seqs, _, slots = index_ref.shape
    count = base.shape[1]

    def delta_copy(source, target):
        top = source.shape[0] - 1
        place = lambda row: source.at[top, row] if len(source.shape) == 3 else source.at[row]
        return copies.group(
            seqs, lambda seq: (place(block_of(seq, slots)), target.at[block_of(seq, slots)])
        )

    delta_copies = [delta_copy(*pair) for pair in zip(deltas_hbm, held)]
    base_copy = copies.group(
        seqs * pieces, lambda at: (base_hbm.at[block_of(at, count)], base.at[at])
    )
    for seq in range(seqs):
        for copy in delta_copies:
            copy(seq).start()
        for piece in range(pieces):
            base_copy(seq * pieces + piece).start()
    out_copy = copies.send_group(
        seqs * pieces, lambda at: (out.at[at], out_hbm.at[block_of(at, count)])
    )

    def one(seq):
        rows = block_of(seq, slots)
        for copy in delta_copies:
            copy(seq).wait()
        if deltas == 1:
            delta = held[0][rows]
        else:
            score, attn, own, other = held
            delta = score[rows, :1] * (attn[rows] + add_low(own[rows], other[rows]).astype(f32))
        high = delta.astype(bf16)
        low = (delta - high.astype(f32)).astype(bf16)
        both = jnp.concatenate([high, low], axis=0)
        slot_id = lax.broadcasted_iota(jnp.int32, (count, slots), 1)
        live = slot_id < lax.div(lengths_ref[0, seq], 8)
        for piece in range(pieces):
            place = piece * count + lax.broadcasted_iota(jnp.int32, (count, slots), 0)
            pick = ((index_ref[seq] == place) & live).astype(bf16)
            at = seq * pieces + piece
            base_copy(at).wait()
            added = dot_nn(jnp.concatenate([pick, pick], axis=1), both)
            out[at] = (base[at].astype(f32) + added).astype(out.dtype)
            out_copy(at).start()

    repeat(seqs, one)
    copies.finish()


def spread(lengths, index, base, deltas, dtype, waits=(), pieces=2):
    seqs, slots = index.shape
    rows, width = base.shape
    steps = seqs * pieces
    index = index[:, None, :]
    held = [pltpu.VMEM(delta.shape[-2:], delta.dtype) for delta in deltas]
    return call(
        functools.partial(spread_kernel, deltas=len(deltas), pieces=pieces),
        [index, base, *deltas],
        waits,
        [lengths],
        grid=(1,),
        in_specs=[whole(index)] + [HBM] * (1 + len(deltas)),
        out_specs=HBM,
        scratch_shapes=[
            pltpu.VMEM((steps, rows // steps, width), bf16),
            pltpu.VMEM((steps, rows // steps, width), dtype),
            *held,
            pltpu.SemaphoreType.DMA((2 * steps + len(deltas) * seqs,)),
        ],
        out_shape=jax.ShapeDtypeStruct((rows, width), dtype),
        compiler_params=params(58),
        name="spread",
        cost_estimate=cost(8),
    )


def add_low(left, right):
    return (left.astype(f32) + right.astype(f32)).astype(bf16)


def swap_nodes(values, bit, nodes):
    return lax.ppermute(values, "seq", [(i, i ^ (1 << bit)) for i in range(nodes)])


def swap_cores(values):
    return lax.ppermute(values, "dp", [(0, 1), (1, 0)])


class Part:
    def __init__(self, order, nodes):
        self.order, self.nodes = order, nodes

    @classmethod
    def halved(cls, gone, kept, order, nodes):
        part = cls(order, nodes)
        part.gone, part.kept = gone, kept
        part.swap()
        return part

    @classmethod
    def of_cores(cls, send, keep, order, nodes):
        part = cls(order, nodes)
        part.kept, part.got = keep, swap_cores(send)
        return part

    @classmethod
    def of_split_cores(cls, send_gone, send_stay, keep_gone, keep_stay, order, nodes):
        part = cls(order, nodes)
        part.halves = (keep_gone, swap_cores(send_gone)), (keep_stay, swap_cores(send_stay))
        return part

    halves = None

    def swap(self):
        self.got = swap_nodes(self.gone, self.order[0], self.nodes)
        self.order = self.order[1:]

    def halve(self, after=()):
        if self.halves:
            (keep_gone, got_gone), (keep_stay, got_stay), *_ = lax.optimization_barrier(
                (*self.halves, *after)
            )
            self.gone, self.kept = add_low(keep_gone, got_gone), add_low(keep_stay, got_stay)
            self.halves = None
            return
        if after:
            self.kept, self.got, *_ = lax.optimization_barrier((self.kept, self.got, *after))
        if self.kept.shape[0] == 1:
            self.kept, self.got = self.kept[0], self.got[0]
        count = self.kept.shape[0] // 2
        halves = [add_low(self.kept[c], self.got[c]) for c in (slice(count, None), slice(count))]
        self.gone, self.kept = [half[0] for half in halves] if count == 1 else halves

    def step(self, after=()):
        self.halve(after)
        self.swap()
        return self.gone


class Chain:
    def __init__(self, parts):
        self.parts = parts

    def step(self, count=1, after=()):
        sent = []
        for _ in range(count):
            sent = []
            for part in self.parts:
                sent.append(part.step([*after, *sent]))
        return sent

    def final(self, after=()):
        for part in self.parts:
            part.halve(after)
        gone = jnp.concatenate([part.gone for part in self.parts], axis=-1)
        self.got = swap_nodes(gone, self.parts[0].order[0], self.parts[0].nodes)
        return [gone]

    def sum(self):
        kept = jnp.concatenate([part.kept for part in self.parts], axis=-1)
        return kept.astype(f32) + self.got.astype(f32)


def both_cores(core, rows, nodes):
    count = rows.shape[0] // 2
    mine, sent = [
        lax.dynamic_slice_in_dim(rows, side * count, count) for side in (core, 1 - core)
    ]
    got = swap_cores(sent)
    shape = (count, nodes, 1, rows.shape[1] // nodes)
    sides = [jnp.where(core == side, mine, got).reshape(shape) for side in (0, 1)]
    return jnp.concatenate(sides, axis=2).reshape(count, -1)


def on_device(
    tokens,
    lengths,
    routed_index,
    out_grad,
    gain_attn,
    w_router,
    w_query,
    w_key,
    w_value,
    w_out,
    gain_mlp,
    w_up,
    w_down,
):
    nodes = lax.axis_size("seq")
    width = tokens.shape[2]
    me = jnp.stack([lax.axis_index("dp"), lax.axis_index("seq")]).astype(jnp.int32)
    index = routed_index[0]
    inputs, cotangent = tokens[0], out_grad[0]
    vectors = [vector.reshape(-1, 128) for vector in (gain_attn, w_router, gain_mlp)]
    (
        chosen, lefts, queries, keys, values, probs, attn_out, feed_own, pulled, score,
    ) = front(
        lengths, index, inputs, cotangent, vectors, w_query, w_key, w_value, w_out
    )
    feed_other = swap_cores(feed_own)
    order = lambda names: link_order(nodes, names)
    span = len(order("x"))
    down_order, up_order = order("nxfy"), order("xynf")
    square_orders = [order("nxyf"), order("yxnf")]
    own_sums, other_sums, *terms = feed(
        me, feed_own, feed_other, w_up, w_down, nodes, [down_order, up_order]
    )
    got_sums = swap_cores(other_sums)
    down = Chain([Part.halved(*terms[:2], down_order, nodes)])
    up = Chain([Part.halved(*terms[2:], up_order, nodes)])
    grads, after_grad, gain_mlp_sum, *square_terms = back(
        me, chosen, attn_out, score, pulled, own_sums, got_sums, vectors[2], queries, keys, values, probs,
        lefts, w_out, nodes, square_orders, width // 2,
    )
    square = Chain(
        [
            Part.of_split_cores(*square_terms[:4], square_orders[0], nodes),
            Part.of_cores(*square_terms[4:], square_orders[1], nodes),
        ]
    )
    mixed_out = spread(
        lengths, index, inputs, [score, attn_out, own_sums, got_sums], bf16, waits=square_terms[:1]
    )
    chosen_grad, gain_attn_sum, router_sum = last(
        chosen, attn_out, own_sums, got_sums, score, pulled, after_grad, grads,
        vectors[0], vectors[1], w_query, w_key, w_value, waits=[mixed_out],
    )
    sums = jnp.sum(jnp.stack([gain_attn_sum, router_sum, gain_mlp_sum]), axis=1)
    sums = sums.reshape(3, 2 * nodes, -1).transpose(1, 0, 2)
    gone = down.step(span, after=[chosen_grad])
    gone += up.step(span, after=gone)
    gone += square.step(after=gone)
    token_grad = spread(lengths, index, cotangent, [chosen_grad], f32, waits=gone)
    gone = down.step(span, after=[token_grad])
    gone = up.step(span, after=gone)
    gone = square.step(span, after=gone)
    gone = down.final(after=gone)
    gone = up.final(after=gone)
    gone = square.step(span, after=gone)
    down_sum, _ = lax.optimization_barrier((both_cores(me[0], down.sum(), nodes), gone[0]))
    gone = square.final(after=[up.sum()])
    sums, *_ = lax.optimization_barrier((sums, *gone))
    sums = jnp.sum(lax.all_to_all(sums, ("seq", "dp"), 0, 0, tiled=True), axis=0)
    square_sum = square.sum()
    return (
        mixed_out[None],
        token_grad[None],
        sums[0],
        sums[1],
        *[square_sum[which].T for which in range(4)],
        sums[2],
        up.sum().T,
        down_sum.T,
    )


def solution(mesh):
    in_specs = (
        P("dp", "seq", None),
        P("dp", "seq"),
        P("dp", "seq", None),
        P("dp", "seq", None),
        P(),
        P(),
        P(),
        P(),
        P(),
        P(),
        P(),
        P(),
        P(),
    )
    out_specs = (
        P("dp", "seq", None),
        P("dp", "seq", None),
        P(("seq", "dp")),
        P(("seq", "dp")),
        P(None, ("seq", "dp")),
        P(None, ("seq", "dp")),
        P(None, ("seq", "dp")),
        P(None, ("seq", "dp")),
        P(("seq", "dp")),
        P(None, ("seq", "dp")),
        P(None, ("seq", "dp")),
    )
    return jax.shard_map(
        on_device, mesh=mesh, in_specs=in_specs, out_specs=out_specs, check_vma=False
    )
```
